32 devices in a mesh: lvl: 8 (over y, x, core), col: 4 (over z).
Axes of the slice: x: 2, y: 2, z: 4, core: 2. Of those that a mesh axis runs over, the one named last changes fastest.
Arguments:
- up_blocks: float32 [16, 512, 512], P('lvl', None, 'col'), may hold values from -1.25 to 1.25
- level_blocks: float32 [16, 512, 512], P('lvl', None, 'col'), may hold values from -11 to 2, as said below
- down_blocks: float32 [16, 512, 512], P('lvl', None, 'col'), may hold values from -1.25 to 1.25
Outputs:
- reduced_level: float32 [8, 512, 512], P('lvl', None, 'col')
- reduced_up: float32 [8, 512, 512], P('lvl', None, 'col')
- reduced_down: float32 [8, 512, 512], P('lvl', None, 'col')
The draws below stay inside these ranges and needn't reach their ends.
Inputs may be any that keep to these rules, and one draw needn't show every extreme that they name: `level_blocks`: every diagonal entry of every level's block is -1 or less.
All inputs are finite; a program needn't handle non-finite values.
Results may differ from the reference program's by a relative error of at most 0.00013.
Values sent between devices are 32-bit elements; how exact they have to be, the bound alone decides.
No kernel may reach another device: no remote copies, remote signals or barrier semaphores. Data moves between devices by JAX's collectives and lax.ppermute only.
A program may use at most 64 MiB of HBM per device.

```python
import math
import jax
import jax.numpy as jnp
from jax import lax

P_SIZE = 512
SWEEPS = 2
LEVELS = 16


def draw_level_blocks(key, part):
    key_entries, key_spread, key_peak, key_height = jax.random.split(jax.random.fold_in(key, 17), 4)
    random_part = jnp.clip(jax.random.normal(key_entries, (LEVELS, P_SIZE, P_SIZE), jnp.float32), -4.0, 4.0)
    peak_scale = jax.random.uniform(key_height, (), jnp.float32, 1.0, 1.5)
    spread = jax.random.uniform(key_spread, (LEVELS, P_SIZE), jnp.float32)
    peak_level = jax.random.randint(key_peak, (), 0, LEVELS)
    level_rank = lax.broadcasted_iota(jnp.float32, (LEVELS, 1, 1), 0)
    level_number = lax.broadcasted_iota(jnp.int32, (LEVELS, 1, 1), 0)
    factor = 1.0 + 2.0 * level_rank / max(LEVELS - 1, 1)
    factor = jnp.where(level_number == peak_level, 3.0 * peak_scale, factor)
    coupling = 0.8 * factor * random_part / math.sqrt(P_SIZE)
    diagonal_values = -factor[:, :, 0] * (1.0 + 0.5 * spread)
    row_index = lax.broadcasted_iota(jnp.int32, (P_SIZE, P_SIZE), 0)
    col_index = lax.broadcasted_iota(jnp.int32, (P_SIZE, P_SIZE), 1)
    return jnp.where(row_index == col_index, diagonal_values[:, :, None], coupling)


def shard_levels(stream_key, shape, shards, smallest, high):
    factor_of = 1.0
    for axis_at, shards_of in shards:
        steps = jax.random.uniform(jax.random.fold_in(jax.random.fold_in(stream_key, 6), axis_at), (shards_of,), jnp.float32, smallest / len(shards), high / len(shards))
        factor_of = factor_of * jnp.repeat(jnp.exp(steps), shape[axis_at] // shards_of).reshape((-1,) + (1,) * (len(shape) - 1 - axis_at))
    return factor_of


def gaussian(rng, shape, scale, most, shards=(), kind=jnp.bfloat16):
    result = scale * jax.random.normal(rng, shape, jnp.float32)
    if shards:
        result = result * shard_levels(rng, shape, shards, -0.22, 0.18)
    return jnp.clip(result, -most, most).astype(kind)


def setup_inputs(seed: int = 0) -> dict:
    key_of = jax.random.split(jax.random.key(seed), 4)
    up_blocks = gaussian(key_of[0], (LEVELS, P_SIZE, P_SIZE), 0.2, 1.25, ((0, 8), (2, 4)), jnp.float32)
    level_blocks = draw_level_blocks(jax.random.fold_in(key_of[3], 71), 0)
    down_blocks = gaussian(key_of[2], (LEVELS, P_SIZE, P_SIZE), 0.2, 1.25, ((0, 8), (2, 4)), jnp.float32)
    return {"up_blocks": up_blocks, "level_blocks": level_blocks, "down_blocks": down_blocks}


def sweeps(level_block, up_block, down_block):
    phases = level_block.shape[0]
    out_rates = -jnp.diagonal(level_block)
    inverse = (1.0 / out_rates)[:, None]
    row_index = lax.broadcasted_iota(jnp.int32, (phases, phases), 0)
    col_index = lax.broadcasted_iota(jnp.int32, (phases, phases), 1)
    coupling = jnp.where(row_index == col_index, jnp.float32(0.0), level_block)
    right_side = jnp.concatenate([up_block, down_block], axis=1)
    solution = right_side * inverse
    for sweep_no in range(SWEEPS):
        product = jnp.dot(coupling, solution, precision=lax.Precision.HIGHEST, preferred_element_type=jnp.float32)
        solution = (right_side + product) * inverse
    return solution


def reference(up_blocks, level_blocks, down_blocks):
    top_rate = jnp.max(-jnp.diagonal(level_blocks, axis1=1, axis2=2))
    solved = lax.map(lambda blocks: sweeps(blocks[0], blocks[1], blocks[2]),
                     (level_blocks[1::2], up_blocks[1::2], down_blocks[1::2]))
    solved_below = jnp.concatenate([jnp.zeros((1,) + solved.shape[1:], jnp.float32), solved[:-1]], axis=0)

    def update(blocks):
        level_block, up_block, down_block, above_side, below_side = blocks
        phases = level_block.shape[0]
        upper_terms = jnp.dot(up_block, above_side, precision=lax.Precision.HIGHEST, preferred_element_type=jnp.float32)
        lower_terms = jnp.dot(down_block, below_side, precision=lax.Precision.HIGHEST, preferred_element_type=jnp.float32)
        new_level = (level_block + upper_terms[:, phases:] + lower_terms[:, :phases]) / top_rate
        return new_level, upper_terms[:, :phases] / top_rate, lower_terms[:, phases:] / top_rate

    reduced_level, reduced_up, reduced_down = lax.map(
        update, (level_blocks[0::2], up_blocks[0::2], down_blocks[0::2], solved, solved_below))
    return reduced_level, reduced_up, reduced_down
```

```python
import jax
import jax.numpy as jnp
from jax import lax
from jax.experimental import pallas as pl
from jax.experimental.pallas import tpu as pltpu
from jax.sharding import PartitionSpec as P

SWEEPS = 2
PEAK_ROWS = 8
F32 = jnp.float32
BF16 = jnp.bfloat16
VMEM = pl.BlockSpec(memory_space=pltpu.VMEM)
SMEM = pl.BlockSpec(memory_space=pltpu.SMEM)


def ring_offsets(shards):
    return [0, *[-d for d in range(1, shards // 2 + 1)], *range(1, (shards - 1) // 2 + 1)]


def split(x):
    high = x.astype(BF16)
    return high, (x - high.astype(F32)).astype(BF16)


def exact_dot(left, right):
    (left_high, left_low), (right_high, right_low) = left, right
    dot = lambda a, b: jnp.dot(a, b, preferred_element_type=F32)
    return dot(left_high, right_high) + (dot(left_high, right_low) + dot(left_low, right_high))


def on_diagonal(rows, cols):
    row = lax.broadcasted_iota(jnp.int32, (rows, cols), 0)
    return row == lax.broadcasted_iota(jnp.int32, (rows, cols), 1)


def pack_kernel(own_row, level_ref, packed_ref):
    _, phases, cols = level_ref.shape
    start = pl.multiple_of(own_row[0], cols)
    own = level_ref[:, pl.ds(start, cols), :]
    lowest = jnp.min(jnp.where(on_diagonal(cols, cols)[None], own, 0.0))
    packed_ref[pl.ds(0, phases), :] = level_ref[1]
    packed_ref[pl.ds(phases, PEAK_ROWS), :] = jnp.full((PEAK_ROWS, cols), -lowest, F32)


def owner_row(own_row, offset, cols, shards):
    return pl.multiple_of(lax.rem(own_row[0] + (offset + shards) * cols, shards * cols), cols)


def solve_kernel(own_row, *refs):
    shards = len(refs) - 9
    blocks = refs[:shards]
    up_ref, down_ref, solved_ref, peak_ref, inverse, high, low, s_high, s_low = refs[shards:]
    phases, cols = inverse.shape
    diagonal = on_diagonal(cols, cols)
    peak = None
    for slot, (offset, block) in enumerate(zip(ring_offsets(shards), blocks)):
        start = owner_row(own_row, offset, cols, shards)
        slot_cols = pl.ds(slot * cols, cols)
        high[:, slot_cols], low[:, slot_cols] = split(block[pl.ds(0, phases), :])
        square = block[pl.ds(start, cols), :]
        rate = -jnp.sum(jnp.where(diagonal, square, 0.0), axis=1, keepdims=True)
        inverse[pl.ds(start, cols), :] = jnp.broadcast_to(1.0 / rate, (cols, cols))
        rows = pl.ds(start, cols)
        high[rows, slot_cols], low[rows, slot_cols] = split(jnp.where(diagonal, 0.0, square))
        block_peak = block[pl.ds(phases, PEAK_ROWS), :]
        peak = block_peak if peak is None else jnp.maximum(peak, block_peak)
    peak_ref[...] = peak
    for side, ref in enumerate((up_ref, down_ref)):
        solved_ref[:, pl.ds(side * cols, cols)] = ref[0] * inverse[...]
    for _ in range(SWEEPS):
        for slot, offset in enumerate(ring_offsets(shards)):
            rows = pl.ds(owner_row(own_row, offset, cols, shards), cols)
            slot_rows = pl.ds(slot * cols, cols)
            s_high[slot_rows, :], s_low[slot_rows, :] = split(solved_ref[rows, :])
        product = exact_dot((high[...], low[...]), (s_high[...], s_low[...]))
        for side, ref in enumerate((up_ref, down_ref)):
            columns = slice(side * cols, (side + 1) * cols)
            solved_ref[:, columns] = (ref[0] + product[:, columns]) * inverse[...]


def gathered_product(own_row, blocks, solved_ref):
    shards, cols = len(blocks), blocks[0].shape[-1]
    left = split(jnp.concatenate([block[...] for block in blocks], axis=1))
    rows = [pl.ds(owner_row(own_row, offset, cols, shards), cols) for offset in ring_offsets(shards)]
    right = split(jnp.concatenate([solved_ref[r, :] for r in rows], axis=0))
    return exact_dot(left, right)


def upper_kernel(own_row, *refs):
    *blocks, solved_ref, out_ref = refs
    out_ref[...] = gathered_product(own_row, blocks, solved_ref)


def lower_kernel(own_row, *refs):
    *blocks, solved_ref, upper_ref, level_ref, peak_ref, new_level, new_up, new_down = refs
    cols = new_up.shape[-1]
    lower = gathered_product(own_row, blocks, solved_ref)
    scale = 1.0 / peak_ref[0:1, :]
    new_up[0] = upper_ref[:, :cols] * scale
    new_down[0] = lower[:, cols:] * scale
    new_level[0] = (level_ref[0] + upper_ref[:, cols:] + lower[:, :cols]) * scale


def per_device(up_blocks, level_blocks, down_blocks):
    levels, phases, cols = level_blocks.shape
    assert levels == 2
    shards = lax.axis_size("col")
    ranges = lax.axis_size("lvl")
    own_row = (lax.axis_index("col") * cols).astype(jnp.int32).reshape(1)
    params = pltpu.CompilerParams(vmem_limit_bytes=32 * 2**20)
    shape = lambda *dims, kind=F32: jax.ShapeDtypeStruct(dims, kind)

    def shifted(block, distance):
        return lax.ppermute(block, "col", [(i, (i + distance) % shards) for i in range(shards)])

    def after(value, *earlier):
        return lax.optimization_barrier((value, *earlier))[0]

    def odd(ref_cols):
        return pl.BlockSpec((1, phases, ref_cols), lambda step: (1, 0, 0))

    packed = pl.pallas_call(
        pack_kernel,
        out_shape=shape(phases + PEAK_ROWS, cols),
        in_specs=[SMEM, VMEM],
        out_specs=VMEM,
        grid=(1,),
        compiler_params=params,
    )(own_row, level_blocks)

    def gather(block):
        found = {0: block}
        for d in range(1, shards // 2 + 1):
            found[-d] = shifted(found[-d + 1], 1)
        for d in range(1, (shards - 1) // 2 + 1):
            found[d] = shifted(found[d - 1], -1)
        return [found[offset] for offset in ring_offsets(shards)]

    level_parts = gather(packed)
    up_parts = gather(after(up_blocks[0], level_parts[1]))
    down_parts = gather(after(down_blocks[0], up_parts[1]))

    solved, peak = pl.pallas_call(
        solve_kernel,
        out_shape=(shape(phases, 2 * cols), shape(PEAK_ROWS, cols)),
        in_specs=[SMEM, *[VMEM] * shards, odd(cols), odd(cols)],
        out_specs=(VMEM, VMEM),
        scratch_shapes=[
            pltpu.VMEM((phases, cols), F32),
            pltpu.VMEM((phases, phases), BF16),
            pltpu.VMEM((phases, phases), BF16),
            pltpu.VMEM((phases, 2 * cols), BF16),
            pltpu.VMEM((phases, 2 * cols), BF16),
        ],
        grid=(1,),
        compiler_params=params,
    )(own_row, *level_parts, up_blocks, down_blocks)

    from_below = lax.ppermute(solved, "lvl", [(i, i + 1) for i in range(ranges - 1)])
    reach = 1
    while reach < ranges:
        other = lax.ppermute(peak, "lvl", [(i, (i + reach) % ranges) for i in range(ranges)])
        peak = jnp.maximum(peak, other)
        reach *= 2

    upper = pl.pallas_call(
        upper_kernel,
        out_shape=shape(phases, 2 * cols),
        in_specs=[SMEM, *[VMEM] * (shards + 1)],
        out_specs=VMEM,
        grid=(1,),
        compiler_params=params,
    )(own_row, *up_parts, solved)

    even = pl.BlockSpec((1, phases, cols), lambda step: (0, 0, 0))
    return pl.pallas_call(
        lower_kernel,
        out_shape=(shape(1, phases, cols),) * 3,
        in_specs=[SMEM, *[VMEM] * (shards + 2), even, VMEM],
        out_specs=(VMEM,) * 3,
        grid=(1,),
        compiler_params=params,
    )(own_row, *down_parts, from_below, upper, level_blocks, peak)


def solution(mesh):
    placed = (P("lvl", None, "col"),) * 3
    return jax.shard_map(per_device, mesh=mesh, in_specs=placed, out_specs=placed, check_vma=False)
```

```python
import jax
import jax.numpy as jnp
from jax import lax
from jax.experimental import pallas as pl
from jax.experimental.pallas import tpu as pltpu
from jax.sharding import PartitionSpec as P

SWEEPS = 2
F32 = jnp.float32
BF16 = jnp.bfloat16
VMEM = pl.BlockSpec(memory_space=pltpu.VMEM)
SMEM = pl.BlockSpec(memory_space=pltpu.SMEM)


def ring_offsets(shards):
    return [0, *[-d for d in range(1, shards // 2 + 1)], *range(1, (shards - 1) // 2 + 1)]


def split(x):
    high = x.astype(BF16)
    return high, (x - high.astype(F32)).astype(BF16)


def exact_dot(left, right):
    (left_high, left_low), (right_high, right_low) = left, right
    dot = lambda a, b: jnp.dot(a, b, preferred_element_type=F32)
    return dot(left_high, right_high) + (dot(left_high, right_low) + dot(left_low, right_high))


def on_diagonal(rows, cols):
    row = lax.broadcasted_iota(jnp.int32, (rows, cols), 0)
    return row == lax.broadcasted_iota(jnp.int32, (rows, cols), 1)


def pack_kernel(own_row, level_ref, packed_ref, peak_ref):
    cols = level_ref.shape[-1]
    own = level_ref[:, pl.ds(pl.multiple_of(own_row[0], cols), cols), :]
    peak_ref[0, 0] = -jnp.min(jnp.where(on_diagonal(cols, cols)[None], own, 0.0))
    packed_ref[...] = level_ref[1]


def stack_kernel(up_ref, down_ref, stacked_ref):
    phases = up_ref.shape[1]
    stacked_ref[pl.ds(0, phases), :] = up_ref[0]
    stacked_ref[pl.ds(phases, phases), :] = down_ref[0]


def owner_row(own_row, offset, cols, shards):
    return pl.multiple_of(lax.rem(own_row[0] + (offset + shards) * cols, shards * cols), cols)


def solve_kernel(own_row, *refs):
    shards = len(refs) - 8
    blocks = refs[:shards]
    up_ref, down_ref, solved_ref, inverse, high, low, s_high, s_low = refs[shards:]
    phases, cols = inverse.shape
    diagonal = on_diagonal(cols, cols)
    for slot, (offset, block) in enumerate(zip(ring_offsets(shards), blocks)):
        rows = pl.ds(owner_row(own_row, offset, cols, shards), cols)
        slot_cols = pl.ds(slot * cols, cols)
        high[:, slot_cols], low[:, slot_cols] = split(block[...])
        square = block[rows, :]
        rate = -jnp.sum(jnp.where(diagonal, square, 0.0), axis=1, keepdims=True)
        inverse[rows, :] = jnp.broadcast_to(1.0 / rate, (cols, cols))
        high[rows, slot_cols], low[rows, slot_cols] = split(jnp.where(diagonal, 0.0, square))
    for side, ref in enumerate((up_ref, down_ref)):
        solved_ref[:, pl.ds(side * cols, cols)] = ref[0] * inverse[...]
    for _ in range(SWEEPS):
        for slot, offset in enumerate(ring_offsets(shards)):
            rows = pl.ds(owner_row(own_row, offset, cols, shards), cols)
            slot_rows = pl.ds(slot * cols, cols)
            s_high[slot_rows, :], s_low[slot_rows, :] = split(solved_ref[rows, :])
        product = exact_dot((high[...], low[...]), (s_high[...], s_low[...]))
        for side, ref in enumerate((up_ref, down_ref)):
            columns = slice(side * cols, (side + 1) * cols)
            solved_ref[:, columns] = (ref[0] + product[:, columns]) * inverse[...]


def gathered_product(own_row, blocks, first_row, solved_ref):
    shards, cols = len(blocks), blocks[0].shape[-1]
    phases = solved_ref.shape[0]
    left = split(jnp.concatenate([block[pl.ds(first_row, phases), :] for block in blocks], axis=1))
    rows = [pl.ds(owner_row(own_row, offset, cols, shards), cols) for offset in ring_offsets(shards)]
    right = split(jnp.concatenate([solved_ref[r, :] for r in rows], axis=0))
    return exact_dot(left, right)


def output_kernel(own_row, peak_ref, *refs):
    *blocks, solved_ref, below_ref, level_ref, new_level, new_up, new_down = refs
    _, phases, cols = new_up.shape
    scale = 1.0 / jnp.full((1, cols), peak_ref[0, 0], F32)
    upper = gathered_product(own_row, blocks, 0, solved_ref)
    new_up[0] = upper[:, :cols] * scale
    lower = gathered_product(own_row, blocks, phases, below_ref)
    new_down[0] = lower[:, cols:] * scale
    new_level[0] = (level_ref[0] + upper[:, cols:] + lower[:, :cols]) * scale


def per_device(up_blocks, level_blocks, down_blocks):
    levels, phases, cols = level_blocks.shape
    assert levels == 2
    shards = lax.axis_size("col")
    ranges = lax.axis_size("lvl")
    own_row = (lax.axis_index("col") * cols).astype(jnp.int32).reshape(1)
    params = pltpu.CompilerParams(vmem_limit_bytes=32 * 2**20)
    shape = lambda *dims, kind=F32: jax.ShapeDtypeStruct(dims, kind)

    def shifted(block, distance):
        return lax.ppermute(block, "col", [(i, (i + distance) % shards) for i in range(shards)])

    def after(value, *earlier):
        return lax.optimization_barrier((value, *earlier))[0]

    def one_level(parity):
        return pl.BlockSpec((1, phases, cols), lambda step: (parity, 0, 0))

    odd, even = one_level(1), one_level(0)
    packed, peak = pl.pallas_call(
        pack_kernel,
        out_shape=(shape(phases, cols), shape(1, 1)),
        in_specs=[SMEM, VMEM],
        out_specs=(VMEM, SMEM),
        grid=(1,),
        compiler_params=params,
    )(own_row, level_blocks)
    stacked = pl.pallas_call(
        stack_kernel,
        out_shape=shape(2 * phases, cols),
        in_specs=[even, even],
        out_specs=VMEM,
        grid=(1,),
        compiler_params=params,
    )(up_blocks, down_blocks)

    level_parts, even_parts = {0: packed}, {0: stacked}

    def step(parts, reached, distance, *earlier):
        block = after(parts[reached], *earlier) if earlier else parts[reached]
        parts[reached - distance] = shifted(block, distance)

    behind, ahead = range(shards // 2), range((shards - 1) // 2)
    step(level_parts, 0, 1)
    for reached in ahead:
        step(level_parts, reached, -1)
    top_rate = lax.pmax(peak, ("lvl", "col"))
    step(even_parts, 0, 1, *[part for at, part in level_parts.items() if at], top_rate)
    for reached in behind[1:]:
        step(level_parts, -reached, 1)
    for reached in ahead:
        step(even_parts, reached, -1, level_parts[-len(behind)])
    for reached in behind[1:]:
        step(even_parts, -reached, 1)
    level_parts = [level_parts[offset] for offset in ring_offsets(shards)]
    even_parts = [even_parts[offset] for offset in ring_offsets(shards)]

    solved = pl.pallas_call(
        solve_kernel,
        out_shape=shape(phases, 2 * cols),
        in_specs=[SMEM, *[VMEM] * shards, odd, odd],
        out_specs=VMEM,
        scratch_shapes=[
            pltpu.VMEM((phases, cols), F32),
            pltpu.VMEM((phases, phases), BF16),
            pltpu.VMEM((phases, phases), BF16),
            pltpu.VMEM((phases, 2 * cols), BF16),
            pltpu.VMEM((phases, 2 * cols), BF16),
        ],
        grid=(1,),
        compiler_params=params,
    )(own_row, *level_parts, up_blocks, down_blocks)
    from_below = lax.ppermute(solved, "lvl", [(i, i + 1) for i in range(ranges - 1)])

    return pl.pallas_call(
        output_kernel,
        out_shape=(shape(1, phases, cols),) * 3,
        in_specs=[SMEM, SMEM, *[VMEM] * (shards + 2), even],
        out_specs=(VMEM,) * 3,
        grid=(1,),
        compiler_params=params,
    )(own_row, top_rate, *even_parts, solved, from_below, level_blocks)


def solution(mesh):
    placed = (P("lvl", None, "col"),) * 3
    return jax.shard_map(per_device, mesh=mesh, in_specs=placed, out_specs=placed, check_vma=False)
```

```python
import functools

import jax
import jax.numpy as jnp
from jax import lax
from jax.experimental import pallas as pl
from jax.experimental.pallas import tpu as pltpu
from jax.sharding import PartitionSpec as P

SWEEPS = 2
PEAK_ROWS = 8
F32 = jnp.float32
BF16 = jnp.bfloat16
VMEM = pl.BlockSpec(memory_space=pltpu.VMEM)
SMEM = pl.BlockSpec(memory_space=pltpu.SMEM)


def ring_offsets(shards):
    return [0, *[-d for d in range(1, shards // 2 + 1)], *range(1, (shards - 1) // 2 + 1)]


def split(x):
    high = x.astype(BF16)
    return high, (x - high.astype(F32)).astype(BF16)


def exact_dot(left, right):
    (left_high, left_low), (right_high, right_low) = left, right
    dot = lambda a, b: jnp.dot(a, b, preferred_element_type=F32)
    return dot(left_high, right_high) + (dot(left_high, right_low) + dot(left_low, right_high))


def on_diagonal(rows, cols):
    row = lax.broadcasted_iota(jnp.int32, (rows, cols), 0)
    return row == lax.broadcasted_iota(jnp.int32, (rows, cols), 1)


def pack_kernel(own_row, level_ref, packed_ref):
    _, phases, cols = level_ref.shape
    own = level_ref[:, pl.ds(pl.multiple_of(own_row[0], cols), cols), :]
    lowest = jnp.min(jnp.where(on_diagonal(cols, cols)[None], own, 0.0))
    packed_ref[pl.ds(0, phases), :] = level_ref[1]
    packed_ref[pl.ds(phases, PEAK_ROWS), :] = jnp.full((PEAK_ROWS, cols), -lowest, F32)


def stack_kernel(up_ref, down_ref, stacked_ref):
    phases = up_ref.shape[1]
    stacked_ref[pl.ds(0, phases), :] = up_ref[0]
    stacked_ref[pl.ds(phases, phases), :] = down_ref[0]


def owner_row(own_row, offset, cols, shards):
    return pl.multiple_of(lax.rem(own_row[0] + (offset + shards) * cols, shards * cols), cols)


def solve_kernel(own_row, *refs):
    shards = len(refs) - 9
    blocks = refs[:shards]
    up_ref, down_ref, solved_ref, peak_ref, inverse, high, low, s_high, s_low = refs[shards:]
    phases, cols = inverse.shape
    diagonal = on_diagonal(cols, cols)
    peak = None
    for slot, (offset, block) in enumerate(zip(ring_offsets(shards), blocks)):
        rows = pl.ds(owner_row(own_row, offset, cols, shards), cols)
        slot_cols = pl.ds(slot * cols, cols)
        high[:, slot_cols], low[:, slot_cols] = split(block[pl.ds(0, phases), :])
        square = block[rows, :]
        rate = -jnp.sum(jnp.where(diagonal, square, 0.0), axis=1, keepdims=True)
        inverse[rows, :] = jnp.broadcast_to(1.0 / rate, (cols, cols))
        high[rows, slot_cols], low[rows, slot_cols] = split(jnp.where(diagonal, 0.0, square))
        block_peak = block[pl.ds(phases, PEAK_ROWS), :]
        peak = block_peak if peak is None else jnp.maximum(peak, block_peak)
    peak_ref[...] = peak
    for side, ref in enumerate((up_ref, down_ref)):
        solved_ref[:, pl.ds(side * cols, cols)] = ref[0] * inverse[...]
    for _ in range(SWEEPS):
        for slot, offset in enumerate(ring_offsets(shards)):
            rows = pl.ds(owner_row(own_row, offset, cols, shards), cols)
            slot_rows = pl.ds(slot * cols, cols)
            s_high[slot_rows, :], s_low[slot_rows, :] = split(solved_ref[rows, :])
        product = exact_dot((high[...], low[...]), (s_high[...], s_low[...]))
        for side, ref in enumerate((up_ref, down_ref)):
            columns = slice(side * cols, (side + 1) * cols)
            solved_ref[:, columns] = (ref[0] + product[:, columns]) * inverse[...]


def gathered_product(own_row, blocks, offsets, shards, first_row, solved_ref):
    cols = blocks[0].shape[-1]
    phases = solved_ref.shape[0]
    left = split(jnp.concatenate([block[pl.ds(first_row, phases), :] for block in blocks], axis=1))
    rows = [pl.ds(owner_row(own_row, offset, cols, shards), cols) for offset in offsets]
    right = split(jnp.concatenate([solved_ref[r, :] for r in rows], axis=0))
    return exact_dot(left, right)


def partial_kernel(offsets, shards, own_row, *refs):
    *blocks, solved_ref, below_ref, level_ref, part_level, part_up, part_down = refs
    phases, cols = part_up.shape
    upper = gathered_product(own_row, blocks, offsets, shards, 0, solved_ref)
    part_up[...] = upper[:, :cols]
    lower = gathered_product(own_row, blocks, offsets, shards, phases, below_ref)
    part_down[...] = lower[:, cols:]
    part_level[...] = level_ref[0] + upper[:, cols:] + lower[:, :cols]


def output_kernel(offsets, shards, own_row, *refs):
    *blocks, solved_ref, below_ref, part_level, part_up, part_down, peak_ref, new_level, new_up, new_down = refs
    phases, cols = part_up.shape
    scale = 1.0 / peak_ref[0:1, :]
    upper = gathered_product(own_row, blocks, offsets, shards, 0, solved_ref)
    new_up[0] = (part_up[...] + upper[:, :cols]) * scale
    lower = gathered_product(own_row, blocks, offsets, shards, phases, below_ref)
    new_down[0] = (part_down[...] + lower[:, cols:]) * scale
    new_level[0] = (part_level[...] + upper[:, cols:] + lower[:, :cols]) * scale


def per_device(up_blocks, level_blocks, down_blocks):
    levels, phases, cols = level_blocks.shape
    assert levels == 2
    shards = lax.axis_size("col")
    ranges = lax.axis_size("lvl")
    own_row = (lax.axis_index("col") * cols).astype(jnp.int32).reshape(1)
    params = pltpu.CompilerParams(vmem_limit_bytes=32 * 2**20)
    shape = lambda *dims, kind=F32: jax.ShapeDtypeStruct(dims, kind)

    def shifted(block, distance):
        return lax.ppermute(block, "col", [(i, (i + distance) % shards) for i in range(shards)])

    def after(value, *earlier):
        return lax.optimization_barrier((value, *earlier))[0]

    def one_level(parity):
        return pl.BlockSpec((1, phases, cols), lambda step: (parity, 0, 0))

    odd, even = one_level(1), one_level(0)
    packed = pl.pallas_call(
        pack_kernel,
        out_shape=shape(phases + PEAK_ROWS, cols),
        in_specs=[SMEM, VMEM],
        out_specs=VMEM,
        grid=(1,),
        compiler_params=params,
    )(own_row, level_blocks)
    stacked = pl.pallas_call(
        stack_kernel,
        out_shape=shape(2 * phases, cols),
        in_specs=[even, even],
        out_specs=VMEM,
        grid=(1,),
        compiler_params=params,
    )(up_blocks, down_blocks)

    level_parts, even_parts = {0: packed}, {0: stacked}

    def step(parts, reached, distance, *earlier):
        block = after(parts[reached], *earlier) if earlier else parts[reached]
        parts[reached - distance] = shifted(block, distance)

    offsets = ring_offsets(shards)
    behind, ahead = range(shards // 2), range((shards - 1) // 2)
    step(level_parts, 0, 1)
    for reached in ahead:
        step(level_parts, reached, -1)
    step(even_parts, 0, 1)
    for reached in behind[1:]:
        step(level_parts, -reached, 1)
    for reached in ahead:
        step(even_parts, reached, -1, level_parts[-1])
    for reached in behind[1:]:
        step(even_parts, -reached, 1)

    solved, peak = pl.pallas_call(
        solve_kernel,
        out_shape=(shape(phases, 2 * cols), shape(PEAK_ROWS, cols)),
        in_specs=[SMEM, *[VMEM] * shards, odd, odd],
        out_specs=(VMEM, VMEM),
        scratch_shapes=[
            pltpu.VMEM((phases, cols), F32),
            pltpu.VMEM((phases, phases), BF16),
            pltpu.VMEM((phases, phases), BF16),
            pltpu.VMEM((phases, 2 * cols), BF16),
            pltpu.VMEM((phases, 2 * cols), BF16),
        ],
        grid=(1,),
        compiler_params=params,
    )(own_row, *[level_parts[offset] for offset in offsets], up_blocks, down_blocks)
    from_below = lax.ppermute(solved, "lvl", [(i, i + 1) for i in range(ranges - 1)])

    peak = after(peak, even_parts[-1])
    reach = 1
    while reach < ranges:
        other = lax.ppermute(peak, "lvl", [(i, (i + reach) % ranges) for i in range(ranges)])
        peak = jnp.maximum(peak, other)
        reach *= 2

    last = -len(behind)
    early = [offset for offset in offsets if offset != last]
    parts = pl.pallas_call(
        functools.partial(partial_kernel, early, shards),
        out_shape=(shape(phases, cols),) * 3,
        in_specs=[SMEM, *[VMEM] * (len(early) + 2), even],
        out_specs=(VMEM,) * 3,
        grid=(1,),
        compiler_params=params,
    )(own_row, *[even_parts[offset] for offset in early], solved, from_below, level_blocks)
    return pl.pallas_call(
        functools.partial(output_kernel, [last], shards),
        out_shape=(shape(1, phases, cols),) * 3,
        in_specs=[SMEM, *[VMEM] * 7],
        out_specs=(VMEM,) * 3,
        grid=(1,),
        compiler_params=params,
    )(own_row, even_parts[last], solved, from_below, *parts, peak)


def solution(mesh):
    placed = (P("lvl", None, "col"),) * 3
    return jax.shard_map(per_device, mesh=mesh, in_specs=placed, out_specs=placed, check_vma=False)
```

```python
import functools

import jax
import jax.numpy as jnp
from jax import lax
from jax.experimental import pallas as pl
from jax.experimental.pallas import tpu as pltpu
from jax.sharding import PartitionSpec as P

SWEEPS = 2
PEAK_ROWS = 8
PAD_ROWS = 16
F32 = jnp.float32
BF16 = jnp.bfloat16
VMEM = pl.BlockSpec(memory_space=pltpu.VMEM)
SMEM = pl.BlockSpec(memory_space=pltpu.SMEM)


def ring_offsets(shards):
    return [0, *[-d for d in range(1, shards // 2 + 1)], *range(1, (shards - 1) // 2 + 1)]


def split(x):
    high = x.astype(BF16)
    return high, (x - high.astype(F32)).astype(BF16)


def exact_dot(left, right):
    (left_high, left_low), (right_high, right_low) = left, right
    dot = lambda a, b: jnp.dot(a, b, preferred_element_type=F32)
    return dot(left_high, right_high) + (dot(left_high, right_low) + dot(left_low, right_high))


def on_diagonal(rows, cols):
    row = lax.broadcasted_iota(jnp.int32, (rows, cols), 0)
    return row == lax.broadcasted_iota(jnp.int32, (rows, cols), 1)


def peak_kernel(own_row, level_ref, peak_ref):
    cols = level_ref.shape[-1]
    own = level_ref[:, pl.ds(pl.multiple_of(own_row[0], cols), cols), :]
    lowest = jnp.min(jnp.where(on_diagonal(cols, cols)[None], own, 0.0))
    peak_ref[...] = jnp.full(peak_ref.shape, -lowest, F32)


def pack_kernel(level_ref, peak_ref, packed_ref):
    phases = level_ref.shape[1]
    packed_ref[pl.ds(0, phases), :] = level_ref[0]
    packed_ref[pl.ds(phases, PEAK_ROWS), :] = peak_ref[...]


def stack_kernel(up_ref, down_ref, stacked_ref):
    phases = up_ref.shape[1]
    stacked_ref[pl.ds(0, phases), :] = up_ref[0]
    stacked_ref[pl.ds(phases, phases), :] = down_ref[0]
    stacked_ref[pl.ds(2 * phases, PAD_ROWS), :] = jnp.zeros((PAD_ROWS, up_ref.shape[2]), F32)


def owner_row(own_row, offset, cols, shards):
    return pl.multiple_of(lax.rem(own_row[0] + (offset + shards) * cols, shards * cols), cols)


def solve_kernel(own_row, *refs):
    shards = len(refs) - 9
    blocks = refs[:shards]
    up_ref, down_ref, solved_ref, peak_ref, inverse, high, low, s_high, s_low = refs[shards:]
    phases, cols = inverse.shape
    diagonal = on_diagonal(cols, cols)
    peak = blocks[0][pl.ds(phases, PEAK_ROWS), :]
    for block in blocks[1:]:
        peak = jnp.maximum(peak, block[pl.ds(phases, PEAK_ROWS), :])
    peak_ref[...] = peak
    for slot, (offset, block) in enumerate(zip(ring_offsets(shards), blocks)):
        rows = pl.ds(owner_row(own_row, offset, cols, shards), cols)
        slot_cols = pl.ds(slot * cols, cols)
        high[:, slot_cols], low[:, slot_cols] = split(block[pl.ds(0, phases), :])
        square = block[rows, :]
        rate = -jnp.sum(jnp.where(diagonal, square, 0.0), axis=1, keepdims=True)
        inverse[rows, :] = jnp.broadcast_to(1.0 / rate, (cols, cols))
        high[rows, slot_cols], low[rows, slot_cols] = split(jnp.where(diagonal, 0.0, square))
    for side, ref in enumerate((up_ref, down_ref)):
        solved_ref[:, pl.ds(side * cols, cols)] = ref[0] * inverse[...]
    for _ in range(SWEEPS):
        for slot, offset in enumerate(ring_offsets(shards)):
            rows = pl.ds(owner_row(own_row, offset, cols, shards), cols)
            slot_rows = pl.ds(slot * cols, cols)
            s_high[slot_rows, :], s_low[slot_rows, :] = split(solved_ref[rows, :])
        product = exact_dot((high[...], low[...]), (s_high[...], s_low[...]))
        for side, ref in enumerate((up_ref, down_ref)):
            columns = slice(side * cols, (side + 1) * cols)
            solved_ref[:, columns] = (ref[0] + product[:, columns]) * inverse[...]


def gathered_product(own_row, blocks, offsets, shards, first_row, solved_ref):
    cols = blocks[0].shape[-1]
    phases = solved_ref.shape[0]
    left = split(jnp.concatenate([block[pl.ds(first_row, phases), :] for block in blocks], axis=1))
    rows = [pl.ds(owner_row(own_row, offset, cols, shards), cols) for offset in offsets]
    right = split(jnp.concatenate([solved_ref[r, :] for r in rows], axis=0))
    return exact_dot(left, right)


def partial_kernel(offsets, shards, own_row, *refs):
    *blocks, solved_ref, below_ref, level_ref, part_level, part_up, part_down = refs
    phases, cols = part_up.shape
    upper = gathered_product(own_row, blocks, offsets, shards, 0, solved_ref)
    part_up[...] = upper[:, :cols]
    lower = gathered_product(own_row, blocks, offsets, shards, phases, below_ref)
    part_down[...] = lower[:, cols:]
    part_level[...] = level_ref[0] + upper[:, cols:] + lower[:, :cols]


def output_kernel(offsets, shards, own_row, *refs):
    *blocks, solved_ref, below_ref, part_level, part_up, part_down, peak_ref, new_level, new_up, new_down = refs
    phases, cols = part_up.shape
    scale = 1.0 / peak_ref[0:1, :]
    upper = gathered_product(own_row, blocks, offsets, shards, 0, solved_ref)
    new_up[0] = (part_up[...] + upper[:, :cols]) * scale
    lower = gathered_product(own_row, blocks, offsets, shards, phases, below_ref)
    new_down[0] = (part_down[...] + lower[:, cols:]) * scale
    new_level[0] = (part_level[...] + upper[:, cols:] + lower[:, :cols]) * scale


def per_device(up_blocks, level_blocks, down_blocks):
    levels, phases, cols = level_blocks.shape
    assert levels == 2
    shards = lax.axis_size("col")
    ranges = lax.axis_size("lvl")
    own_row = (lax.axis_index("col") * cols).astype(jnp.int32).reshape(1)
    params = pltpu.CompilerParams(vmem_limit_bytes=32 * 2**20)
    shape = lambda *dims, kind=F32: jax.ShapeDtypeStruct(dims, kind)

    def shifted(block, distance):
        return lax.ppermute(block, "col", [(i, (i + distance) % shards) for i in range(shards)])

    def after(value, *earlier):
        return lax.optimization_barrier((value, *earlier))[0]

    def one_level(parity):
        return pl.BlockSpec((1, phases, cols), lambda step: (parity, 0, 0))

    odd, even = one_level(1), one_level(0)
    stacked = pl.pallas_call(
        stack_kernel,
        out_shape=shape(2 * phases + PAD_ROWS, cols),
        in_specs=[even, even],
        out_specs=VMEM,
        grid=(1,),
        compiler_params=params,
    )(up_blocks, down_blocks)

    peak = pl.pallas_call(
        peak_kernel,
        out_shape=shape(PEAK_ROWS, cols),
        in_specs=[SMEM, VMEM],
        out_specs=VMEM,
        grid=(1,),
        compiler_params=params,
    )(after(own_row, stacked), level_blocks)
    reach = 1
    while reach < ranges:
        route = [(i, (i + reach) % ranges) for i in range(ranges)]
        peak = jnp.maximum(peak, lax.ppermute(peak, "lvl", route))
        reach *= 2
    packed = pl.pallas_call(
        pack_kernel,
        out_shape=shape(phases + PEAK_ROWS, cols),
        in_specs=[odd, VMEM],
        out_specs=VMEM,
        grid=(1,),
        compiler_params=params,
    )(level_blocks, peak)
    level_parts, even_parts = {0: packed}, {0: stacked}

    def step(parts, reached, distance, *earlier):
        block = after(parts[reached], *earlier) if earlier else parts[reached]
        parts[reached - distance] = shifted(block, distance)

    offsets = ring_offsets(shards)
    behind, ahead = range(shards // 2), range((shards - 1) // 2)
    step(even_parts, 0, 1)
    for reached in behind:
        step(level_parts, -reached, 1)
    for reached in ahead:
        step(level_parts, reached, -1)
    for reached in ahead:
        step(even_parts, reached, -1, level_parts[-1])
    for reached in behind[1:]:
        step(even_parts, -reached, 1)

    solved, peak = pl.pallas_call(
        solve_kernel,
        out_shape=(shape(phases, 2 * cols), shape(PEAK_ROWS, cols)),
        in_specs=[SMEM, *[VMEM] * shards, odd, odd],
        out_specs=(VMEM, VMEM),
        scratch_shapes=[
            pltpu.VMEM((phases, cols), F32),
            pltpu.VMEM((phases, phases), BF16),
            pltpu.VMEM((phases, phases), BF16),
            pltpu.VMEM((phases, 2 * cols), BF16),
            pltpu.VMEM((phases, 2 * cols), BF16),
        ],
        grid=(1,),
        compiler_params=params,
    )(after(own_row, even_parts[-1]), *[level_parts[offset] for offset in offsets], up_blocks, down_blocks)
    from_below = lax.ppermute(solved, "lvl", [(i, i + 1) for i in range(ranges - 1)])

    last = -len(behind)
    early = [offset for offset in offsets if offset != last]
    parts = pl.pallas_call(
        functools.partial(partial_kernel, early, shards),
        out_shape=(shape(phases, cols),) * 3,
        in_specs=[SMEM, *[VMEM] * (len(early) + 2), even],
        out_specs=(VMEM,) * 3,
        grid=(1,),
        compiler_params=params,
        cost_estimate=pl.CostEstimate(flops=0, bytes_accessed=0, transcendentals=0),
    )(own_row, *[even_parts[offset] for offset in early], solved, from_below, level_blocks)
    return pl.pallas_call(
        functools.partial(output_kernel, [last], shards),
        out_shape=(shape(1, phases, cols),) * 3,
        in_specs=[SMEM, *[VMEM] * 7],
        out_specs=(VMEM,) * 3,
        grid=(1,),
        compiler_params=params,
    )(own_row, even_parts[last], solved, from_below, *parts, peak)


def solution(mesh):
    placed = (P("lvl", None, "col"),) * 3
    return jax.shard_map(per_device, mesh=mesh, in_specs=placed, out_specs=placed, check_vma=False)
```

```python
import functools

import jax
import jax.numpy as jnp
from jax import lax
from jax.experimental import pallas as pl
from jax.experimental.pallas import tpu as pltpu
from jax.sharding import PartitionSpec as P

SWEEPS = 2
PEAK_ROWS = 8
PAD_ROWS = 16
F32 = jnp.float32
BF16 = jnp.bfloat16
VMEM = pl.BlockSpec(memory_space=pltpu.VMEM)
ANY = pl.BlockSpec(memory_space=pl.ANY)
SMEM = pl.BlockSpec(memory_space=pltpu.SMEM)


def ring_offsets(shards):
    return [0, *[-d for d in range(1, shards // 2 + 1)], *range(1, (shards - 1) // 2 + 1)]


def split(x):
    high = x.astype(BF16)
    return high, (x - high.astype(F32)).astype(BF16)


def exact_dot(left, right):
    (left_high, left_low), (right_high, right_low) = left, right
    dot = lambda a, b: jnp.dot(a, b, preferred_element_type=F32)
    return dot(left_high, right_high) + (dot(left_high, right_low) + dot(left_low, right_high))


def on_diagonal(rows, cols):
    row = lax.broadcasted_iota(jnp.int32, (rows, cols), 0)
    return row == lax.broadcasted_iota(jnp.int32, (rows, cols), 1)


def send_kernel(up_ref, level_ref, down_ref, all_ref, odd_ref, even_ref, sems):
    _, phases, _ = level_ref.shape
    rows = lambda ref, part: ref.at[pl.ds(part * phases, phases), :]
    copies = [
        pltpu.make_async_copy(source, target, sems.at[at])
        for at, (source, target) in enumerate(
            (
                (level_ref.at[1], rows(all_ref, 0)),
                (up_ref.at[0], rows(all_ref, 1)),
                (down_ref.at[0], rows(all_ref, 2)),
                (level_ref.at[1], odd_ref),
                (up_ref.at[0], rows(even_ref, 0)),
                (down_ref.at[0], rows(even_ref, 1)),
            )
        )
    ]
    for copy in copies:
        copy.start()
    for copy in copies:
        copy.wait()


def peak_kernel(own_row, level_ref, peak_ref):
    cols = level_ref.shape[-1]
    own = level_ref[:, pl.ds(pl.multiple_of(own_row[0], cols), cols), :]
    lowest = jnp.min(jnp.where(on_diagonal(cols, cols)[None], own, 0.0))
    peak_ref[...] = jnp.full(peak_ref.shape, -lowest, F32)


def owner_row(own_row, offset, cols, shards):
    return pl.multiple_of(lax.rem(own_row[0] + (offset + shards) * cols, shards * cols), cols)


def solve_kernel(own_row, *refs):
    shards = len(refs) - 8
    blocks = [refs[0].at[0], *refs[1:shards]]
    up_ref, down_ref, solved_ref, inverse, high, low, s_high, s_low = refs[shards:]
    phases, cols = inverse.shape
    diagonal = on_diagonal(cols, cols)
    for slot, (offset, block) in enumerate(zip(ring_offsets(shards), blocks)):
        rows = pl.ds(owner_row(own_row, offset, cols, shards), cols)
        slot_cols = pl.ds(slot * cols, cols)
        high[:, slot_cols], low[:, slot_cols] = split(block[pl.ds(0, phases), :])
        square = block[rows, :]
        rate = -jnp.sum(jnp.where(diagonal, square, 0.0), axis=1, keepdims=True)
        inverse[rows, :] = jnp.broadcast_to(1.0 / rate, (cols, cols))
        high[rows, slot_cols], low[rows, slot_cols] = split(jnp.where(diagonal, 0.0, square))
    for side, ref in enumerate((up_ref, down_ref)):
        solved_ref[:, pl.ds(side * cols, cols)] = ref[0] * inverse[...]
    for _ in range(SWEEPS):
        for slot, offset in enumerate(ring_offsets(shards)):
            rows = pl.ds(owner_row(own_row, offset, cols, shards), cols)
            slot_rows = pl.ds(slot * cols, cols)
            s_high[slot_rows, :], s_low[slot_rows, :] = split(solved_ref[rows, :])
        product = exact_dot((high[...], low[...]), (s_high[...], s_low[...]))
        for side, ref in enumerate((up_ref, down_ref)):
            columns = slice(side * cols, (side + 1) * cols)
            solved_ref[:, columns] = (ref[0] + product[:, columns]) * inverse[...]


def gathered_product(own_row, blocks, offsets, shards, solved_ref):
    phases, cols = solved_ref.shape[0], blocks[0].shape[-1]
    left = split(jnp.concatenate([block[...] for block in blocks], axis=1))
    rows = [pl.ds(owner_row(own_row, offset, cols, shards), cols) for offset in offsets]
    right = split(jnp.concatenate([solved_ref[r, :] for r in rows], axis=0))
    return exact_dot(left, right)


def partial_kernel(first_rows, offsets, shards, own_row, up_ref, down_ref, *refs):
    *blocks, solved_ref, below_ref, level_ref, part_level, part_up, part_down = refs
    phases, cols = part_up.shape
    ups = [ref.at[pl.ds(first, phases), :] for first, ref in zip(first_rows, blocks)]
    downs = [ref.at[pl.ds(first + phases, phases), :] for first, ref in zip(first_rows, blocks)]
    upper = gathered_product(own_row, [up_ref.at[0], *ups], offsets, shards, solved_ref)
    part_up[...] = upper[:, :cols]
    lower = gathered_product(own_row, [down_ref.at[0], *downs], offsets, shards, below_ref)
    part_down[...] = lower[:, cols:]
    part_level[...] = level_ref[0] + upper[:, cols:] + lower[:, :cols]


def output_kernel(offset, shards, own_row, *refs):
    block, solved_ref, below_ref, part_level, part_up, part_down, peak_ref, new_level, new_up, new_down = refs
    phases, cols = part_up.shape
    scale = 1.0 / peak_ref[0:1, :]
    up, down = block.at[pl.ds(0, phases), :], block.at[pl.ds(phases, phases), :]
    upper = gathered_product(own_row, [up], [offset], shards, solved_ref)
    new_up[0] = (part_up[...] + upper[:, :cols]) * scale
    lower = gathered_product(own_row, [down], [offset], shards, below_ref)
    new_down[0] = (part_down[...] + lower[:, cols:]) * scale
    new_level[0] = (part_level[...] + upper[:, cols:] + lower[:, :cols]) * scale


def per_device(up_blocks, level_blocks, down_blocks):
    levels, phases, cols = level_blocks.shape
    assert levels == 2
    shards = lax.axis_size("col")
    ranges = lax.axis_size("lvl")
    own_row = (lax.axis_index("col") * cols).astype(jnp.int32).reshape(1)
    params = pltpu.CompilerParams(vmem_limit_bytes=32 * 2**20)
    shape = lambda *dims, kind=F32: jax.ShapeDtypeStruct(dims, kind)

    def shifted(block, distance):
        return lax.ppermute(block, "col", [(i, (i + distance) % shards) for i in range(shards)])

    def after(value, *earlier):
        return lax.optimization_barrier((value, *earlier))[0]

    def one_level(parity):
        return pl.BlockSpec((1, phases, cols), lambda step: (parity, 0, 0))

    odd, even = one_level(1), one_level(0)
    block, even_rows = shape(phases, cols), 2 * phases + PAD_ROWS
    everything, odd_block, even_blocks = pl.pallas_call(
        send_kernel,
        out_shape=(shape(phases + even_rows, cols), block, shape(even_rows, cols)),
        in_specs=[ANY] * 3,
        out_specs=(ANY,) * 3,
        scratch_shapes=[pltpu.SemaphoreType.DMA((6,))],
        grid=(1,),
        compiler_params=pltpu.CompilerParams(vmem_limit_bytes=60 * 2**20),
    )(up_blocks, level_blocks, down_blocks)
    peak = pl.pallas_call(
        peak_kernel,
        out_shape=shape(PEAK_ROWS, cols),
        in_specs=[SMEM, VMEM],
        out_specs=VMEM,
        grid=(1,),
        compiler_params=params,
    )(own_row, level_blocks)
    reach = 1
    while reach < ranges:
        route = [(i, (i + reach) % ranges) for i in range(ranges)]
        peak = jnp.maximum(peak, lax.ppermute(peak, "lvl", route))
        reach *= 2

    offsets = ring_offsets(shards)
    behind, ahead = range(1, shards // 2), range((shards - 1) // 2)
    first = shifted(everything, 1)
    level_parts, even_parts = {0: odd_block, -1: first[:phases]}, {0: even_blocks, -1: first[phases:]}

    def step(parts, reached, distance, *earlier):
        block = after(parts[reached], *earlier) if earlier else parts[reached]
        parts[reached - distance] = shifted(block, distance)

    for reached in ahead:
        step(level_parts, reached, -1)
    for reached in behind:
        step(level_parts, -reached, 1, peak)
    for reached in ahead:
        step(even_parts, reached, -1, first)
    for reached in behind:
        step(even_parts, -reached, 1)
    level_parts[0], level_parts[-1] = level_blocks, first
    for found in [shifted(peak, distance) for distance in range(1, shards)]:
        peak = jnp.maximum(peak, found)

    solved = pl.pallas_call(
        solve_kernel,
        out_shape=shape(phases, 2 * cols),
        in_specs=[SMEM, odd, *[VMEM] * (shards - 1), odd, odd],
        out_specs=VMEM,
        scratch_shapes=[
            pltpu.VMEM((phases, cols), F32),
            pltpu.VMEM((phases, phases), BF16),
            pltpu.VMEM((phases, phases), BF16),
            pltpu.VMEM((phases, 2 * cols), BF16),
            pltpu.VMEM((phases, 2 * cols), BF16),
        ],
        grid=(1,),
        compiler_params=params,
    )(own_row, *[level_parts[offset] for offset in offsets], up_blocks, down_blocks)
    from_below = lax.ppermute(solved, "lvl", [(i, i + 1) for i in range(ranges - 1)])

    last = -(shards // 2)
    early = [offset for offset in offsets[1:] if offset != last]
    first_rows = [phases if offset == -1 else 0 for offset in early]
    even_parts[-1] = first
    parts = pl.pallas_call(
        functools.partial(partial_kernel, first_rows, [0, *early], shards),
        out_shape=(block,) * 3,
        in_specs=[SMEM, even, even, *[VMEM] * (len(early) + 2), even],
        out_specs=(VMEM,) * 3,
        grid=(1,),
        compiler_params=params,
        cost_estimate=pl.CostEstimate(flops=0, bytes_accessed=0, transcendentals=0),
    )(own_row, up_blocks, down_blocks, *[even_parts[offset] for offset in early], solved, from_below, level_blocks)
    return pl.pallas_call(
        functools.partial(output_kernel, last, shards),
        out_shape=(shape(1, phases, cols),) * 3,
        in_specs=[SMEM, *[VMEM] * 7],
        out_specs=(VMEM,) * 3,
        grid=(1,),
        compiler_params=params,
    )(own_row, even_parts[last], solved, from_below, *parts, peak)


def solution(mesh):
    placed = (P("lvl", None, "col"),) * 3
    return jax.shard_map(per_device, mesh=mesh, in_specs=placed, out_specs=placed, check_vma=False)
```

```python
import functools

import jax
import jax.numpy as jnp
from jax import lax
from jax.experimental import pallas as pl
from jax.experimental.pallas import tpu as pltpu
from jax.sharding import PartitionSpec as P

SWEEPS = 2
PEAK_ROWS = 8
PAD_ROWS = 16
F32 = jnp.float32
BF16 = jnp.bfloat16
VMEM = pl.BlockSpec(memory_space=pltpu.VMEM)
ANY = pl.BlockSpec(memory_space=pl.ANY)
SMEM = pl.BlockSpec(memory_space=pltpu.SMEM)


def ring_offsets(shards):
    return [0, *[-d for d in range(1, shards // 2 + 1)], *range(1, (shards - 1) // 2 + 1)]


def split(x):
    high = x.astype(BF16)
    return high, (x - high.astype(F32)).astype(BF16)


def exact_dot(left, right):
    (left_high, left_low), (right_high, right_low) = left, right
    dot = lambda a, b: jnp.dot(a, b, preferred_element_type=F32)
    return dot(left_high, right_high) + (dot(left_high, right_low) + dot(left_low, right_high))


def on_diagonal(rows, cols):
    row = lax.broadcasted_iota(jnp.int32, (rows, cols), 0)
    return row == lax.broadcasted_iota(jnp.int32, (rows, cols), 1)


def prepare_kernel(own_row, up_ref, level_ref, down_ref, sent_ref, peak_ref, square, sems):
    _, phases, cols = level_ref.shape
    own = pl.ds(pl.multiple_of(own_row[0], cols), cols)
    sources = [level_ref.at[:, own, :], level_ref.at[1], up_ref.at[0], down_ref.at[0]]
    targets = [square, *[sent_ref.at[pl.ds(part * phases, phases), :] for part in range(3)]]
    copies = [
        pltpu.make_async_copy(source, target, sems.at[at])
        for at, (source, target) in enumerate(zip(sources, targets))
    ]
    for copy in copies:
        copy.start()
    copies[0].wait()
    lowest = jnp.min(jnp.where(on_diagonal(cols, cols)[None], square[...], 0.0))
    peak_ref[...] = jnp.full(peak_ref.shape, -lowest, F32)
    for copy in copies[1:]:
        copy.wait()


def with_peak_kernel(rows, block_row, peak_row, block_ref, peak_ref, out_ref):
    out_ref[pl.ds(0, rows), :] = block_ref[pl.ds(block_row, rows), :]
    for at in range(rows, out_ref.shape[0], PEAK_ROWS):
        out_ref[pl.ds(at, PEAK_ROWS), :] = peak_ref[pl.ds(peak_row, PEAK_ROWS), :]


def owner_row(own_row, offset, cols, shards):
    return pl.multiple_of(lax.rem(own_row[0] + (offset + shards) * cols, shards * cols), cols)


def solve_kernel(own_row, *refs):
    shards = len(refs) - 8
    blocks = [refs[0].at[0], *refs[1:shards]]
    up_ref, down_ref, solved_ref, inverse, high, low, s_high, s_low = refs[shards:]
    phases, cols = inverse.shape
    diagonal = on_diagonal(cols, cols)
    for slot, (offset, block) in enumerate(zip(ring_offsets(shards), blocks)):
        rows = pl.ds(owner_row(own_row, offset, cols, shards), cols)
        slot_cols = pl.ds(slot * cols, cols)
        high[:, slot_cols], low[:, slot_cols] = split(block[pl.ds(0, phases), :])
        square = block[rows, :]
        rate = -jnp.sum(jnp.where(diagonal, square, 0.0), axis=1, keepdims=True)
        inverse[rows, :] = jnp.broadcast_to(1.0 / rate, (cols, cols))
        high[rows, slot_cols], low[rows, slot_cols] = split(jnp.where(diagonal, 0.0, square))
    for side, ref in enumerate((up_ref, down_ref)):
        solved_ref[:, pl.ds(side * cols, cols)] = ref[0] * inverse[...]
    for _ in range(SWEEPS):
        for slot, offset in enumerate(ring_offsets(shards)):
            rows = pl.ds(owner_row(own_row, offset, cols, shards), cols)
            slot_rows = pl.ds(slot * cols, cols)
            s_high[slot_rows, :], s_low[slot_rows, :] = split(solved_ref[rows, :])
        product = exact_dot((high[...], low[...]), (s_high[...], s_low[...]))
        for side, ref in enumerate((up_ref, down_ref)):
            columns = slice(side * cols, (side + 1) * cols)
            solved_ref[:, columns] = (ref[0] + product[:, columns]) * inverse[...]


def gathered_product(own_row, blocks, offsets, shards, solved_ref):
    phases, cols = solved_ref.shape[0], blocks[0].shape[-1]
    left = split(jnp.concatenate([block[...] for block in blocks], axis=1))
    rows = [pl.ds(owner_row(own_row, offset, cols, shards), cols) for offset in offsets]
    right = split(jnp.concatenate([solved_ref[r, :] for r in rows], axis=0))
    return exact_dot(left, right)


def largest(peak, blocks, row):
    for block in blocks:
        peak = jnp.maximum(peak, block[pl.ds(row, PEAK_ROWS), :])
    return peak


def partial_kernel(shards, own_row, up_ref, down_ref, peak_ref, *refs):
    *blocks, solved_ref, below_ref, level_ref, part_level, part_up, part_down, part_peak = refs
    phases, cols = part_up.shape
    offsets = [offset for offset in ring_offsets(shards) if offset != -(shards // 2)]
    levels, evens = blocks[: shards // 2 - 1], blocks[shards // 2 - 1 :]
    peak = largest(peak_ref[...], levels, phases)
    part_peak[...] = largest(peak, evens[1:], 2 * phases)
    first_rows = [phases if offset == -1 else 0 for offset in offsets[1:]]
    ups = [ref.at[pl.ds(first, phases), :] for first, ref in zip(first_rows, evens)]
    downs = [ref.at[pl.ds(first + phases, phases), :] for first, ref in zip(first_rows, evens)]
    upper = gathered_product(own_row, [up_ref.at[0], *ups], offsets, shards, solved_ref)
    part_up[...] = upper[:, :cols]
    lower = gathered_product(own_row, [down_ref.at[0], *downs], offsets, shards, below_ref)
    part_down[...] = lower[:, cols:]
    part_level[...] = level_ref[0] + upper[:, cols:] + lower[:, :cols]


def output_kernel(shards, own_row, *refs):
    block, solved_ref, below_ref, part_level, part_up, part_down, part_peak, new_level, new_up, new_down = refs
    phases, cols = part_up.shape
    offsets = [-(shards // 2)]
    scale = 1.0 / largest(part_peak[...], [block], 2 * phases)[0:1, :]
    up, down = block.at[pl.ds(0, phases), :], block.at[pl.ds(phases, phases), :]
    upper = gathered_product(own_row, [up], offsets, shards, solved_ref)
    new_up[0] = (part_up[...] + upper[:, :cols]) * scale
    lower = gathered_product(own_row, [down], offsets, shards, below_ref)
    new_down[0] = (part_down[...] + lower[:, cols:]) * scale
    new_level[0] = (part_level[...] + upper[:, cols:] + lower[:, :cols]) * scale


def per_device(up_blocks, level_blocks, down_blocks):
    levels, phases, cols = level_blocks.shape
    shards = lax.axis_size("col")
    ranges = lax.axis_size("lvl")
    assert levels == 2 and shards >= 4
    own_row = (lax.axis_index("col") * cols).astype(jnp.int32).reshape(1)
    params = pltpu.CompilerParams(vmem_limit_bytes=32 * 2**20)
    shape = lambda *dims, kind=F32: jax.ShapeDtypeStruct(dims, kind)
    block = shape(phases, cols)

    def shifted(part, distance):
        return lax.ppermute(part, "col", [(i, (i + distance) % shards) for i in range(shards)])

    def one_level(parity):
        return pl.BlockSpec((1, phases, cols), lambda step: (parity, 0, 0))

    odd, even = one_level(1), one_level(0)
    sent, peak = pl.pallas_call(
        prepare_kernel,
        out_shape=(shape(3 * phases, cols), shape(PEAK_ROWS, cols)),
        in_specs=[SMEM] + [ANY] * 3,
        out_specs=(VMEM, VMEM),
        scratch_shapes=[pltpu.VMEM((levels, cols, cols), F32), pltpu.SemaphoreType.DMA((4,))],
        grid=(1,),
        compiler_params=params,
    )(own_row, *[pltpu.with_memory_space_constraint(x, pltpu.HBM) for x in (up_blocks, level_blocks, down_blocks)])

    first = shifted(sent, 1)
    reach = 1
    while reach < ranges:
        route = [(i, (i + reach) % ranges) for i in range(ranges)]
        peak = jnp.maximum(peak, lax.ppermute(peak, "lvl", route))
        reach *= 2

    def with_peak(rows, extra, part, block_row, rates, peak_row):
        return pl.pallas_call(
            functools.partial(with_peak_kernel, rows, block_row, peak_row),
            out_shape=shape(rows + extra, cols),
            in_specs=[VMEM, VMEM],
            out_specs=VMEM,
            grid=(1,),
            compiler_params=params,
        )(part, rates)

    level_parts = {-1: first}
    even_parts = {-1: first}
    rates, peak_row = peak, 0
    for reached in range(1, shards // 2):
        part = with_peak(phases, PEAK_ROWS, level_parts[-reached], 0, rates, peak_row)
        rates = level_parts[-reached - 1] = shifted(part, 1)
        peak_row = phases
    level_parts[1] = shifted(sent[: phases + 2 * PAD_ROWS], -1)
    even_now = lax.optimization_barrier((sent, first))[0]
    even_parts[1] = shifted(with_peak(2 * phases, PAD_ROWS, even_now, phases, peak, 0), -1)
    for reached in range(1, (shards - 1) // 2):
        level_parts[reached + 1] = shifted(level_parts[reached], -1)
        even_parts[reached + 1] = shifted(even_parts[reached], -1)
    for reached in range(1, shards // 2):
        block_row = phases if reached == 1 else 0
        part = with_peak(2 * phases, PAD_ROWS, even_parts[-reached], block_row, rates, peak_row)
        even_parts[-reached - 1] = shifted(part, 1)

    offsets = ring_offsets(shards)[1:]
    solved = pl.pallas_call(
        solve_kernel,
        out_shape=shape(phases, 2 * cols),
        in_specs=[SMEM, odd, *[VMEM] * (shards - 1), odd, odd],
        out_specs=VMEM,
        scratch_shapes=[
            pltpu.VMEM((phases, cols), F32),
            pltpu.VMEM((phases, phases), BF16),
            pltpu.VMEM((phases, phases), BF16),
            pltpu.VMEM((phases, 2 * cols), BF16),
            pltpu.VMEM((phases, 2 * cols), BF16),
        ],
        grid=(1,),
        compiler_params=params,
    )(own_row, level_blocks, *[level_parts[offset] for offset in offsets], up_blocks, down_blocks)
    from_below = lax.ppermute(solved, "lvl", [(i, i + 1) for i in range(ranges - 1)])

    last = -(shards // 2)
    early = [level_parts[offset] for offset in offsets if offset < -1]
    early += [even_parts[offset] for offset in offsets if offset != last]
    parts = pl.pallas_call(
        functools.partial(partial_kernel, shards),
        out_shape=(block, block, block, shape(PEAK_ROWS, cols)),
        in_specs=[SMEM, even, even, *[VMEM] * (len(early) + 3), even],
        out_specs=(VMEM,) * 4,
        grid=(1,),
        compiler_params=params,
        cost_estimate=pl.CostEstimate(flops=0, bytes_accessed=0, transcendentals=0),
    )(own_row, up_blocks, down_blocks, peak, *early, solved, from_below, level_blocks)
    return pl.pallas_call(
        functools.partial(output_kernel, shards),
        out_shape=(shape(1, phases, cols),) * 3,
        in_specs=[SMEM, *[VMEM] * 7],
        out_specs=(VMEM,) * 3,
        grid=(1,),
        compiler_params=params,
    )(own_row, even_parts[last], solved, from_below, *parts)


def solution(mesh):
    placed = (P("lvl", None, "col"),) * 3
    return jax.shard_map(per_device, mesh=mesh, in_specs=placed, out_specs=placed, check_vma=False)
```

```python
import functools

import jax
import jax.numpy as jnp
from jax import lax
from jax.experimental import pallas as pl
from jax.experimental.pallas import tpu as pltpu
from jax.sharding import PartitionSpec as P

SWEEPS = 2
PEAK_ROWS = 8
PAD_ROWS = 16
F32 = jnp.float32
BF16 = jnp.bfloat16
VMEM = pl.BlockSpec(memory_space=pltpu.VMEM)
ANY = pl.BlockSpec(memory_space=pl.ANY)
SMEM = pl.BlockSpec(memory_space=pltpu.SMEM)


def ring_offsets(shards):
    return [0, *[-d for d in range(1, shards // 2 + 1)], *range(1, (shards - 1) // 2 + 1)]


def split(x):
    high = x.astype(BF16)
    return high, (x - high.astype(F32)).astype(BF16)


def exact_dot(left, right):
    (left_high, left_low), (right_high, right_low) = left, right
    dot = lambda a, b: jnp.dot(a, b, preferred_element_type=F32)
    return dot(left_high, right_high) + (dot(left_high, right_low) + dot(left_low, right_high))


def on_diagonal(rows, cols):
    row = lax.broadcasted_iota(jnp.int32, (rows, cols), 0)
    return row == lax.broadcasted_iota(jnp.int32, (rows, cols), 1)


def prepare_kernel(own_row, up_ref, level_ref, down_ref, sent_ref, peak_ref, square, sems):
    _, phases, cols = level_ref.shape
    own = pl.ds(pl.multiple_of(own_row[0], cols), cols)
    sources = [level_ref.at[:, own, :], level_ref.at[1], up_ref.at[0], down_ref.at[0]]
    targets = [square, *[sent_ref.at[pl.ds(part * phases, phases), :] for part in range(3)]]
    copies = [
        pltpu.make_async_copy(source, target, sems.at[at])
        for at, (source, target) in enumerate(zip(sources, targets))
    ]
    for copy in copies:
        copy.start()
    copies[0].wait()
    lowest = jnp.min(jnp.where(on_diagonal(cols, cols)[None], square[...], 0.0))
    peak_ref[...] = jnp.full(peak_ref.shape, -lowest, F32)
    for copy in copies[1:]:
        copy.wait()


def with_peak_kernel(rows, block_row, peak_row, block_ref, peak_ref, out_ref):
    out_ref[pl.ds(0, rows), :] = block_ref[pl.ds(block_row, rows), :]
    for at in range(rows, out_ref.shape[0], PEAK_ROWS):
        out_ref[pl.ds(at, PEAK_ROWS), :] = peak_ref[pl.ds(peak_row, PEAK_ROWS), :]


def owner_row(own_row, offset, cols, shards):
    return pl.multiple_of(lax.rem(own_row[0] + (offset + shards) * cols, shards * cols), cols)


def solve_kernel(own_row, *refs):
    shards = len(refs) - 8
    blocks = [refs[0].at[0], *refs[1:shards]]
    up_ref, down_ref, solved_ref, inverse, high, low, s_high, s_low = refs[shards:]
    phases, cols = inverse.shape
    diagonal = on_diagonal(cols, cols)
    for slot, (offset, block) in enumerate(zip(ring_offsets(shards), blocks)):
        rows = pl.ds(owner_row(own_row, offset, cols, shards), cols)
        slot_cols = pl.ds(slot * cols, cols)
        high[:, slot_cols], low[:, slot_cols] = split(block[pl.ds(0, phases), :])
        square = block[rows, :]
        rate = -jnp.sum(jnp.where(diagonal, square, 0.0), axis=1, keepdims=True)
        inverse[rows, :] = jnp.broadcast_to(1.0 / rate, (cols, cols))
        high[rows, slot_cols], low[rows, slot_cols] = split(jnp.where(diagonal, 0.0, square))
    for side, ref in enumerate((up_ref, down_ref)):
        solved_ref[:, pl.ds(side * cols, cols)] = ref[0] * inverse[...]
    for _ in range(SWEEPS):
        for slot, offset in enumerate(ring_offsets(shards)):
            rows = pl.ds(owner_row(own_row, offset, cols, shards), cols)
            slot_rows = pl.ds(slot * cols, cols)
            s_high[slot_rows, :], s_low[slot_rows, :] = split(solved_ref[rows, :])
        product = exact_dot((high[...], low[...]), (s_high[...], s_low[...]))
        for side, ref in enumerate((up_ref, down_ref)):
            columns = slice(side * cols, (side + 1) * cols)
            solved_ref[:, columns] = (ref[0] + product[:, columns]) * inverse[...]


def gathered_product(own_row, blocks, offsets, shards, solved_ref):
    phases, cols = solved_ref.shape[0], blocks[0].shape[-1]
    left = split(jnp.concatenate([block[...] for block in blocks], axis=1))
    rows = [pl.ds(owner_row(own_row, offset, cols, shards), cols) for offset in offsets]
    right = split(jnp.concatenate([solved_ref[r, :] for r in rows], axis=0))
    return exact_dot(left, right)


def largest(peak, blocks, row):
    for block in blocks:
        peak = jnp.maximum(peak, block[pl.ds(row, PEAK_ROWS), :])
    return peak


def partial_kernel(shards, own_row, up_ref, down_ref, peak_ref, *refs):
    *blocks, solved_ref, below_ref, level_ref, part_level, part_up, part_down, part_peak = refs
    phases, cols = part_up.shape
    offsets = [offset for offset in ring_offsets(shards) if offset != -(shards // 2)]
    levels, evens = blocks[: shards // 2 - 1], blocks[shards // 2 - 1 :]
    peak = largest(peak_ref[...], levels, phases)
    part_peak[...] = largest(peak, evens[1:], 2 * phases)
    first_rows = [phases if offset == -1 else 0 for offset in offsets[1:]]
    ups = [ref.at[pl.ds(first, phases), :] for first, ref in zip(first_rows, evens)]
    downs = [ref.at[pl.ds(first + phases, phases), :] for first, ref in zip(first_rows, evens)]
    upper = gathered_product(own_row, [up_ref.at[0], *ups], offsets, shards, solved_ref)
    part_up[...] = upper[:, :cols]
    lower = gathered_product(own_row, [down_ref.at[0], *downs], offsets, shards, below_ref)
    part_down[...] = lower[:, cols:]
    part_level[...] = level_ref[0] + upper[:, cols:] + lower[:, :cols]


def output_kernel(shards, own_row, *refs):
    block, solved_ref, below_ref, part_level, part_up, part_down, part_peak, new_level, new_up, new_down = refs
    phases, cols = part_up.shape
    offsets = [-(shards // 2)]
    scale = 1.0 / largest(part_peak[...], [block], 2 * phases)[0:1, :]
    up, down = block.at[pl.ds(0, phases), :], block.at[pl.ds(phases, phases), :]
    upper = gathered_product(own_row, [up], offsets, shards, solved_ref)
    new_up[0] = (part_up[...] + upper[:, :cols]) * scale
    lower = gathered_product(own_row, [down], offsets, shards, below_ref)
    new_down[0] = (part_down[...] + lower[:, cols:]) * scale
    new_level[0] = (part_level[...] + upper[:, cols:] + lower[:, :cols]) * scale


def per_device(up_blocks, level_blocks, down_blocks):
    levels, phases, cols = level_blocks.shape
    shards = lax.axis_size("col")
    ranges = lax.axis_size("lvl")
    assert levels == 2 and shards >= 4
    own_row = (lax.axis_index("col") * cols).astype(jnp.int32).reshape(1)
    params = pltpu.CompilerParams(vmem_limit_bytes=32 * 2**20)
    shape = lambda *dims, kind=F32: jax.ShapeDtypeStruct(dims, kind)
    block = shape(phases, cols)

    def shifted(part, distance):
        return lax.ppermute(part, "col", [(i, (i + distance) % shards) for i in range(shards)])

    def one_level(parity):
        return pl.BlockSpec((1, phases, cols), lambda step: (parity, 0, 0))

    odd, even = one_level(1), one_level(0)
    sent, peak = pl.pallas_call(
        prepare_kernel,
        out_shape=(shape(3 * phases, cols), shape(PEAK_ROWS, cols)),
        in_specs=[SMEM] + [ANY] * 3,
        out_specs=(VMEM, VMEM),
        scratch_shapes=[pltpu.VMEM((levels, cols, cols), F32), pltpu.SemaphoreType.DMA((4,))],
        grid=(1,),
        compiler_params=params,
    )(own_row, *[pltpu.with_memory_space_constraint(x, pltpu.HBM) for x in (up_blocks, level_blocks, down_blocks)])

    first = shifted(sent, 1)
    reach = 1
    while reach < ranges:
        route = [(i, (i + reach) % ranges) for i in range(ranges)]
        peak = jnp.maximum(peak, lax.ppermute(peak, "lvl", route))
        reach *= 2

    def with_peak(rows, extra, part, block_row, rates, peak_row):
        return pl.pallas_call(
            functools.partial(with_peak_kernel, rows, block_row, peak_row),
            out_shape=shape(rows + extra, cols),
            in_specs=[VMEM, VMEM],
            out_specs=VMEM,
            grid=(1,),
            compiler_params=params,
        )(part, rates)

    level_parts = {-1: first}
    even_parts = {-1: first}
    rates, peak_row = peak, 0
    for reached in range(1, shards // 2):
        part = with_peak(phases, PEAK_ROWS, level_parts[-reached], 0, rates, peak_row)
        rates = level_parts[-reached - 1] = shifted(part, 1)
        peak_row = phases
    level_now = lax.optimization_barrier((sent, peak))[0]
    level_parts[1] = shifted(level_now[: phases + 2 * PAD_ROWS], -1)
    even_now = lax.optimization_barrier((sent, level_parts[1]))[0]
    even_parts[1] = shifted(with_peak(2 * phases, PAD_ROWS, even_now, phases, peak, 0), -1)
    for reached in range(1, (shards - 1) // 2):
        level_parts[reached + 1] = shifted(level_parts[reached], -1)
        even_parts[reached + 1] = shifted(even_parts[reached], -1)
    for reached in range(1, shards // 2):
        block_row = phases if reached == 1 else 0
        part = with_peak(2 * phases, PAD_ROWS, even_parts[-reached], block_row, rates, peak_row)
        even_parts[-reached - 1] = shifted(part, 1)

    offsets = ring_offsets(shards)[1:]
    solved = pl.pallas_call(
        solve_kernel,
        out_shape=shape(phases, 2 * cols),
        in_specs=[SMEM, odd, *[VMEM] * (shards - 1), odd, odd],
        out_specs=VMEM,
        scratch_shapes=[
            pltpu.VMEM((phases, cols), F32),
            pltpu.VMEM((phases, phases), BF16),
            pltpu.VMEM((phases, phases), BF16),
            pltpu.VMEM((phases, 2 * cols), BF16),
            pltpu.VMEM((phases, 2 * cols), BF16),
        ],
        grid=(1,),
        compiler_params=params,
    )(own_row, level_blocks, *[level_parts[offset] for offset in offsets], up_blocks, down_blocks)
    from_below = lax.ppermute(solved, "lvl", [(i, i + 1) for i in range(ranges - 1)])

    last = -(shards // 2)
    early = [level_parts[offset] for offset in offsets if offset < -1]
    early += [even_parts[offset] for offset in offsets if offset != last]
    parts = pl.pallas_call(
        functools.partial(partial_kernel, shards),
        out_shape=(block, block, block, shape(PEAK_ROWS, cols)),
        in_specs=[SMEM, even, even, *[VMEM] * (len(early) + 3), even],
        out_specs=(VMEM,) * 4,
        grid=(1,),
        compiler_params=params,
        cost_estimate=pl.CostEstimate(flops=0, bytes_accessed=0, transcendentals=0),
    )(own_row, up_blocks, down_blocks, peak, *early, solved, from_below, level_blocks)
    return pl.pallas_call(
        functools.partial(output_kernel, shards),
        out_shape=(shape(1, phases, cols),) * 3,
        in_specs=[SMEM, *[VMEM] * 7],
        out_specs=(VMEM,) * 3,
        grid=(1,),
        compiler_params=params,
    )(own_row, even_parts[last], solved, from_below, *parts)


def solution(mesh):
    placed = (P("lvl", None, "col"),) * 3
    return jax.shard_map(per_device, mesh=mesh, in_specs=placed, out_specs=placed, check_vma=False)
```

```python
import functools

import jax
import jax.numpy as jnp
from jax import lax
from jax.experimental import pallas as pl
from jax.experimental.pallas import tpu as pltpu
from jax.sharding import PartitionSpec as P

SWEEPS = 2
PEAK_ROWS = 8
F32 = jnp.float32
BF16 = jnp.bfloat16
VMEM = pl.BlockSpec(memory_space=pltpu.VMEM)
ANY = pl.BlockSpec(memory_space=pl.ANY)
SMEM = pl.BlockSpec(memory_space=pltpu.SMEM)


def split(x):
    high = x.astype(BF16)
    return high, (x - high.astype(F32)).astype(BF16)


def exact_dot(left, right):
    (left_high, left_low), (right_high, right_low) = left, right
    dot = lambda a, b: jnp.dot(a, b, preferred_element_type=F32)
    return dot(left_high, right_high) + (dot(left_high, right_low) + dot(left_low, right_high))


def on_diagonal(rows, cols):
    row = lax.broadcasted_iota(jnp.int32, (rows, cols), 0)
    return row == lax.broadcasted_iota(jnp.int32, (rows, cols), 1)


def prepare_kernel(place, up_ref, level_ref, down_ref, first_ref, down_out_ref, peak_ref, square, sems):
    _, phases, cols = level_ref.shape
    own = pl.ds(pl.multiple_of(place[0] * cols, cols), cols)
    sources = [level_ref.at[:, own, :], level_ref.at[1], up_ref.at[0], down_ref.at[0]]
    targets = [square, first_ref.at[pl.ds(0, phases), :], first_ref.at[pl.ds(phases, phases), :], down_out_ref]
    copies = [
        pltpu.make_async_copy(source, target, sems.at[at])
        for at, (source, target) in enumerate(zip(sources, targets))
    ]
    for copy in copies:
        copy.start()
    copies[0].wait()
    lowest = jnp.min(jnp.where(on_diagonal(cols, cols)[None], square[...], 0.0))
    peak_ref[...] = jnp.full(peak_ref.shape, -lowest, F32)
    for copy in copies[1:]:
        copy.wait()


def stack_kernel(ranges, *refs):
    *parts, out_ref = refs
    at = 0
    for (first, rows), ref in zip(ranges, parts):
        out_ref[pl.ds(at, rows), :] = ref[pl.ds(first, rows), :]
        at += rows


def either_kernel(place, right_ref, left_ref, out_ref):
    out_ref[...] = jnp.where(place[0] >= 2, right_ref[...], left_ref[...])


def rows_of(place, offset, cols, shards):
    owner = lax.rem(place[0] + (offset + shards), shards)
    return pl.ds(pl.multiple_of(owner * cols, cols), cols)


def solve_kernel(shards, place, own_ref, right_ref, left_ref, far_ref, end_ref, up_ref, down_ref, solved_ref, *scratch):
    inverse, high, low, s_high, s_low = scratch
    phases, cols = inverse.shape
    diagonal = on_diagonal(cols, cols)
    offsets = (0, -1, 1, 2)

    def block(slot, rows):
        if slot == 0:
            return own_ref[0, rows, :]
        if slot == 1:
            return jnp.where(place[0] == 0, end_ref[rows, :], right_ref[rows, :])
        if slot == 2:
            return jnp.where(place[0] == shards - 1, end_ref[rows, :], left_ref[rows, :])
        return far_ref[rows, :]

    for slot, offset in enumerate(offsets):
        rows = rows_of(place, offset, cols, shards)
        slot_cols = pl.ds(slot * cols, cols)
        high[:, slot_cols], low[:, slot_cols] = split(block(slot, pl.ds(0, phases)))
        square = block(slot, rows)
        rate = -jnp.sum(jnp.where(diagonal, square, 0.0), axis=1, keepdims=True)
        inverse[rows, :] = jnp.broadcast_to(1.0 / rate, (cols, cols))
        high[rows, slot_cols], low[rows, slot_cols] = split(jnp.where(diagonal, 0.0, square))
    for side, ref in enumerate((up_ref, down_ref)):
        solved_ref[:, pl.ds(side * cols, cols)] = ref[0] * inverse[...]
    for _ in range(SWEEPS):
        for slot, offset in enumerate(offsets):
            rows, slot_rows = rows_of(place, offset, cols, shards), pl.ds(slot * cols, cols)
            s_high[slot_rows, :], s_low[slot_rows, :] = split(solved_ref[rows, :])
        product = exact_dot((high[...], low[...]), (s_high[...], s_low[...]))
        for side, ref in enumerate((up_ref, down_ref)):
            columns = slice(side * cols, (side + 1) * cols)
            solved_ref[:, columns] = (ref[0] + product[:, columns]) * inverse[...]


def gathered_product(blocks, rows, solved_ref):
    left = split(jnp.concatenate(blocks, axis=1))
    right = split(jnp.concatenate([solved_ref[r, :] for r in rows], axis=0))
    return exact_dot(left, right)


def partial_kernel(shards, place, up_ref, down_ref, peak_ref, first_right, first_left, down_right, down_left, far_ref, *refs):
    solved_ref, below_ref, level_ref, part_level, part_up, part_down, part_peak = refs
    phases, cols = part_up.shape
    rows = [rows_of(place, offset, cols, shards) for offset in (0, -1, 1, 2)]
    top, middle = pl.ds(0, phases), pl.ds(phases, phases)
    ups = [up_ref[0], first_right[middle, :], first_left[middle, :], far_ref[top, :]]
    downs = [down_ref[0], down_right[top, :], down_left[top, :], far_ref[middle, :]]
    upper = gathered_product(ups, rows, solved_ref)
    part_up[...] = upper[:, :cols]
    lower = gathered_product(downs, rows, below_ref)
    part_down[...] = lower[:, cols:]
    part_level[...] = level_ref[0] + upper[:, cols:] + lower[:, :cols]
    peak = peak_ref[...]
    for ref, row in ((down_right, phases), (down_left, phases), (far_ref, 2 * phases)):
        peak = jnp.maximum(peak, ref[pl.ds(row, PEAK_ROWS), :])
    part_peak[...] = peak


def output_kernel(shards, place, end_ref, solved_ref, below_ref, *refs):
    part_level, part_up, part_down, part_peak, new_level, new_up, new_down = refs
    phases, cols = part_up.shape
    peak = jnp.maximum(part_peak[...], end_ref[pl.ds(2 * phases, PEAK_ROWS), :])
    scale = 1.0 / peak[0:1, :]
    last = pl.multiple_of(jnp.where(place[0] == 0, (shards - 1) * cols, 0), cols)
    rows = [pl.ds(last, cols)]
    upper = gathered_product([end_ref[pl.ds(0, phases), :]], rows, solved_ref)
    new_up[0] = (part_up[...] + upper[:, :cols]) * scale
    lower = gathered_product([end_ref[pl.ds(phases, phases), :]], rows, below_ref)
    new_down[0] = (part_down[...] + lower[:, cols:]) * scale
    new_level[0] = (part_level[...] + upper[:, cols:] + lower[:, :cols]) * scale


def per_device(up_blocks, level_blocks, down_blocks):
    levels, phases, cols = level_blocks.shape
    shards = lax.axis_size("col")
    ranges = lax.axis_size("lvl")
    assert levels == 2 and shards == 4
    place = lax.axis_index("col").astype(jnp.int32).reshape(1)
    params = pltpu.CompilerParams(vmem_limit_bytes=32 * 2**20)
    shape = lambda rows, columns=cols: jax.ShapeDtypeStruct((rows, columns), F32)

    def call(kernel, out_shape, in_specs, *operands, scratch=(), **options):
        out_specs = jax.tree.map(lambda _: VMEM, out_shape)
        return pl.pallas_call(
            kernel,
            out_shape=out_shape,
            in_specs=in_specs,
            out_specs=out_specs,
            scratch_shapes=scratch,
            grid=(1,),
            compiler_params=params,
            **options,
        )(*operands)

    def one_level(parity):
        return pl.BlockSpec((1, phases, cols), lambda step: (parity, 0, 0))

    def to_right(part, step):
        return lax.ppermute(part, "col", [(i, i + 1) for i in range(step - 1, shards - 1)])

    def to_left(part, step):
        return lax.ppermute(part, "col", [(i, i - 1) for i in range(1, shards - step + 1)])

    def to_ends(part):
        return lax.ppermute(part, "col", [(1, 0), (shards - 2, shards - 1)])

    def stack(*pieces):
        ranges_of = [(first, rows) for _, first, rows in pieces]
        kernel = functools.partial(stack_kernel, ranges_of)
        return call(kernel, shape(sum(rows for _, rows in ranges_of)), [VMEM] * len(pieces), *[p[0] for p in pieces])

    def either(right, left):
        return call(either_kernel, shape(right.shape[0]), [SMEM, VMEM, VMEM], place, right, left)

    odd, even = one_level(1), one_level(0)
    in_hbm = [pltpu.with_memory_space_constraint(x, pltpu.HBM) for x in (up_blocks, level_blocks, down_blocks)]
    first, down, peak = call(
        prepare_kernel,
        (shape(2 * phases), shape(phases), shape(PEAK_ROWS)),
        [SMEM] + [ANY] * 3,
        place,
        *in_hbm,
        scratch=[pltpu.VMEM((levels, cols, cols), F32), pltpu.SemaphoreType.DMA((4,))],
    )
    first_right, first_left = to_right(first, 1), to_left(first, 1)
    reach = 1
    while reach < ranges:
        route = [(i, (i + reach) % ranges) for i in range(ranges)]
        peak = jnp.maximum(peak, lax.ppermute(peak, "lvl", route))
        reach *= 2
    down = stack((down, 0, phases), (peak, 0, PEAK_ROWS))
    down_right, down_left = to_right(down, 1), to_left(down, 1)

    level_far = either(to_right(first_right[:phases], 2), to_left(first_left[:phases], 2))
    level_end = to_ends(level_far)
    even_right = stack((first_right, phases, phases), (down_right, 0, phases + PEAK_ROWS))
    even_left = stack((first_left, phases, phases), (down_left, 0, phases + PEAK_ROWS))
    even_far = either(to_right(even_right, 2), to_left(even_left, 2))
    even_end = to_ends(even_far)

    solved = call(
        functools.partial(solve_kernel, shards),
        shape(phases, 2 * cols),
        [SMEM, odd, *[VMEM] * 4, odd, odd],
        place,
        level_blocks,
        first_right,
        first_left,
        level_far,
        level_end,
        up_blocks,
        down_blocks,
        scratch=[
            pltpu.VMEM((phases, cols), F32),
            pltpu.VMEM((phases, phases), BF16),
            pltpu.VMEM((phases, phases), BF16),
            pltpu.VMEM((phases, 2 * cols), BF16),
            pltpu.VMEM((phases, 2 * cols), BF16),
        ],
    )
    from_below = lax.ppermute(solved, "lvl", [(i, i + 1) for i in range(ranges - 1)])

    parts = call(
        functools.partial(partial_kernel, shards),
        (shape(phases),) * 3 + (shape(PEAK_ROWS),),
        [SMEM, even, even, *[VMEM] * 8, even],
        place,
        up_blocks,
        down_blocks,
        peak,
        first_right,
        first_left,
        down_right,
        down_left,
        even_far,
        solved,
        from_below,
        level_blocks,
        cost_estimate=pl.CostEstimate(flops=0, bytes_accessed=0, transcendentals=0),
    )
    return call(
        functools.partial(output_kernel, shards),
        (jax.ShapeDtypeStruct((1, phases, cols), F32),) * 3,
        [SMEM] + [VMEM] * 7,
        place,
        even_end,
        solved,
        from_below,
        *parts,
    )


def solution(mesh):
    placed = (P("lvl", None, "col"),) * 3
    return jax.shard_map(per_device, mesh=mesh, in_specs=placed, out_specs=placed, check_vma=False)
```

```python
import functools

import jax
import jax.numpy as jnp
from jax import lax
from jax.experimental import pallas as pl
from jax.experimental.pallas import tpu as pltpu
from jax.sharding import PartitionSpec as P

SWEEPS = 2
PEAK_ROWS = 8
SLOTS = 4
F32 = jnp.float32
BF16 = jnp.bfloat16
VMEM = pl.BlockSpec(memory_space=pltpu.VMEM)
ANY = pl.BlockSpec(memory_space=pl.ANY)
SMEM = pl.BlockSpec(memory_space=pltpu.SMEM)


def split(x):
    high = x.astype(BF16)
    return high, (x - high.astype(F32)).astype(BF16)


def exact_dot(left, right):
    (left_high, left_low), (right_high, right_low) = left, right
    dot = lambda a, b: jnp.dot(a, b, preferred_element_type=F32)
    return dot(left_high, right_high) + (dot(left_high, right_low) + dot(left_low, right_high))


def on_diagonal(rows, cols):
    row = lax.broadcasted_iota(jnp.int32, (rows, cols), 0)
    return row == lax.broadcasted_iota(jnp.int32, (rows, cols), 1)


def prepare_kernel(owners, up_ref, level_ref, down_ref, sent_ref, peak_ref, square, sems):
    _, phases, cols = level_ref.shape
    own = rows_of(owners, 0, cols)
    sources = [level_ref.at[:, own, :], level_ref.at[1], up_ref.at[0], down_ref.at[0]]
    targets = [square, *[sent_ref.at[pl.ds(part * phases, phases), :] for part in range(3)]]
    copies = [
        pltpu.make_async_copy(source, target, sems.at[at])
        for at, (source, target) in enumerate(zip(sources, targets))
    ]
    for copy in copies:
        copy.start()
    copies[0].wait()
    lowest = jnp.min(jnp.where(on_diagonal(cols, cols)[None], square[...], 0.0))
    peak_ref[...] = jnp.full(peak_ref.shape, -lowest, F32)
    for copy in copies[1:]:
        copy.wait()


def stack_kernel(ranges, *refs):
    *parts, out_ref = refs
    at = 0
    for (first, rows), ref in zip(ranges, parts):
        out_ref[pl.ds(at, rows), :] = ref[pl.ds(first, rows), :]
        at += rows


def rows_of(owners, slot, cols):
    return pl.ds(pl.multiple_of(owners[slot] * cols, cols), cols)


def solve_kernel(owners, own_ref, *refs):
    *others, up_ref, down_ref, solved_ref, inverse, high, low, s_high, s_low = refs
    phases, cols = inverse.shape
    diagonal = on_diagonal(cols, cols)
    blocks = [own_ref.at[0], *others]
    for slot, block in enumerate(blocks):
        rows, slot_cols = rows_of(owners, slot, cols), pl.ds(slot * cols, cols)
        high[:, slot_cols], low[:, slot_cols] = split(block[pl.ds(0, phases), :])
        square = block[rows, :]
        rate = -jnp.sum(jnp.where(diagonal, square, 0.0), axis=1, keepdims=True)
        inverse[rows, :] = jnp.broadcast_to(1.0 / rate, (cols, cols))
        high[rows, slot_cols], low[rows, slot_cols] = split(jnp.where(diagonal, 0.0, square))
    for side, ref in enumerate((up_ref, down_ref)):
        solved_ref[:, pl.ds(side * cols, cols)] = ref[0] * inverse[...]
    for _ in range(SWEEPS):
        for slot in range(len(blocks)):
            rows, slot_rows = rows_of(owners, slot, cols), pl.ds(slot * cols, cols)
            s_high[slot_rows, :], s_low[slot_rows, :] = split(solved_ref[rows, :])
        product = exact_dot((high[...], low[...]), (s_high[...], s_low[...]))
        for side, ref in enumerate((up_ref, down_ref)):
            columns = slice(side * cols, (side + 1) * cols)
            solved_ref[:, columns] = (ref[0] + product[:, columns]) * inverse[...]


def gathered_product(owners, blocks, first_slot, solved_ref):
    cols = blocks[0].shape[-1]
    left = split(jnp.concatenate(blocks, axis=1))
    rows = [rows_of(owners, first_slot + at, cols) for at in range(len(blocks))]
    right = split(jnp.concatenate([solved_ref[r, :] for r in rows], axis=0))
    return exact_dot(left, right)


def partial_kernel(owners, up_ref, down_ref, peak_ref, level_near, near_ref, far_ref, *refs):
    solved_ref, below_ref, level_ref, part_level, part_up, part_down, part_peak = refs
    phases, cols = part_up.shape
    part = lambda ref, at: ref[pl.ds(at * phases, phases), :]
    upper = gathered_product(owners, [up_ref[0], part(near_ref, 1), part(far_ref, 0)], 0, solved_ref)
    part_up[...] = upper[:, :cols]
    lower = gathered_product(owners, [down_ref[0], part(near_ref, 2), part(far_ref, 1)], 0, below_ref)
    part_down[...] = lower[:, cols:]
    part_level[...] = level_ref[0] + upper[:, cols:] + lower[:, :cols]
    others = [level_near[pl.ds(phases, PEAK_ROWS), :], far_ref[pl.ds(2 * phases, PEAK_ROWS), :]]
    part_peak[...] = jnp.maximum(peak_ref[...], jnp.maximum(*others))


def output_kernel(owners, last_ref, solved_ref, below_ref, *refs):
    part_level, part_up, part_down, part_peak, new_level, new_up, new_down = refs
    phases, cols = part_up.shape
    peak = jnp.maximum(part_peak[...], last_ref[pl.ds(2 * phases, PEAK_ROWS), :])
    scale = 1.0 / peak[0:1, :]
    last = SLOTS - 1
    upper = gathered_product(owners, [last_ref[pl.ds(0, phases), :]], last, solved_ref)
    new_up[0] = (part_up[...] + upper[:, :cols]) * scale
    lower = gathered_product(owners, [last_ref[pl.ds(phases, phases), :]], last, below_ref)
    new_down[0] = (part_down[...] + lower[:, cols:]) * scale
    new_level[0] = (part_level[...] + upper[:, cols:] + lower[:, :cols]) * scale


def per_device(up_blocks, level_blocks, down_blocks):
    levels, phases, cols = level_blocks.shape
    shards = lax.axis_size("col")
    ranges = lax.axis_size("lvl")
    assert levels == 2 and shards == SLOTS
    place = lax.axis_index("col").astype(jnp.int32)
    owners = jnp.stack([place ^ distance for distance in (0, 1, 3, 2)])
    params = pltpu.CompilerParams(vmem_limit_bytes=32 * 2**20)
    shape = lambda rows, columns=cols: jax.ShapeDtypeStruct((rows, columns), F32)

    def call(kernel, out_shape, in_specs, *operands, scratch=(), **options):
        return pl.pallas_call(
            kernel,
            out_shape=out_shape,
            in_specs=in_specs,
            out_specs=jax.tree.map(lambda _: VMEM, out_shape),
            scratch_shapes=scratch,
            grid=(1,),
            compiler_params=params,
            **options,
        )(*operands)

    def one_level(parity):
        return pl.BlockSpec((1, phases, cols), lambda step: (parity, 0, 0))

    def exchanged(part, distance):
        return lax.ppermute(part, "col", [(i, i ^ distance) for i in range(shards)])

    def stack(*pieces):
        ranges_of = [(first, rows) for _, first, rows in pieces]
        kernel = functools.partial(stack_kernel, ranges_of)
        return call(kernel, shape(sum(rows for _, rows in ranges_of)), [VMEM] * len(pieces), *[p[0] for p in pieces])

    odd, even = one_level(1), one_level(0)
    in_hbm = [pltpu.with_memory_space_constraint(x, pltpu.HBM) for x in (up_blocks, level_blocks, down_blocks)]
    sent, peak = call(
        prepare_kernel,
        (shape(3 * phases), shape(PEAK_ROWS)),
        [SMEM] + [ANY] * 3,
        owners,
        *in_hbm,
        scratch=[pltpu.VMEM((levels, cols, cols), F32), pltpu.SemaphoreType.DMA((4,))],
    )
    level_far = exchanged(sent[:phases], 3)
    near = exchanged(sent, 1)
    reach = 1
    while reach < ranges:
        route = [(i, (i + reach) % ranges) for i in range(ranges)]
        peak = jnp.maximum(peak, lax.ppermute(peak, "lvl", route))
        reach *= 2
    sent_now = lax.optimization_barrier((sent, level_far))[0]
    even_far = exchanged(stack((sent_now, phases, 2 * phases), (peak, 0, PEAK_ROWS)), 3)
    level_last = exchanged(stack((level_far, 0, phases), (peak, 0, PEAK_ROWS)), 1)
    even_last = exchanged(even_far, 1)

    solved = call(
        solve_kernel,
        shape(phases, 2 * cols),
        [SMEM, odd, *[VMEM] * 3, odd, odd],
        owners,
        level_blocks,
        near,
        level_far,
        level_last,
        up_blocks,
        down_blocks,
        scratch=[
            pltpu.VMEM((phases, cols), F32),
            pltpu.VMEM((phases, phases), BF16),
            pltpu.VMEM((phases, phases), BF16),
            pltpu.VMEM((phases, 2 * cols), BF16),
            pltpu.VMEM((phases, 2 * cols), BF16),
        ],
    )
    from_below = lax.ppermute(solved, "lvl", [(i, i + 1) for i in range(ranges - 1)])

    parts = call(
        partial_kernel,
        (shape(phases),) * 3 + (shape(PEAK_ROWS),),
        [SMEM, even, even, *[VMEM] * 6, even],
        owners,
        up_blocks,
        down_blocks,
        peak,
        level_last,
        near,
        even_far,
        solved,
        from_below,
        level_blocks,
        cost_estimate=pl.CostEstimate(flops=0, bytes_accessed=0, transcendentals=0),
    )
    return call(
        output_kernel,
        (jax.ShapeDtypeStruct((1, phases, cols), F32),) * 3,
        [SMEM] + [VMEM] * 7,
        owners,
        even_last,
        solved,
        from_below,
        *parts,
    )


def solution(mesh):
    placed = (P("lvl", None, "col"),) * 3
    return jax.shard_map(per_device, mesh=mesh, in_specs=placed, out_specs=placed, check_vma=False)
```

```python
import functools

import jax
import jax.numpy as jnp
from jax import lax
from jax.experimental import pallas as pl
from jax.experimental.pallas import tpu as pltpu
from jax.sharding import PartitionSpec as P

SWEEPS = 2
PEAK_ROWS = 8
DISTANCES = (0, 1, 3, 2)
F32 = jnp.float32
BF16 = jnp.bfloat16
VMEM = pl.BlockSpec(memory_space=pltpu.VMEM)
ANY = pl.BlockSpec(memory_space=pl.ANY)
SMEM = pl.BlockSpec(memory_space=pltpu.SMEM)


def split(x):
    high = x.astype(BF16)
    return high, (x - high.astype(F32)).astype(BF16)


def exact_dot(left, right):
    (left_high, left_low), (right_high, right_low) = left, right
    dot = lambda a, b: jnp.dot(a, b, preferred_element_type=F32)
    return dot(left_high, right_high) + (dot(left_high, right_low) + dot(left_low, right_high))


def on_diagonal(rows, cols):
    row = lax.broadcasted_iota(jnp.int32, (rows, cols), 0)
    return row == lax.broadcasted_iota(jnp.int32, (rows, cols), 1)


def prepare_kernel(place, up_ref, level_ref, down_ref, odd_ref, even_ref, square, sems):
    _, phases, cols = level_ref.shape
    own = rows_of(place, 0, cols)
    sources = [level_ref.at[:, own, :], level_ref.at[1], up_ref.at[0], down_ref.at[0]]
    top, middle = pl.ds(0, phases), pl.ds(phases, phases)
    targets = [square, odd_ref.at[top, :], even_ref.at[top, :], even_ref.at[middle, :]]
    copies = [
        pltpu.make_async_copy(source, target, sems.at[at])
        for at, (source, target) in enumerate(zip(sources, targets))
    ]
    for copy in copies:
        copy.start()
    copies[0].wait()
    lowest = jnp.min(jnp.where(on_diagonal(cols, cols)[None], square[...], 0.0))
    odd_ref[pl.ds(phases, PEAK_ROWS), :] = jnp.full((PEAK_ROWS, cols), -lowest, F32)
    for copy in copies[1:]:
        copy.wait()


def rows_of(place, slot, cols):
    return pl.ds(pl.multiple_of((place[0] ^ DISTANCES[slot]) * cols, cols), cols)


def solve_kernel(place, own_ref, *refs):
    *blocks, up_ref, down_ref, solved_ref, peak_ref, inverse, high, low, s_high, s_low = refs
    phases, cols = inverse.shape
    blocks = [own_ref, *blocks]
    peak = own_ref[pl.ds(phases, PEAK_ROWS), :]
    for block in blocks[1:]:
        peak = jnp.maximum(peak, block[pl.ds(phases, PEAK_ROWS), :])
    peak_ref[...] = peak
    diagonal = on_diagonal(cols, cols)
    for slot, block in enumerate(blocks):
        rows, slot_cols = rows_of(place, slot, cols), pl.ds(slot * cols, cols)
        high[:, slot_cols], low[:, slot_cols] = split(block[pl.ds(0, phases), :])
        square = block[rows, :]
        rate = -jnp.sum(jnp.where(diagonal, square, 0.0), axis=1, keepdims=True)
        inverse[rows, :] = jnp.broadcast_to(1.0 / rate, (cols, cols))
        high[rows, slot_cols], low[rows, slot_cols] = split(jnp.where(diagonal, 0.0, square))
    for side, ref in enumerate((up_ref, down_ref)):
        solved_ref[:, pl.ds(side * cols, cols)] = ref[0] * inverse[...]
    for _ in range(SWEEPS):
        for slot in range(len(blocks)):
            rows, slot_rows = rows_of(place, slot, cols), pl.ds(slot * cols, cols)
            s_high[slot_rows, :], s_low[slot_rows, :] = split(solved_ref[rows, :])
        product = exact_dot((high[...], low[...]), (s_high[...], s_low[...]))
        for side, ref in enumerate((up_ref, down_ref)):
            columns = slice(side * cols, (side + 1) * cols)
            solved_ref[:, columns] = (ref[0] + product[:, columns]) * inverse[...]


def gathered_product(place, blocks, first_slot, solved_ref):
    cols = blocks[0].shape[-1]
    left = split(jnp.concatenate(blocks, axis=1))
    rows = [rows_of(place, first_slot + at, cols) for at in range(len(blocks))]
    right = split(jnp.concatenate([solved_ref[r, :] for r in rows], axis=0))
    return exact_dot(left, right)


def partial_kernel(place, own_ref, near_ref, far_ref, solved_ref, below_ref, level_ref, part_level, part_up, part_down):
    phases, cols = part_up.shape
    top, middle = pl.ds(0, phases), pl.ds(phases, phases)
    blocks = (own_ref, near_ref, far_ref)
    upper = gathered_product(place, [ref[top, :] for ref in blocks], 0, solved_ref)
    part_up[...] = upper[:, :cols]
    lower = gathered_product(place, [ref[middle, :] for ref in blocks], 0, below_ref)
    part_down[...] = lower[:, cols:]
    part_level[...] = level_ref[0] + upper[:, cols:] + lower[:, :cols]


def output_kernel(place, last_ref, solved_ref, below_ref, *refs):
    part_level, part_up, part_down, peak_ref, new_level, new_up, new_down = refs
    phases, cols = part_up.shape
    scale = 1.0 / peak_ref[0:1, :]
    last = len(DISTANCES) - 1
    upper = gathered_product(place, [last_ref[pl.ds(0, phases), :]], last, solved_ref)
    new_up[0] = (part_up[...] + upper[:, :cols]) * scale
    lower = gathered_product(place, [last_ref[pl.ds(phases, phases), :]], last, below_ref)
    new_down[0] = (part_down[...] + lower[:, cols:]) * scale
    new_level[0] = (part_level[...] + upper[:, cols:] + lower[:, :cols]) * scale


def per_device(up_blocks, level_blocks, down_blocks):
    levels, phases, cols = level_blocks.shape
    shards = lax.axis_size("col")
    ranges = lax.axis_size("lvl")
    assert levels == 2 and shards == len(DISTANCES)
    place = lax.axis_index("col").astype(jnp.int32).reshape(1)
    params = pltpu.CompilerParams(vmem_limit_bytes=32 * 2**20)
    shape = lambda rows, columns=cols: jax.ShapeDtypeStruct((rows, columns), F32)

    def call(kernel, out_shape, in_specs, *operands, scratch=(), **options):
        return pl.pallas_call(
            kernel,
            out_shape=out_shape,
            in_specs=in_specs,
            out_specs=jax.tree.map(lambda _: VMEM, out_shape),
            scratch_shapes=scratch,
            grid=(1,),
            compiler_params=params,
            **options,
        )(*operands)

    def one_level(parity):
        return pl.BlockSpec((1, phases, cols), lambda step: (parity, 0, 0))

    def exchanged(part, distance):
        return lax.ppermute(part, "col", [(i, i ^ distance) for i in range(shards)])

    def after(value, *earlier):
        return lax.optimization_barrier((value, *earlier))[0]

    odd, even = one_level(1), one_level(0)
    in_hbm = [pltpu.with_memory_space_constraint(x, pltpu.HBM) for x in (up_blocks, level_blocks, down_blocks)]
    odd_block, even_blocks = call(
        prepare_kernel,
        (shape(phases + PEAK_ROWS), shape(2 * phases)),
        [SMEM] + [ANY] * 3,
        place,
        *in_hbm,
        scratch=[pltpu.VMEM((levels, cols, cols), F32), pltpu.SemaphoreType.DMA((4,))],
    )
    level_far, level_near = exchanged(odd_block, 3), exchanged(odd_block, 1)
    even_far, even_near = exchanged(even_blocks, 3), exchanged(even_blocks, 1)
    level_last, even_last = exchanged(level_far, 1), exchanged(even_far, 1)

    solved, peak = call(
        solve_kernel,
        (shape(phases, 2 * cols), shape(PEAK_ROWS)),
        [SMEM, *[VMEM] * 4, odd, odd],
        place,
        odd_block,
        level_near,
        level_far,
        level_last,
        up_blocks,
        down_blocks,
        scratch=[
            pltpu.VMEM((phases, cols), F32),
            pltpu.VMEM((phases, phases), BF16),
            pltpu.VMEM((phases, phases), BF16),
            pltpu.VMEM((phases, 2 * cols), BF16),
            pltpu.VMEM((phases, 2 * cols), BF16),
        ],
    )
    from_below = lax.ppermute(solved, "lvl", [(i, i + 1) for i in range(ranges - 1)])

    peak, reach = after(peak, even_far), 1
    while reach < ranges:
        route = [(i, (i + reach) % ranges) for i in range(ranges)]
        peak = jnp.maximum(peak, lax.ppermute(peak, "lvl", route))
        reach *= 2

    parts = call(
        partial_kernel,
        (shape(phases),) * 3,
        [SMEM, *[VMEM] * 5, even],
        place,
        even_blocks,
        even_near,
        even_far,
        solved,
        from_below,
        level_blocks,
        cost_estimate=pl.CostEstimate(flops=0, bytes_accessed=0, transcendentals=0),
    )
    return call(
        output_kernel,
        (jax.ShapeDtypeStruct((1, phases, cols), F32),) * 3,
        [SMEM] + [VMEM] * 7,
        place,
        even_last,
        solved,
        from_below,
        *parts,
        peak,
    )


def solution(mesh):
    placed = (P("lvl", None, "col"),) * 3
    return jax.shard_map(per_device, mesh=mesh, in_specs=placed, out_specs=placed, check_vma=False)
```

```python
import functools

import jax
import jax.numpy as jnp
from jax import lax
from jax.experimental import pallas as pl
from jax.experimental.pallas import tpu as pltpu
from jax.sharding import PartitionSpec as P

SWEEPS = 2
PEAK_ROWS = 8
DISTANCES = (0, 1, 3, 2)
F32 = jnp.float32
BF16 = jnp.bfloat16
VMEM = pl.BlockSpec(memory_space=pltpu.VMEM)
ANY = pl.BlockSpec(memory_space=pl.ANY)
SMEM = pl.BlockSpec(memory_space=pltpu.SMEM)


def split(x):
    high = x.astype(BF16)
    return high, (x - high.astype(F32)).astype(BF16)


def exact_dot(left, right):
    (left_high, left_low), (right_high, right_low) = left, right
    dot = lambda a, b: jnp.dot(a, b, preferred_element_type=F32)
    return dot(left_high, right_high) + (dot(left_high, right_low) + dot(left_low, right_high))


def on_diagonal(rows, cols):
    row = lax.broadcasted_iota(jnp.int32, (rows, cols), 0)
    return row == lax.broadcasted_iota(jnp.int32, (rows, cols), 1)


def prepare_kernel(place, up_ref, level_ref, down_ref, sent_ref, square, sems):
    _, phases, cols = level_ref.shape
    own = rows_of(place, 0, cols)
    sources = [level_ref.at[:, own, :], level_ref.at[1], up_ref.at[0], down_ref.at[0]]
    starts = (0, phases + PEAK_ROWS, 2 * phases + PEAK_ROWS)
    targets = [square, *[sent_ref.at[pl.ds(start, phases), :] for start in starts]]
    copies = [
        pltpu.make_async_copy(source, target, sems.at[at])
        for at, (source, target) in enumerate(zip(sources, targets))
    ]
    for copy in copies:
        copy.start()
    copies[0].wait()
    lowest = jnp.min(jnp.where(on_diagonal(cols, cols)[None], square[...], 0.0))
    sent_ref[pl.ds(phases, PEAK_ROWS), :] = jnp.full((PEAK_ROWS, cols), -lowest, F32)
    for copy in copies[1:]:
        copy.wait()


def stack_kernel(ranges, *refs):
    *parts, out_ref = refs
    at = 0
    for (first, rows), ref in zip(ranges, parts):
        out_ref[pl.ds(at, rows), :] = ref[pl.ds(first, rows), :]
        at += rows


def rows_of(place, slot, cols):
    return pl.ds(pl.multiple_of((place[0] ^ DISTANCES[slot]) * cols, cols), cols)


def solve_kernel(place, own_ref, *refs):
    *blocks, up_ref, down_ref, solved_ref, inverse, high, low, s_high, s_low = refs
    phases, cols = inverse.shape
    blocks = [own_ref, *blocks]
    diagonal = on_diagonal(cols, cols)
    for slot, block in enumerate(blocks):
        rows, slot_cols = rows_of(place, slot, cols), pl.ds(slot * cols, cols)
        high[:, slot_cols], low[:, slot_cols] = split(block[pl.ds(0, phases), :])
        square = block[rows, :]
        rate = -jnp.sum(jnp.where(diagonal, square, 0.0), axis=1, keepdims=True)
        inverse[rows, :] = jnp.broadcast_to(1.0 / rate, (cols, cols))
        high[rows, slot_cols], low[rows, slot_cols] = split(jnp.where(diagonal, 0.0, square))
    for side, ref in enumerate((up_ref, down_ref)):
        solved_ref[:, pl.ds(side * cols, cols)] = ref[0] * inverse[...]
    for _ in range(SWEEPS):
        for slot in range(len(blocks)):
            rows, slot_rows = rows_of(place, slot, cols), pl.ds(slot * cols, cols)
            s_high[slot_rows, :], s_low[slot_rows, :] = split(solved_ref[rows, :])
        product = exact_dot((high[...], low[...]), (s_high[...], s_low[...]))
        for side, ref in enumerate((up_ref, down_ref)):
            columns = slice(side * cols, (side + 1) * cols)
            solved_ref[:, columns] = (ref[0] + product[:, columns]) * inverse[...]


def gathered_product(place, blocks, first_slot, solved_ref):
    cols = blocks[0].shape[-1]
    left = split(jnp.concatenate(blocks, axis=1))
    rows = [rows_of(place, first_slot + at, cols) for at in range(len(blocks))]
    right = split(jnp.concatenate([solved_ref[r, :] for r in rows], axis=0))
    return exact_dot(left, right)


def partial_kernel(place, own_ref, near_ref, level_last_ref, far_ref, solved_ref, below_ref, level_ref, part_level, part_up, part_down):
    phases, cols = part_up.shape
    top, middle = pl.ds(0, phases), pl.ds(phases, phases)
    own_up, own_down = (pl.ds(start + PEAK_ROWS, phases) for start in (phases, 2 * phases))
    upper = gathered_product(place, [own_ref[own_up, :], near_ref[own_up, :], far_ref[top, :]], 0, solved_ref)
    part_up[...] = upper[:, :cols]
    lower = gathered_product(place, [own_ref[own_down, :], level_last_ref[middle, :], far_ref[middle, :]], 0, below_ref)
    part_down[...] = lower[:, cols:]
    part_level[...] = level_ref[0] + upper[:, cols:] + lower[:, :cols]


def output_kernel(place, last_ref, solved_ref, below_ref, *refs):
    part_level, part_up, part_down, peak_ref, new_level, new_up, new_down = refs
    phases, cols = part_up.shape
    scale = 1.0 / peak_ref[0:1, :]
    last = len(DISTANCES) - 1
    upper = gathered_product(place, [last_ref[pl.ds(0, phases), :]], last, solved_ref)
    new_up[0] = (part_up[...] + upper[:, :cols]) * scale
    lower = gathered_product(place, [last_ref[pl.ds(phases, phases), :]], last, below_ref)
    new_down[0] = (part_down[...] + lower[:, cols:]) * scale
    new_level[0] = (part_level[...] + upper[:, cols:] + lower[:, :cols]) * scale


def per_device(up_blocks, level_blocks, down_blocks):
    levels, phases, cols = level_blocks.shape
    shards = lax.axis_size("col")
    ranges = lax.axis_size("lvl")
    assert levels == 2 and shards == len(DISTANCES)
    place = lax.axis_index("col").astype(jnp.int32).reshape(1)
    params = pltpu.CompilerParams(vmem_limit_bytes=32 * 2**20)
    shape = lambda rows, columns=cols: jax.ShapeDtypeStruct((rows, columns), F32)

    def call(kernel, out_shape, in_specs, *operands, scratch=(), **options):
        return pl.pallas_call(
            kernel,
            out_shape=out_shape,
            in_specs=in_specs,
            out_specs=jax.tree.map(lambda _: VMEM, out_shape),
            scratch_shapes=scratch,
            grid=(1,),
            compiler_params=params,
            **options,
        )(*operands)

    def one_level(parity):
        return pl.BlockSpec((1, phases, cols), lambda step: (parity, 0, 0))

    def exchanged(part, distance):
        return lax.ppermute(part, "col", [(i, i ^ distance) for i in range(shards)])

    def after(value, *earlier):
        return lax.optimization_barrier((value, *earlier))[0]

    def stack(*pieces):
        ranges_of = [(first, rows) for _, first, rows in pieces]
        kernel = functools.partial(stack_kernel, ranges_of)
        return call(kernel, shape(sum(rows for _, rows in ranges_of)), [VMEM] * len(pieces), *[p[0] for p in pieces])

    odd, even = one_level(1), one_level(0)
    in_hbm = [pltpu.with_memory_space_constraint(x, pltpu.HBM) for x in (up_blocks, level_blocks, down_blocks)]
    sent = call(
        prepare_kernel,
        shape(3 * phases + PEAK_ROWS),
        [SMEM] + [ANY] * 3,
        place,
        *in_hbm,
        scratch=[pltpu.VMEM((levels, cols, cols), F32), pltpu.SemaphoreType.DMA((4,))],
    )
    up_row, down_row = phases + PEAK_ROWS, 2 * phases + PEAK_ROWS
    level_far, near = exchanged(sent[:up_row], 3), exchanged(sent[:down_row], 1)
    peak = exchanged(sent[phases:up_row], 2)
    sent_now = after(sent, level_far, peak)
    for part in (sent, level_far, near):
        peak = jnp.maximum(peak, part[phases:up_row])
    even_far = exchanged(sent_now[up_row:], 3)
    level_last = exchanged(stack((level_far, 0, phases), (sent, down_row, phases)), 1)
    even_last = exchanged(even_far, 1)
    reach = 1
    while reach < ranges:
        route = [(i, (i + reach) % ranges) for i in range(ranges)]
        peak = jnp.maximum(peak, lax.ppermute(peak, "lvl", route))
        reach *= 2

    solved = call(
        solve_kernel,
        shape(phases, 2 * cols),
        [SMEM, *[VMEM] * 4, odd, odd],
        after(place, peak),
        sent,
        near,
        level_far,
        level_last,
        up_blocks,
        down_blocks,
        scratch=[
            pltpu.VMEM((phases, cols), F32),
            pltpu.VMEM((phases, phases), BF16),
            pltpu.VMEM((phases, phases), BF16),
            pltpu.VMEM((phases, 2 * cols), BF16),
            pltpu.VMEM((phases, 2 * cols), BF16),
        ],
    )
    from_below = lax.ppermute(solved, "lvl", [(i, i + 1) for i in range(ranges - 1)])

    parts = call(
        partial_kernel,
        (shape(phases),) * 3,
        [SMEM, *[VMEM] * 6, even],
        place,
        sent,
        near,
        level_last,
        even_far,
        solved,
        from_below,
        level_blocks,
        cost_estimate=pl.CostEstimate(flops=0, bytes_accessed=0, transcendentals=0),
    )
    return call(
        output_kernel,
        (jax.ShapeDtypeStruct((1, phases, cols), F32),) * 3,
        [SMEM] + [VMEM] * 7,
        place,
        even_last,
        solved,
        from_below,
        *parts,
        peak,
    )


def solution(mesh):
    placed = (P("lvl", None, "col"),) * 3
    return jax.shard_map(per_device, mesh=mesh, in_specs=placed, out_specs=placed, check_vma=False)
```

```python
import functools

import jax
import jax.numpy as jnp
from jax import lax
from jax.experimental import pallas as pl
from jax.experimental.pallas import tpu as pltpu
from jax.sharding import PartitionSpec as P

SWEEPS = 2
PEAK_ROWS = 8
DISTANCES = (0, 1, 3, 2)
F32 = jnp.float32
BF16 = jnp.bfloat16
VMEM = pl.BlockSpec(memory_space=pltpu.VMEM)
ANY = pl.BlockSpec(memory_space=pl.ANY)
SMEM = pl.BlockSpec(memory_space=pltpu.SMEM)


def split(x):
    high = x.astype(BF16)
    return high, (x - high.astype(F32)).astype(BF16)


def exact_dot(left, right):
    (left_high, left_low), (right_high, right_low) = left, right
    dot = lambda a, b: jnp.dot(a, b, preferred_element_type=F32)
    return dot(left_high, right_high) + (dot(left_high, right_low) + dot(left_low, right_high))


def on_diagonal(rows, cols):
    row = lax.broadcasted_iota(jnp.int32, (rows, cols), 0)
    return row == lax.broadcasted_iota(jnp.int32, (rows, cols), 1)


def prepare_kernel(place, up_ref, level_ref, down_ref, sent_ref, square, sems):
    _, phases, cols = level_ref.shape
    own = rows_of(place, 0, cols)
    sources = [level_ref.at[:, own, :], level_ref.at[1], up_ref.at[0], down_ref.at[0]]
    starts = (0, phases + PEAK_ROWS, 2 * phases + PEAK_ROWS)
    targets = [square, *[sent_ref.at[pl.ds(start, phases), :] for start in starts]]
    copies = [
        pltpu.make_async_copy(source, target, sems.at[at])
        for at, (source, target) in enumerate(zip(sources, targets))
    ]
    for copy in copies:
        copy.start()
    copies[0].wait()
    lowest = jnp.min(jnp.where(on_diagonal(cols, cols)[None], square[...], 0.0))
    sent_ref[pl.ds(phases, PEAK_ROWS), :] = jnp.full((PEAK_ROWS, cols), -lowest, F32)
    for copy in copies[1:]:
        copy.wait()


def stack_kernel(ranges, *refs):
    *parts, out_ref = refs
    at = 0
    for (first, rows), ref in zip(ranges, parts):
        out_ref[pl.ds(at, rows), :] = ref[pl.ds(first, rows), :]
        at += rows


def rows_of(place, slot, cols):
    return pl.ds(pl.multiple_of((place[0] ^ DISTANCES[slot]) * cols, cols), cols)


def solve_kernel(place, own_ref, *refs):
    *blocks, up_ref, down_ref, solved_ref, inverse, high, low, s_high, s_low = refs
    phases, cols = inverse.shape
    blocks = [own_ref, *blocks]
    diagonal = on_diagonal(cols, cols)
    for slot, block in enumerate(blocks):
        rows, slot_cols = rows_of(place, slot, cols), pl.ds(slot * cols, cols)
        high[:, slot_cols], low[:, slot_cols] = split(block[pl.ds(0, phases), :])
        square = block[rows, :]
        rate = -jnp.sum(jnp.where(diagonal, square, 0.0), axis=1, keepdims=True)
        inverse[rows, :] = jnp.broadcast_to(1.0 / rate, (cols, cols))
        high[rows, slot_cols], low[rows, slot_cols] = split(jnp.where(diagonal, 0.0, square))
    for side, ref in enumerate((up_ref, down_ref)):
        solved_ref[:, pl.ds(side * cols, cols)] = ref[0] * inverse[...]
    for _ in range(SWEEPS):
        for slot in range(len(blocks)):
            rows, slot_rows = rows_of(place, slot, cols), pl.ds(slot * cols, cols)
            s_high[slot_rows, :], s_low[slot_rows, :] = split(solved_ref[rows, :])
        product = exact_dot((high[...], low[...]), (s_high[...], s_low[...]))
        for side, ref in enumerate((up_ref, down_ref)):
            columns = slice(side * cols, (side + 1) * cols)
            solved_ref[:, columns] = (ref[0] + product[:, columns]) * inverse[...]


def gathered_product(place, blocks, first_slot, solved_ref):
    cols = blocks[0].shape[-1]
    left = split(jnp.concatenate(blocks, axis=1))
    rows = [rows_of(place, first_slot + at, cols) for at in range(len(blocks))]
    right = split(jnp.concatenate([solved_ref[r, :] for r in rows], axis=0))
    return exact_dot(left, right)


def partial_kernel(place, own_ref, near_ref, level_last_ref, far_ref, solved_ref, below_ref, level_ref, part_level, part_up, part_down):
    phases, cols = part_up.shape
    top, middle = pl.ds(0, phases), pl.ds(phases, phases)
    own_up, own_down = (pl.ds(start + PEAK_ROWS, phases) for start in (phases, 2 * phases))
    upper = gathered_product(place, [own_ref[own_up, :], near_ref[own_up, :], far_ref[top, :]], 0, solved_ref)
    part_up[...] = upper[:, :cols]
    lower = gathered_product(place, [own_ref[own_down, :], level_last_ref[middle, :], far_ref[middle, :]], 0, below_ref)
    part_down[...] = lower[:, cols:]
    part_level[...] = level_ref[0] + upper[:, cols:] + lower[:, :cols]


def output_kernel(place, last_ref, solved_ref, below_ref, *refs):
    part_level, part_up, part_down, peak_ref, new_level, new_up, new_down = refs
    phases, cols = part_up.shape
    scale = 1.0 / jnp.maximum(peak_ref[...], last_ref[pl.ds(2 * phases, PEAK_ROWS), :])[0:1, :]
    last = len(DISTANCES) - 1
    upper = gathered_product(place, [last_ref[pl.ds(0, phases), :]], last, solved_ref)
    new_up[0] = (part_up[...] + upper[:, :cols]) * scale
    lower = gathered_product(place, [last_ref[pl.ds(phases, phases), :]], last, below_ref)
    new_down[0] = (part_down[...] + lower[:, cols:]) * scale
    new_level[0] = (part_level[...] + upper[:, cols:] + lower[:, :cols]) * scale


def per_device(up_blocks, level_blocks, down_blocks):
    levels, phases, cols = level_blocks.shape
    shards = lax.axis_size("col")
    ranges = lax.axis_size("lvl")
    assert levels == 2 and shards == len(DISTANCES)
    place = lax.axis_index("col").astype(jnp.int32).reshape(1)
    params = pltpu.CompilerParams(vmem_limit_bytes=32 * 2**20)
    shape = lambda rows, columns=cols: jax.ShapeDtypeStruct((rows, columns), F32)

    def call(kernel, out_shape, in_specs, *operands, scratch=(), **options):
        return pl.pallas_call(
            kernel,
            out_shape=out_shape,
            in_specs=in_specs,
            out_specs=jax.tree.map(lambda _: VMEM, out_shape),
            scratch_shapes=scratch,
            grid=(1,),
            compiler_params=params,
            **options,
        )(*operands)

    def one_level(parity):
        return pl.BlockSpec((1, phases, cols), lambda step: (parity, 0, 0))

    def exchanged(part, distance):
        return lax.ppermute(part, "col", [(i, i ^ distance) for i in range(shards)])

    def after(value, *earlier):
        return lax.optimization_barrier((value, *earlier))[0]

    def stack(*pieces):
        ranges_of = [(first, rows) for _, first, rows in pieces]
        kernel = functools.partial(stack_kernel, ranges_of)
        return call(kernel, shape(sum(rows for _, rows in ranges_of)), [VMEM] * len(pieces), *[p[0] for p in pieces])

    odd, even = one_level(1), one_level(0)
    in_hbm = [pltpu.with_memory_space_constraint(x, pltpu.HBM) for x in (up_blocks, level_blocks, down_blocks)]
    sent = call(
        prepare_kernel,
        shape(3 * phases + PEAK_ROWS),
        [SMEM] + [ANY] * 3,
        place,
        *in_hbm,
        scratch=[pltpu.VMEM((levels, cols, cols), F32), pltpu.SemaphoreType.DMA((4,))],
    )
    up_row, down_row = phases + PEAK_ROWS, 2 * phases + PEAK_ROWS
    level_far, near = exchanged(sent[:up_row], 3), exchanged(sent[:down_row], 1)
    even_far = exchanged(after(sent, level_far)[up_row:], 3)
    level_last = exchanged(stack((level_far, 0, phases), (sent, down_row, phases)), 1)
    peak = jnp.maximum(sent[phases:up_row], level_far[phases:])
    reach = 1
    while reach < ranges:
        route = [(i, (i + reach) % ranges) for i in range(ranges)]
        peak = jnp.maximum(peak, lax.ppermute(peak, "lvl", route))
        reach *= 2
    even_last = exchanged(stack((even_far, 0, 2 * phases), (peak, 0, PEAK_ROWS)), 1)

    solved = call(
        solve_kernel,
        shape(phases, 2 * cols),
        [SMEM, *[VMEM] * 4, odd, odd],
        after(place, peak),
        sent,
        near,
        level_far,
        level_last,
        up_blocks,
        down_blocks,
        scratch=[
            pltpu.VMEM((phases, cols), F32),
            pltpu.VMEM((phases, phases), BF16),
            pltpu.VMEM((phases, phases), BF16),
            pltpu.VMEM((phases, 2 * cols), BF16),
            pltpu.VMEM((phases, 2 * cols), BF16),
        ],
    )
    from_below = lax.ppermute(solved, "lvl", [(i, i + 1) for i in range(ranges - 1)])

    parts = call(
        partial_kernel,
        (shape(phases),) * 3,
        [SMEM, *[VMEM] * 6, even],
        place,
        sent,
        near,
        level_last,
        even_far,
        solved,
        from_below,
        level_blocks,
        cost_estimate=pl.CostEstimate(flops=0, bytes_accessed=0, transcendentals=0),
    )
    return call(
        output_kernel,
        (jax.ShapeDtypeStruct((1, phases, cols), F32),) * 3,
        [SMEM] + [VMEM] * 7,
        place,
        even_last,
        solved,
        from_below,
        *parts,
        peak,
    )


def solution(mesh):
    placed = (P("lvl", None, "col"),) * 3
    return jax.shard_map(per_device, mesh=mesh, in_specs=placed, out_specs=placed, check_vma=False)
```

```python
import functools

import jax
import jax.numpy as jnp
from jax import lax
from jax.experimental import pallas as pl
from jax.experimental.pallas import tpu as pltpu
from jax.sharding import PartitionSpec as P

SWEEPS = 2
PEAK_ROWS = 8
PAD_ROWS = 24
DISTANCES = (0, 1, 3, 2)
F32 = jnp.float32
BF16 = jnp.bfloat16
VMEM = pl.BlockSpec(memory_space=pltpu.VMEM)
ANY = pl.BlockSpec(memory_space=pl.ANY)
SMEM = pl.BlockSpec(memory_space=pltpu.SMEM)


def split(x):
    high = x.astype(BF16)
    return high, (x - high.astype(F32)).astype(BF16)


def exact_dot(left, right):
    (left_high, left_low), (right_high, right_low) = left, right
    dot = lambda a, b: jnp.dot(a, b, preferred_element_type=F32)
    return dot(left_high, right_high) + (dot(left_high, right_low) + dot(left_low, right_high))


def on_diagonal(rows, cols):
    row = lax.broadcasted_iota(jnp.int32, (rows, cols), 0)
    return row == lax.broadcasted_iota(jnp.int32, (rows, cols), 1)


def prepare_kernel(place, up_ref, level_ref, down_ref, sent_ref, square, sems):
    _, phases, cols = level_ref.shape
    own = rows_of(place, 0, cols)
    sources = [level_ref.at[:, own, :], level_ref.at[1], up_ref.at[0], down_ref.at[0]]
    starts = (0, phases + PEAK_ROWS, 2 * phases + PEAK_ROWS)
    targets = [square, *[sent_ref.at[pl.ds(start, phases), :] for start in starts]]
    copies = [
        pltpu.make_async_copy(source, target, sems.at[at])
        for at, (source, target) in enumerate(zip(sources, targets))
    ]
    for copy in copies:
        copy.start()
    copies[0].wait()
    lowest = jnp.min(jnp.where(on_diagonal(cols, cols)[None], square[...], 0.0))
    sent_ref[pl.ds(phases, PEAK_ROWS), :] = jnp.full((PEAK_ROWS, cols), -lowest, F32)
    for copy in copies[1:]:
        copy.wait()


def stack_kernel(ranges, *refs):
    *parts, out_ref = refs
    at = 0
    for (first, rows), ref in zip(ranges, parts):
        out_ref[pl.ds(at, rows), :] = ref[pl.ds(first, rows), :]
        at += rows


def rows_of(place, slot, cols):
    return pl.ds(pl.multiple_of((place[0] ^ DISTANCES[slot]) * cols, cols), cols)


def solve_kernel(place, own_ref, *refs):
    *blocks, up_ref, down_ref, solved_ref, inverse, high, low, s_high, s_low = refs
    phases, cols = inverse.shape
    blocks = [own_ref, *blocks]
    diagonal = on_diagonal(cols, cols)
    for slot, block in enumerate(blocks):
        rows, slot_cols = rows_of(place, slot, cols), pl.ds(slot * cols, cols)
        high[:, slot_cols], low[:, slot_cols] = split(block[pl.ds(0, phases), :])
        square = block[rows, :]
        rate = -jnp.sum(jnp.where(diagonal, square, 0.0), axis=1, keepdims=True)
        inverse[rows, :] = jnp.broadcast_to(1.0 / rate, (cols, cols))
        high[rows, slot_cols], low[rows, slot_cols] = split(jnp.where(diagonal, 0.0, square))
    for side, ref in enumerate((up_ref, down_ref)):
        solved_ref[:, pl.ds(side * cols, cols)] = ref[0] * inverse[...]
    for _ in range(SWEEPS):
        for slot in range(len(blocks)):
            rows, slot_rows = rows_of(place, slot, cols), pl.ds(slot * cols, cols)
            s_high[slot_rows, :], s_low[slot_rows, :] = split(solved_ref[rows, :])
        product = exact_dot((high[...], low[...]), (s_high[...], s_low[...]))
        for side, ref in enumerate((up_ref, down_ref)):
            columns = slice(side * cols, (side + 1) * cols)
            solved_ref[:, columns] = (ref[0] + product[:, columns]) * inverse[...]


def gathered_product(place, blocks, first_slot, solved_ref):
    cols = blocks[0].shape[-1]
    left = split(jnp.concatenate(blocks, axis=1))
    rows = [rows_of(place, first_slot + at, cols) for at in range(len(blocks))]
    right = split(jnp.concatenate([solved_ref[r, :] for r in rows], axis=0))
    return exact_dot(left, right)


def partial_kernel(place, own_ref, near_ref, down_near_ref, far_ref, solved_ref, below_ref, level_ref, part_level, part_up, part_down):
    phases, cols = part_up.shape
    top, middle = pl.ds(0, phases), pl.ds(phases, phases)
    own_up, own_down = (pl.ds(start + PEAK_ROWS, phases) for start in (phases, 2 * phases))
    upper = gathered_product(place, [own_ref[own_up, :], near_ref[own_up, :], far_ref[top, :]], 0, solved_ref)
    part_up[...] = upper[:, :cols]
    lower = gathered_product(place, [own_ref[own_down, :], down_near_ref[...], far_ref[middle, :]], 0, below_ref)
    part_down[...] = lower[:, cols:]
    part_level[...] = level_ref[0] + upper[:, cols:] + lower[:, :cols]


def output_kernel(place, last_ref, solved_ref, below_ref, *refs):
    part_level, part_up, part_down, peak_ref, new_level, new_up, new_down = refs
    phases, cols = part_up.shape
    scale = 1.0 / jnp.maximum(peak_ref[...], last_ref[pl.ds(2 * phases, PEAK_ROWS), :])[0:1, :]
    last = len(DISTANCES) - 1
    upper = gathered_product(place, [last_ref[pl.ds(0, phases), :]], last, solved_ref)
    new_up[0] = (part_up[...] + upper[:, :cols]) * scale
    lower = gathered_product(place, [last_ref[pl.ds(phases, phases), :]], last, below_ref)
    new_down[0] = (part_down[...] + lower[:, cols:]) * scale
    new_level[0] = (part_level[...] + upper[:, cols:] + lower[:, :cols]) * scale


def per_device(up_blocks, level_blocks, down_blocks):
    levels, phases, cols = level_blocks.shape
    shards = lax.axis_size("col")
    ranges = lax.axis_size("lvl")
    assert levels == 2 and shards == len(DISTANCES)
    place = lax.axis_index("col").astype(jnp.int32).reshape(1)
    params = pltpu.CompilerParams(vmem_limit_bytes=32 * 2**20)
    shape = lambda rows, columns=cols: jax.ShapeDtypeStruct((rows, columns), F32)

    def call(kernel, out_shape, in_specs, *operands, scratch=(), **options):
        return pl.pallas_call(
            kernel,
            out_shape=out_shape,
            in_specs=in_specs,
            out_specs=jax.tree.map(lambda _: VMEM, out_shape),
            scratch_shapes=scratch,
            grid=(1,),
            compiler_params=params,
            **options,
        )(*operands)

    def one_level(parity):
        return pl.BlockSpec((1, phases, cols), lambda step: (parity, 0, 0))

    def exchanged(part, distance):
        return lax.ppermute(part, "col", [(i, i ^ distance) for i in range(shards)])

    def after(value, *earlier):
        return lax.optimization_barrier((value, *earlier))[0]

    def stack(*pieces):
        ranges_of = [(first, rows) for _, first, rows in pieces]
        kernel = functools.partial(stack_kernel, ranges_of)
        return call(kernel, shape(sum(rows for _, rows in ranges_of)), [VMEM] * len(pieces), *[p[0] for p in pieces])

    odd, even = one_level(1), one_level(0)
    in_hbm = [pltpu.with_memory_space_constraint(x, pltpu.HBM) for x in (up_blocks, level_blocks, down_blocks)]
    sent = call(
        prepare_kernel,
        shape(3 * phases + PEAK_ROWS),
        [SMEM] + [ANY] * 3,
        place,
        *in_hbm,
        scratch=[pltpu.VMEM((levels, cols, cols), F32), pltpu.SemaphoreType.DMA((4,))],
    )
    up_row, down_row = phases + PEAK_ROWS, 2 * phases + PEAK_ROWS
    level_far, near = exchanged(sent[: up_row + PAD_ROWS], 3), exchanged(sent[:down_row], 1)
    level_last = exchanged(level_far, 1)
    even_far = exchanged(after(sent, level_far)[up_row:], 3)
    peak = jnp.maximum(sent[phases:up_row], level_far[phases:up_row])
    peaks, reach = [peak], 1
    while reach < ranges:
        route = [(i, (i + reach) % ranges) for i in range(ranges)]
        peaks.append(jnp.maximum(peaks[-1], lax.ppermute(peaks[-1], "lvl", route)))
        reach *= 2
    peak = peaks[-1]
    down_near = exchanged(after(sent, peaks[1])[down_row:], 1)
    even_last = exchanged(stack((after(even_far, down_near), 0, 2 * phases), (peak, 0, PEAK_ROWS)), 1)

    solved = call(
        solve_kernel,
        shape(phases, 2 * cols),
        [SMEM, *[VMEM] * 4, odd, odd],
        after(place, peak),
        sent,
        near,
        level_far,
        level_last,
        up_blocks,
        down_blocks,
        scratch=[
            pltpu.VMEM((phases, cols), F32),
            pltpu.VMEM((phases, phases), BF16),
            pltpu.VMEM((phases, phases), BF16),
            pltpu.VMEM((phases, 2 * cols), BF16),
            pltpu.VMEM((phases, 2 * cols), BF16),
        ],
    )
    from_below = lax.ppermute(solved, "lvl", [(i, i + 1) for i in range(ranges - 1)])

    parts = call(
        partial_kernel,
        (shape(phases),) * 3,
        [SMEM, *[VMEM] * 6, even],
        place,
        sent,
        near,
        down_near,
        even_far,
        solved,
        from_below,
        level_blocks,
        cost_estimate=pl.CostEstimate(flops=0, bytes_accessed=0, transcendentals=0),
    )
    return call(
        output_kernel,
        (jax.ShapeDtypeStruct((1, phases, cols), F32),) * 3,
        [SMEM] + [VMEM] * 7,
        place,
        even_last,
        solved,
        from_below,
        *parts,
        peak,
    )


def solution(mesh):
    placed = (P("lvl", None, "col"),) * 3
    return jax.shard_map(per_device, mesh=mesh, in_specs=placed, out_specs=placed, check_vma=False)
```

```python
import functools

import jax
import jax.numpy as jnp
from jax import lax
from jax.experimental import pallas as pl
from jax.experimental.pallas import tpu as pltpu
from jax.sharding import PartitionSpec as P

SWEEPS = 2
PEAK_ROWS = 8
PAD_ROWS = 24
DISTANCES = (0, 1, 3, 2)
F32 = jnp.float32
BF16 = jnp.bfloat16
VMEM = pl.BlockSpec(memory_space=pltpu.VMEM)
ANY = pl.BlockSpec(memory_space=pl.ANY)
SMEM = pl.BlockSpec(memory_space=pltpu.SMEM)


def split(x):
    high = x.astype(BF16)
    return high, (x - high.astype(F32)).astype(BF16)


def exact_dot(left, right):
    (left_high, left_low), (right_high, right_low) = left, right
    dot = lambda a, b: jnp.dot(a, b, preferred_element_type=F32)
    return dot(left_high, right_high) + (dot(left_high, right_low) + dot(left_low, right_high))


def on_diagonal(rows, cols):
    row = lax.broadcasted_iota(jnp.int32, (rows, cols), 0)
    return row == lax.broadcasted_iota(jnp.int32, (rows, cols), 1)


def prepare_kernel(place, up_ref, level_ref, down_ref, sent_ref, square, sems):
    _, phases, cols = level_ref.shape
    own = rows_of(place, 0, cols)
    sources = [level_ref.at[:, own, :], level_ref.at[1], up_ref.at[0], down_ref.at[0]]
    starts = (0, phases + PEAK_ROWS, 2 * phases + PEAK_ROWS)
    targets = [square, *[sent_ref.at[pl.ds(start, phases), :] for start in starts]]
    copies = [
        pltpu.make_async_copy(source, target, sems.at[at])
        for at, (source, target) in enumerate(zip(sources, targets))
    ]
    for copy in copies:
        copy.start()
    copies[0].wait()
    lowest = jnp.min(jnp.where(on_diagonal(cols, cols)[None], square[...], 0.0))
    sent_ref[pl.ds(phases, PEAK_ROWS), :] = jnp.full((PEAK_ROWS, cols), -lowest, F32)
    for copy in copies[1:]:
        copy.wait()


def stack_kernel(ranges, *refs):
    *parts, out_ref = refs
    at = 0
    for (first, rows), ref in zip(ranges, parts):
        out_ref[pl.ds(at, rows), :] = ref[pl.ds(first, rows), :]
        at += rows


def rows_of(place, slot, cols):
    return pl.ds(pl.multiple_of((place[0] ^ DISTANCES[slot]) * cols, cols), cols)


def solve_kernel(place, own_ref, *refs):
    *blocks, up_ref, down_ref, solved_ref, inverse, high, low, s_high, s_low = refs
    phases, cols = inverse.shape
    blocks = [own_ref, *blocks]
    diagonal = on_diagonal(cols, cols)
    for slot, block in enumerate(blocks):
        rows, slot_cols = rows_of(place, slot, cols), pl.ds(slot * cols, cols)
        high[:, slot_cols], low[:, slot_cols] = split(block[pl.ds(0, phases), :])
        square = block[rows, :]
        rate = -jnp.sum(jnp.where(diagonal, square, 0.0), axis=1, keepdims=True)
        inverse[rows, :] = jnp.broadcast_to(1.0 / rate, (cols, cols))
        high[rows, slot_cols], low[rows, slot_cols] = split(jnp.where(diagonal, 0.0, square))
    for side, ref in enumerate((up_ref, down_ref)):
        solved_ref[:, pl.ds(side * cols, cols)] = ref[0] * inverse[...]
    for _ in range(SWEEPS):
        for slot in range(len(blocks)):
            rows, slot_rows = rows_of(place, slot, cols), pl.ds(slot * cols, cols)
            s_high[slot_rows, :], s_low[slot_rows, :] = split(solved_ref[rows, :])
        product = exact_dot((high[...], low[...]), (s_high[...], s_low[...]))
        for side, ref in enumerate((up_ref, down_ref)):
            columns = slice(side * cols, (side + 1) * cols)
            solved_ref[:, columns] = (ref[0] + product[:, columns]) * inverse[...]


def gathered_product(place, blocks, first_slot, solved_ref):
    cols = blocks[0].shape[-1]
    left = split(jnp.concatenate(blocks, axis=1))
    rows = [rows_of(place, first_slot + at, cols) for at in range(len(blocks))]
    right = split(jnp.concatenate([solved_ref[r, :] for r in rows], axis=0))
    return exact_dot(left, right)


def upper_kernel(place, own_ref, near_ref, far_ref, solved_ref, level_ref, part_level, part_up):
    phases, cols = part_up.shape
    up = pl.ds(phases + PEAK_ROWS, phases)
    blocks = [own_ref[up, :], near_ref[up, :], far_ref[pl.ds(0, phases), :]]
    upper = gathered_product(place, blocks, 0, solved_ref)
    part_up[...] = upper[:, :cols]
    part_level[...] = level_ref[0] + upper[:, cols:]


def lower_kernel(place, own_ref, near_ref, far_ref, below_ref, upper_level, part_level, part_down):
    phases, cols = part_down.shape
    blocks = [own_ref[pl.ds(2 * phases + PEAK_ROWS, phases), :], near_ref[...], far_ref[pl.ds(phases, phases), :]]
    lower = gathered_product(place, blocks, 0, below_ref)
    part_down[...] = lower[:, cols:]
    part_level[...] = upper_level[...] + lower[:, :cols]


def output_kernel(place, last_ref, solved_ref, below_ref, *refs):
    part_level, part_up, part_down, peak_ref, new_level, new_up, new_down = refs
    phases, cols = part_up.shape
    scale = 1.0 / jnp.maximum(peak_ref[...], last_ref[pl.ds(2 * phases, PEAK_ROWS), :])[0:1, :]
    last = len(DISTANCES) - 1
    upper = gathered_product(place, [last_ref[pl.ds(0, phases), :]], last, solved_ref)
    new_up[0] = (part_up[...] + upper[:, :cols]) * scale
    lower = gathered_product(place, [last_ref[pl.ds(phases, phases), :]], last, below_ref)
    new_down[0] = (part_down[...] + lower[:, cols:]) * scale
    new_level[0] = (part_level[...] + upper[:, cols:] + lower[:, :cols]) * scale


def per_device(up_blocks, level_blocks, down_blocks):
    levels, phases, cols = level_blocks.shape
    shards = lax.axis_size("col")
    ranges = lax.axis_size("lvl")
    assert levels == 2 and shards == len(DISTANCES)
    place = lax.axis_index("col").astype(jnp.int32).reshape(1)
    params = pltpu.CompilerParams(vmem_limit_bytes=32 * 2**20)
    shape = lambda rows, columns=cols: jax.ShapeDtypeStruct((rows, columns), F32)

    def call(kernel, out_shape, in_specs, *operands, scratch=(), **options):
        return pl.pallas_call(
            kernel,
            out_shape=out_shape,
            in_specs=in_specs,
            out_specs=jax.tree.map(lambda _: VMEM, out_shape),
            scratch_shapes=scratch,
            grid=(1,),
            compiler_params=params,
            **options,
        )(*operands)

    def one_level(parity):
        return pl.BlockSpec((1, phases, cols), lambda step: (parity, 0, 0))

    def exchanged(part, distance):
        return lax.ppermute(part, "col", [(i, i ^ distance) for i in range(shards)])

    def after(value, *earlier):
        return lax.optimization_barrier((value, *earlier))[0]

    def stack(*pieces):
        ranges_of = [(first, rows) for _, first, rows in pieces]
        kernel = functools.partial(stack_kernel, ranges_of)
        return call(kernel, shape(sum(rows for _, rows in ranges_of)), [VMEM] * len(pieces), *[p[0] for p in pieces])

    odd, even = one_level(1), one_level(0)
    in_hbm = [pltpu.with_memory_space_constraint(x, pltpu.HBM) for x in (up_blocks, level_blocks, down_blocks)]
    sent = call(
        prepare_kernel,
        shape(3 * phases + PEAK_ROWS),
        [SMEM] + [ANY] * 3,
        place,
        *in_hbm,
        scratch=[pltpu.VMEM((levels, cols, cols), F32), pltpu.SemaphoreType.DMA((4,))],
    )
    up_row, down_row = phases + PEAK_ROWS, 2 * phases + PEAK_ROWS
    level_far, near = exchanged(sent[: up_row + PAD_ROWS], 3), exchanged(sent[:down_row], 1)
    level_last = exchanged(level_far, 1)
    even_far = exchanged(after(sent, level_far)[up_row:], 3)
    peak = jnp.maximum(sent[phases:up_row], level_far[phases:up_row])
    peaks, reach = [peak], 1
    while reach < ranges:
        route = [(i, (i + reach) % ranges) for i in range(ranges)]
        peaks.append(jnp.maximum(peaks[-1], lax.ppermute(peaks[-1], "lvl", route)))
        reach *= 2
    peak = peaks[-1]
    down_near = exchanged(after(sent, level_far)[down_row:], 1)
    even_last = exchanged(stack((even_far, 0, 2 * phases), (peak, 0, PEAK_ROWS)), 1)

    solved = call(
        solve_kernel,
        shape(phases, 2 * cols),
        [SMEM, *[VMEM] * 4, odd, odd],
        after(place, peak),
        sent,
        near,
        level_far,
        level_last,
        up_blocks,
        down_blocks,
        scratch=[
            pltpu.VMEM((phases, cols), F32),
            pltpu.VMEM((phases, phases), BF16),
            pltpu.VMEM((phases, phases), BF16),
            pltpu.VMEM((phases, 2 * cols), BF16),
            pltpu.VMEM((phases, 2 * cols), BF16),
        ],
    )
    from_below = lax.ppermute(after(solved, down_near), "lvl", [(i, i + 1) for i in range(ranges - 1)])

    free = pl.CostEstimate(flops=0, bytes_accessed=0, transcendentals=0)
    upper_level, part_up = call(
        upper_kernel,
        (shape(phases),) * 2,
        [SMEM, *[VMEM] * 4, even],
        place,
        sent,
        near,
        even_far,
        solved,
        level_blocks,
        cost_estimate=free,
    )
    part_level, part_down = call(
        lower_kernel,
        (shape(phases),) * 2,
        [SMEM, *[VMEM] * 5],
        place,
        sent,
        down_near,
        even_far,
        from_below,
        upper_level,
        cost_estimate=free,
    )
    return call(
        output_kernel,
        (jax.ShapeDtypeStruct((1, phases, cols), F32),) * 3,
        [SMEM] + [VMEM] * 7,
        place,
        even_last,
        solved,
        from_below,
        part_level,
        part_up,
        part_down,
        peak,
    )


def solution(mesh):
    placed = (P("lvl", None, "col"),) * 3
    return jax.shard_map(per_device, mesh=mesh, in_specs=placed, out_specs=placed, check_vma=False)
```

```python
import functools

import jax
import jax.numpy as jnp
from jax import lax
from jax.experimental import pallas as pl
from jax.experimental.pallas import tpu as pltpu
from jax.sharding import PartitionSpec as P

SWEEPS = 2
PEAK_ROWS = 8
PAD_ROWS = 24
DISTANCES = (0, 1, 3, 2)
F32 = jnp.float32
BF16 = jnp.bfloat16
VMEM = pl.BlockSpec(memory_space=pltpu.VMEM)
ANY = pl.BlockSpec(memory_space=pl.ANY)
SMEM = pl.BlockSpec(memory_space=pltpu.SMEM)


def split(x):
    high = x.astype(BF16)
    return high, (x - high.astype(F32)).astype(BF16)


def exact_dot(left, right):
    (left_high, left_low), (right_high, right_low) = left, right
    dot = lambda a, b: jnp.dot(a, b, preferred_element_type=F32)
    return dot(left_high, right_high) + (dot(left_high, right_low) + dot(left_low, right_high))


def on_diagonal(rows, cols):
    row = lax.broadcasted_iota(jnp.int32, (rows, cols), 0)
    return row == lax.broadcasted_iota(jnp.int32, (rows, cols), 1)


def prepare_kernel(place, up_ref, level_ref, down_ref, sent_ref, square, sems):
    _, phases, cols = level_ref.shape
    own = rows_of(place, 0, cols)
    sources = [level_ref.at[:, own, :], level_ref.at[1], up_ref.at[0], down_ref.at[0]]
    starts = (0, phases + PEAK_ROWS, 2 * phases + PEAK_ROWS)
    targets = [square, *[sent_ref.at[pl.ds(start, phases), :] for start in starts]]
    copies = [
        pltpu.make_async_copy(source, target, sems.at[at])
        for at, (source, target) in enumerate(zip(sources, targets))
    ]
    for copy in copies:
        copy.start()
    copies[0].wait()
    lowest = jnp.min(jnp.where(on_diagonal(cols, cols)[None], square[...], 0.0))
    sent_ref[pl.ds(phases, PEAK_ROWS), :] = jnp.full((PEAK_ROWS, cols), -lowest, F32)
    for copy in copies[1:]:
        copy.wait()


def stack_kernel(ranges, *refs):
    *parts, out_ref = refs
    at = 0
    for (first, rows), ref in zip(ranges, parts):
        out_ref[pl.ds(at, rows), :] = ref[pl.ds(first, rows), :]
        at += rows


def rows_of(place, slot, cols):
    return pl.ds(pl.multiple_of((place[0] ^ DISTANCES[slot]) * cols, cols), cols)


def solve_kernel(place, own_ref, *refs):
    *blocks, up_ref, down_ref, solved_ref, inverse, high, low, s_high, s_low = refs
    phases, cols = inverse.shape
    blocks = [own_ref, *blocks]
    diagonal = on_diagonal(cols, cols)
    for slot, block in enumerate(blocks):
        rows, slot_cols = rows_of(place, slot, cols), pl.ds(slot * cols, cols)
        high[:, slot_cols], low[:, slot_cols] = split(block[pl.ds(0, phases), :])
        square = block[rows, :]
        rate = -jnp.sum(jnp.where(diagonal, square, 0.0), axis=1, keepdims=True)
        inverse[rows, :] = jnp.broadcast_to(1.0 / rate, (cols, cols))
        high[rows, slot_cols], low[rows, slot_cols] = split(jnp.where(diagonal, 0.0, square))
    for side, ref in enumerate((up_ref, down_ref)):
        solved_ref[:, pl.ds(side * cols, cols)] = ref[0] * inverse[...]
    for _ in range(SWEEPS):
        for slot in range(len(blocks)):
            rows, slot_rows = rows_of(place, slot, cols), pl.ds(slot * cols, cols)
            s_high[slot_rows, :], s_low[slot_rows, :] = split(solved_ref[rows, :])
        product = exact_dot((high[...], low[...]), (s_high[...], s_low[...]))
        for side, ref in enumerate((up_ref, down_ref)):
            columns = slice(side * cols, (side + 1) * cols)
            solved_ref[:, columns] = (ref[0] + product[:, columns]) * inverse[...]


def gathered_product(place, blocks, first_slot, solved_ref):
    cols = blocks[0].shape[-1]
    left = split(jnp.concatenate(blocks, axis=1))
    rows = [rows_of(place, first_slot + at, cols) for at in range(len(blocks))]
    right = split(jnp.concatenate([solved_ref[r, :] for r in rows], axis=0))
    return exact_dot(left, right)


def upper_kernel(place, own_ref, near_ref, far_ref, last_ref, solved_ref, level_ref, part_level, part_up):
    phases, cols = part_up.shape
    up = pl.ds(phases + PEAK_ROWS, phases)
    upper = gathered_product(place, [own_ref[up, :], near_ref[up, :], far_ref[...], last_ref[...]], 0, solved_ref)
    part_up[...] = upper[:, :cols]
    part_level[...] = level_ref[0] + upper[:, cols:]


def lower_kernel(place, own_ref, near_ref, far_ref, below_ref, upper_level, part_level, part_down):
    phases, cols = part_down.shape
    blocks = [own_ref[pl.ds(2 * phases + PEAK_ROWS, phases), :], near_ref[...], far_ref[...]]
    lower = gathered_product(place, blocks, 0, below_ref)
    part_down[...] = lower[:, cols:]
    part_level[...] = upper_level[...] + lower[:, :cols]


def output_kernel(place, last_ref, below_ref, part_level, part_up, part_down, peak_ref, new_level, new_up, new_down):
    phases, cols = part_up.shape
    scale = 1.0 / jnp.maximum(peak_ref[...], last_ref[pl.ds(phases, PEAK_ROWS), :])[0:1, :]
    new_up[0] = part_up[...] * scale
    lower = gathered_product(place, [last_ref[pl.ds(0, phases), :]], len(DISTANCES) - 1, below_ref)
    new_down[0] = (part_down[...] + lower[:, cols:]) * scale
    new_level[0] = (part_level[...] + lower[:, :cols]) * scale


def per_device(up_blocks, level_blocks, down_blocks):
    levels, phases, cols = level_blocks.shape
    shards = lax.axis_size("col")
    ranges = lax.axis_size("lvl")
    assert levels == 2 and shards == len(DISTANCES)
    place = lax.axis_index("col").astype(jnp.int32).reshape(1)
    params = pltpu.CompilerParams(vmem_limit_bytes=32 * 2**20)
    shape = lambda rows, columns=cols: jax.ShapeDtypeStruct((rows, columns), F32)

    def call(kernel, out_shape, in_specs, *operands, scratch=(), **options):
        return pl.pallas_call(
            kernel,
            out_shape=out_shape,
            in_specs=in_specs,
            out_specs=jax.tree.map(lambda _: VMEM, out_shape),
            scratch_shapes=scratch,
            grid=(1,),
            compiler_params=params,
            **options,
        )(*operands)

    def one_level(parity):
        return pl.BlockSpec((1, phases, cols), lambda step: (parity, 0, 0))

    def exchanged(part, distance):
        return lax.ppermute(part, "col", [(i, i ^ distance) for i in range(shards)])

    def after(value, *earlier):
        return lax.optimization_barrier((value, *earlier))[0]

    def stack(*pieces):
        ranges_of = [(first, rows) for _, first, rows in pieces]
        kernel = functools.partial(stack_kernel, ranges_of)
        return call(kernel, shape(sum(rows for _, rows in ranges_of)), [VMEM] * len(pieces), *[p[0] for p in pieces])

    odd, even = one_level(1), one_level(0)
    in_hbm = [pltpu.with_memory_space_constraint(x, pltpu.HBM) for x in (up_blocks, level_blocks, down_blocks)]
    sent = call(
        prepare_kernel,
        shape(3 * phases + PEAK_ROWS),
        [SMEM] + [ANY] * 3,
        place,
        *in_hbm,
        scratch=[pltpu.VMEM((levels, cols, cols), F32), pltpu.SemaphoreType.DMA((4,))],
    )
    up_row, down_row = phases + PEAK_ROWS, 2 * phases + PEAK_ROWS
    level_far, near = exchanged(sent[: up_row + PAD_ROWS], 3), exchanged(sent[:down_row], 1)
    level_last = exchanged(level_far, 1)
    up_far = exchanged(after(sent, level_far)[up_row:down_row], 3)
    down_near = exchanged(after(sent, level_far)[down_row:], 1)
    down_far = exchanged(after(sent, up_far)[down_row:], 3)
    up_last = exchanged(up_far, 1)
    peak = jnp.maximum(sent[phases:up_row], level_far[phases:up_row])
    peaks, reach = [peak], 1
    while reach < ranges:
        route = [(i, (i + reach) % ranges) for i in range(ranges)]
        peaks.append(jnp.maximum(peaks[-1], lax.ppermute(peaks[-1], "lvl", route)))
        reach *= 2
    peak = peaks[-1]
    down_last = exchanged(stack((down_far, 0, phases), (peak, 0, PEAK_ROWS)), 1)

    solved = call(
        solve_kernel,
        shape(phases, 2 * cols),
        [SMEM, *[VMEM] * 4, odd, odd],
        after(place, peak),
        sent,
        near,
        level_far,
        level_last,
        up_blocks,
        down_blocks,
        scratch=[
            pltpu.VMEM((phases, cols), F32),
            pltpu.VMEM((phases, phases), BF16),
            pltpu.VMEM((phases, phases), BF16),
            pltpu.VMEM((phases, 2 * cols), BF16),
            pltpu.VMEM((phases, 2 * cols), BF16),
        ],
    )
    from_below = lax.ppermute(after(solved, down_near), "lvl", [(i, i + 1) for i in range(ranges - 1)])

    free = pl.CostEstimate(flops=0, bytes_accessed=0, transcendentals=0)
    upper_level, part_up = call(
        upper_kernel,
        (shape(phases),) * 2,
        [SMEM, *[VMEM] * 5, even],
        place,
        sent,
        near,
        up_far,
        up_last,
        solved,
        level_blocks,
        cost_estimate=free,
    )
    part_level, part_down = call(
        lower_kernel,
        (shape(phases),) * 2,
        [SMEM, *[VMEM] * 5],
        place,
        sent,
        down_near,
        down_far,
        from_below,
        upper_level,
        cost_estimate=free,
    )
    return call(
        output_kernel,
        (jax.ShapeDtypeStruct((1, phases, cols), F32),) * 3,
        [SMEM] + [VMEM] * 6,
        place,
        down_last,
        from_below,
        part_level,
        part_up,
        part_down,
        peak,
    )


def solution(mesh):
    placed = (P("lvl", None, "col"),) * 3
    return jax.shard_map(per_device, mesh=mesh, in_specs=placed, out_specs=placed, check_vma=False)
```

```python
import functools

import jax
import jax.numpy as jnp
from jax import lax
from jax.experimental import pallas as pl
from jax.experimental.pallas import tpu as pltpu
from jax.sharding import PartitionSpec as P

SWEEPS = 2
PEAK_ROWS = 8
PAD_ROWS = 24
DISTANCES = (0, 1, 3, 2)
F32 = jnp.float32
BF16 = jnp.bfloat16
VMEM = pl.BlockSpec(memory_space=pltpu.VMEM)
ANY = pl.BlockSpec(memory_space=pl.ANY)
SMEM = pl.BlockSpec(memory_space=pltpu.SMEM)


def split(x):
    high = x.astype(BF16)
    return high, (x - high.astype(F32)).astype(BF16)


def exact_dot(left, right):
    (left_high, left_low), (right_high, right_low) = left, right
    dot = lambda a, b: jnp.dot(a, b, preferred_element_type=F32)
    return dot(left_high, right_high) + (dot(left_high, right_low) + dot(left_low, right_high))


def on_diagonal(rows, cols):
    row = lax.broadcasted_iota(jnp.int32, (rows, cols), 0)
    return row == lax.broadcasted_iota(jnp.int32, (rows, cols), 1)


def prepare_kernel(place, up_ref, level_ref, down_ref, sent_ref, square, sems):
    _, phases, cols = level_ref.shape
    own = rows_of(place, 0, cols)
    sources = [level_ref.at[:, own, :], level_ref.at[1], up_ref.at[0], down_ref.at[0]]
    starts = (0, phases + PEAK_ROWS, 2 * phases + PEAK_ROWS)
    targets = [square, *[sent_ref.at[pl.ds(start, phases), :] for start in starts]]
    copies = [
        pltpu.make_async_copy(source, target, sems.at[at])
        for at, (source, target) in enumerate(zip(sources, targets))
    ]
    for copy in copies:
        copy.start()
    copies[0].wait()
    lowest = jnp.min(jnp.where(on_diagonal(cols, cols)[None], square[...], 0.0))
    sent_ref[pl.ds(phases, PEAK_ROWS), :] = jnp.full((PEAK_ROWS, cols), -lowest, F32)
    for copy in copies[1:]:
        copy.wait()


def stack_kernel(ranges, *refs):
    *parts, out_ref = refs
    at = 0
    for (first, rows), ref in zip(ranges, parts):
        out_ref[pl.ds(at, rows), :] = ref[pl.ds(first, rows), :]
        at += rows


def rows_of(place, slot, cols):
    return pl.ds(pl.multiple_of((place[0] ^ DISTANCES[slot]) * cols, cols), cols)


def solve_kernel(place, own_ref, *refs):
    *blocks, up_ref, down_ref, solved_ref, inverse, high, low, s_high, s_low = refs
    phases, cols = inverse.shape
    blocks = [own_ref, *blocks]
    diagonal = on_diagonal(cols, cols)
    for slot, block in enumerate(blocks):
        rows, slot_cols = rows_of(place, slot, cols), pl.ds(slot * cols, cols)
        high[:, slot_cols], low[:, slot_cols] = split(block[pl.ds(0, phases), :])
        square = block[rows, :]
        rate = -jnp.sum(jnp.where(diagonal, square, 0.0), axis=1, keepdims=True)
        inverse[rows, :] = jnp.broadcast_to(1.0 / rate, (cols, cols))
        high[rows, slot_cols], low[rows, slot_cols] = split(jnp.where(diagonal, 0.0, square))
    for side, ref in enumerate((up_ref, down_ref)):
        solved_ref[:, pl.ds(side * cols, cols)] = ref[0] * inverse[...]
    for _ in range(SWEEPS):
        for slot in range(len(blocks)):
            rows, slot_rows = rows_of(place, slot, cols), pl.ds(slot * cols, cols)
            s_high[slot_rows, :], s_low[slot_rows, :] = split(solved_ref[rows, :])
        product = exact_dot((high[...], low[...]), (s_high[...], s_low[...]))
        for side, ref in enumerate((up_ref, down_ref)):
            columns = slice(side * cols, (side + 1) * cols)
            solved_ref[:, columns] = (ref[0] + product[:, columns]) * inverse[...]


def gathered_product(place, blocks, first_slot, solved_ref):
    cols = blocks[0].shape[-1]
    left = split(jnp.concatenate(blocks, axis=1))
    rows = [rows_of(place, first_slot + at, cols) for at in range(len(blocks))]
    right = split(jnp.concatenate([solved_ref[r, :] for r in rows], axis=0))
    return exact_dot(left, right)


def upper_kernel(place, own_ref, near_ref, far_ref, last_ref, solved_ref, level_ref, part_level, part_up):
    phases, cols = part_up.shape
    up = pl.ds(phases + PEAK_ROWS, phases)
    upper = gathered_product(place, [own_ref[up, :], near_ref[up, :], far_ref[...], last_ref[...]], 0, solved_ref)
    part_up[...] = upper[:, :cols]
    part_level[...] = level_ref[0] + upper[:, cols:]


def lower_kernel(place, own_ref, near_ref, far_ref, below_ref, upper_level, part_level, part_down):
    phases, cols = part_down.shape
    blocks = [own_ref[pl.ds(2 * phases + PEAK_ROWS, phases), :], near_ref[...], far_ref[...]]
    lower = gathered_product(place, blocks, 0, below_ref)
    part_down[...] = lower[:, cols:]
    part_level[...] = upper_level[...] + lower[:, :cols]


def output_kernel(place, last_ref, below_ref, part_level, part_up, part_down, peak_ref, new_level, new_up, new_down):
    phases, cols = part_up.shape
    scale = 1.0 / jnp.maximum(peak_ref[...], last_ref[pl.ds(phases, PEAK_ROWS), :])[0:1, :]
    new_up[0] = part_up[...] * scale
    lower = gathered_product(place, [last_ref[pl.ds(0, phases), :]], len(DISTANCES) - 1, below_ref)
    new_down[0] = (part_down[...] + lower[:, cols:]) * scale
    new_level[0] = (part_level[...] + lower[:, :cols]) * scale


def per_device(up_blocks, level_blocks, down_blocks):
    levels, phases, cols = level_blocks.shape
    shards = lax.axis_size("col")
    ranges = lax.axis_size("lvl")
    assert levels == 2 and shards == len(DISTANCES)
    place = lax.axis_index("col").astype(jnp.int32).reshape(1)
    params = pltpu.CompilerParams(vmem_limit_bytes=32 * 2**20)
    shape = lambda rows, columns=cols: jax.ShapeDtypeStruct((rows, columns), F32)

    def call(kernel, out_shape, in_specs, *operands, scratch=(), **options):
        return pl.pallas_call(
            kernel,
            out_shape=out_shape,
            in_specs=in_specs,
            out_specs=jax.tree.map(lambda _: VMEM, out_shape),
            scratch_shapes=scratch,
            grid=(1,),
            compiler_params=params,
            **options,
        )(*operands)

    def one_level(parity):
        return pl.BlockSpec((1, phases, cols), lambda step: (parity, 0, 0))

    def exchanged(part, distance):
        return lax.ppermute(part, "col", [(i, i ^ distance) for i in range(shards)])

    def after(value, *earlier):
        return lax.optimization_barrier((value, *earlier))[0]

    def stack(*pieces):
        ranges_of = [(first, rows) for _, first, rows in pieces]
        kernel = functools.partial(stack_kernel, ranges_of)
        return call(kernel, shape(sum(rows for _, rows in ranges_of)), [VMEM] * len(pieces), *[p[0] for p in pieces])

    odd, even = one_level(1), one_level(0)
    in_hbm = [pltpu.with_memory_space_constraint(x, pltpu.HBM) for x in (up_blocks, level_blocks, down_blocks)]
    sent = call(
        prepare_kernel,
        shape(3 * phases + PEAK_ROWS),
        [SMEM] + [ANY] * 3,
        place,
        *in_hbm,
        scratch=[pltpu.VMEM((levels, cols, cols), F32), pltpu.SemaphoreType.DMA((4,))],
    )
    up_row, down_row = phases + PEAK_ROWS, 2 * phases + PEAK_ROWS
    level_far, near = exchanged(sent[: up_row + PAD_ROWS], 3), exchanged(sent[:down_row], 1)
    level_last = exchanged(level_far, 1)
    up_far = exchanged(after(sent, level_far)[up_row:down_row], 3)
    down_near = exchanged(after(sent, level_far)[down_row:], 1)
    down_far = exchanged(after(sent, up_far)[down_row:], 3)
    peak = jnp.maximum(sent[phases:up_row], level_far[phases:up_row])
    peaks, reach = [peak], 1
    while reach < ranges:
        route = [(i, (i + reach) % ranges) for i in range(ranges)]
        peaks.append(jnp.maximum(peaks[-1], lax.ppermute(peaks[-1], "lvl", route)))
        reach *= 2
    peak = peaks[-1]
    up_last = exchanged(after(up_far, peak), 1)
    down_last = exchanged(stack((down_far, 0, phases), (peak, 0, PEAK_ROWS)), 1)

    solved = call(
        solve_kernel,
        shape(phases, 2 * cols),
        [SMEM, *[VMEM] * 4, odd, odd],
        after(place, peak),
        sent,
        near,
        level_far,
        level_last,
        up_blocks,
        down_blocks,
        scratch=[
            pltpu.VMEM((phases, cols), F32),
            pltpu.VMEM((phases, phases), BF16),
            pltpu.VMEM((phases, phases), BF16),
            pltpu.VMEM((phases, 2 * cols), BF16),
            pltpu.VMEM((phases, 2 * cols), BF16),
        ],
    )
    from_below = lax.ppermute(after(solved, down_near, up_last), "lvl", [(i, i + 1) for i in range(ranges - 1)])

    free = pl.CostEstimate(flops=0, bytes_accessed=0, transcendentals=0)
    upper_level, part_up = call(
        upper_kernel,
        (shape(phases),) * 2,
        [SMEM, *[VMEM] * 5, even],
        place,
        sent,
        near,
        up_far,
        up_last,
        solved,
        level_blocks,
        cost_estimate=free,
    )
    part_level, part_down = call(
        lower_kernel,
        (shape(phases),) * 2,
        [SMEM, *[VMEM] * 5],
        place,
        sent,
        down_near,
        down_far,
        from_below,
        upper_level,
        cost_estimate=free,
    )
    return call(
        output_kernel,
        (jax.ShapeDtypeStruct((1, phases, cols), F32),) * 3,
        [SMEM] + [VMEM] * 6,
        place,
        down_last,
        from_below,
        part_level,
        part_up,
        part_down,
        peak,
    )


def solution(mesh):
    placed = (P("lvl", None, "col"),) * 3
    return jax.shard_map(per_device, mesh=mesh, in_specs=placed, out_specs=placed, check_vma=False)
```

```python
import functools

import jax
import jax.numpy as jnp
from jax import lax
from jax.experimental import pallas as pl
from jax.experimental.pallas import tpu as pltpu
from jax.sharding import PartitionSpec as P

SWEEPS = 2
PEAK_ROWS = 8
F32 = jnp.float32
BF16 = jnp.bfloat16
VMEM = pl.BlockSpec(memory_space=pltpu.VMEM)
ANY = pl.BlockSpec(memory_space=pl.ANY)
SMEM = pl.BlockSpec(memory_space=pltpu.SMEM)


def split(x):
    high = x.astype(BF16)
    return high, (x - high.astype(F32)).astype(BF16)


def exact_dot(left, right):
    (left_high, left_low), (right_high, right_low) = left, right
    dot = lambda a, b: jnp.dot(a, b, preferred_element_type=F32)
    return dot(left_high, right_high) + (dot(left_high, right_low) + dot(left_low, right_high))


def on_diagonal(rows, cols):
    row = lax.broadcasted_iota(jnp.int32, (rows, cols), 0)
    return row == lax.broadcasted_iota(jnp.int32, (rows, cols), 1)


def prepare_kernel(place, up_ref, level_ref, down_ref, sent_ref, square, sems):
    _, phases, cols = level_ref.shape
    own = rows_of(place, 0, cols)
    sources = [level_ref.at[:, own, :], level_ref.at[1], up_ref.at[0], down_ref.at[0]]
    starts = (0, phases + PEAK_ROWS, 2 * phases + PEAK_ROWS)
    targets = [square, *[sent_ref.at[pl.ds(start, phases), :] for start in starts]]
    copies = [
        pltpu.make_async_copy(source, target, sems.at[at])
        for at, (source, target) in enumerate(zip(sources, targets))
    ]
    for copy in copies:
        copy.start()
    copies[0].wait()
    lowest = jnp.min(jnp.where(on_diagonal(cols, cols)[None], square[...], 0.0))
    sent_ref[pl.ds(phases, PEAK_ROWS), :] = jnp.full((PEAK_ROWS, cols), -lowest, F32)
    for copy in copies[1:]:
        copy.wait()


def stack_kernel(ranges, *refs):
    *parts, out_ref = refs
    at = 0
    for (first, rows), ref in zip(ranges, parts):
        out_ref[pl.ds(at, rows), :] = ref[pl.ds(first, rows), :]
        at += rows


def rows_of(place, slot, cols):
    z = place[0]
    inner = (z ^ (z >> 1)) & 1
    return pl.ds(pl.multiple_of((z ^ (0, 1, 2 + inner, 3 - inner)[slot]) * cols, cols), cols)


def solve_kernel(place, own_ref, near_ref, inner_ref, hand_ref, cross_ref, last_ref, up_ref, down_ref, solved_ref, *scratch):
    inverse, high, low, s_high, s_low = scratch
    phases, cols = inverse.shape
    diagonal = on_diagonal(cols, cols)
    blocks = [(own_ref,), (near_ref,), (inner_ref, hand_ref), (cross_ref, last_ref)]

    def part(refs, rows):
        return sum(ref[rows, :] for ref in refs[1:]) + refs[0][rows, :] if len(refs) > 1 else refs[0][rows, :]

    for slot, refs in enumerate(blocks):
        rows, slot_cols = rows_of(place, slot, cols), pl.ds(slot * cols, cols)
        high[:, slot_cols], low[:, slot_cols] = split(part(refs, pl.ds(0, phases)))
        square = part(refs, rows)
        rate = -jnp.sum(jnp.where(diagonal, square, 0.0), axis=1, keepdims=True)
        inverse[rows, :] = jnp.broadcast_to(1.0 / rate, (cols, cols))
        high[rows, slot_cols], low[rows, slot_cols] = split(jnp.where(diagonal, 0.0, square))
    for side, ref in enumerate((up_ref, down_ref)):
        solved_ref[:, pl.ds(side * cols, cols)] = ref[0] * inverse[...]
    for _ in range(SWEEPS):
        for slot in range(len(blocks)):
            rows, slot_rows = rows_of(place, slot, cols), pl.ds(slot * cols, cols)
            s_high[slot_rows, :], s_low[slot_rows, :] = split(solved_ref[rows, :])
        product = exact_dot((high[...], low[...]), (s_high[...], s_low[...]))
        for side, ref in enumerate((up_ref, down_ref)):
            columns = slice(side * cols, (side + 1) * cols)
            solved_ref[:, columns] = (ref[0] + product[:, columns]) * inverse[...]


def gathered_product(place, blocks, first_slot, solved_ref):
    cols = blocks[0].shape[-1]
    left = split(jnp.concatenate(blocks, axis=1))
    rows = [rows_of(place, first_slot + at, cols) for at in range(len(blocks))]
    right = split(jnp.concatenate([solved_ref[r, :] for r in rows], axis=0))
    return exact_dot(left, right)


def upper_kernel(place, own_ref, near_ref, inner_ref, hand_ref, cross_ref, solved_ref, level_ref, part_level, part_up):
    phases, cols = part_up.shape
    up, top = pl.ds(phases + PEAK_ROWS, phases), pl.ds(0, phases)
    blocks = [own_ref[up, :], near_ref[up, :], inner_ref[up, :] + hand_ref[up, :], cross_ref[top, :]]
    upper = gathered_product(place, blocks, 0, solved_ref)
    part_up[...] = upper[:, :cols]
    part_level[...] = level_ref[0] + upper[:, cols:]


def lower_kernel(place, own_ref, near_ref, inner_ref, hand_ref, cross_ref, below_ref, upper_level, peak_ref, *parts):
    part_level, part_down, part_peak = parts
    phases, cols = part_down.shape
    down, middle = pl.ds(2 * phases + PEAK_ROWS, phases), pl.ds(phases, phases)
    blocks = [own_ref[down, :], near_ref[down, :], inner_ref[down, :] + hand_ref[down, :], cross_ref[middle, :]]
    lower = gathered_product(place, blocks, 0, below_ref)
    part_down[...] = lower[:, cols:]
    part_level[...] = upper_level[...] + lower[:, :cols]
    part_peak[...] = jnp.maximum(peak_ref[...], cross_ref[pl.ds(2 * phases, PEAK_ROWS), :])


def output_kernel(place, last_ref, solved_ref, below_ref, part_level, part_up, part_down, peak_ref, *outs):
    new_level, new_up, new_down = outs
    phases, cols = part_up.shape
    scale = 1.0 / jnp.maximum(peak_ref[...], last_ref[pl.ds(2 * phases, PEAK_ROWS), :])[0:1, :]
    upper = gathered_product(place, [last_ref[pl.ds(0, phases), :]], 3, solved_ref)
    new_up[0] = (part_up[...] + upper[:, :cols]) * scale
    lower = gathered_product(place, [last_ref[pl.ds(phases, phases), :]], 3, below_ref)
    new_down[0] = (part_down[...] + lower[:, cols:]) * scale
    new_level[0] = (part_level[...] + upper[:, cols:] + lower[:, :cols]) * scale


def per_device(up_blocks, level_blocks, down_blocks):
    levels, phases, cols = level_blocks.shape
    shards = lax.axis_size("col")
    ranges = lax.axis_size("lvl")
    assert levels == 2 and shards == 4
    place = lax.axis_index("col").astype(jnp.int32).reshape(1)
    params = pltpu.CompilerParams(vmem_limit_bytes=32 * 2**20)
    shape = lambda rows, columns=cols: jax.ShapeDtypeStruct((rows, columns), F32)

    def call(kernel, out_shape, in_specs, *operands, scratch=(), **options):
        return pl.pallas_call(
            kernel,
            out_shape=out_shape,
            in_specs=in_specs,
            out_specs=jax.tree.map(lambda _: VMEM, out_shape),
            scratch_shapes=scratch,
            grid=(1,),
            compiler_params=params,
            **options,
        )(*operands)

    def one_level(parity):
        return pl.BlockSpec((1, phases, cols), lambda step: (parity, 0, 0))

    def near(part):
        return lax.ppermute(part, "col", [(i, i ^ 1) for i in range(shards)])

    def inner(part):
        return lax.ppermute(part, "col", [(1, 2), (2, 1)])

    def to_ends(part):
        return lax.ppermute(part, "col", [(1, 0), (shards - 2, shards - 1)])

    def after(value, *earlier):
        return lax.optimization_barrier((value, *earlier))[0]

    def stack(*pieces):
        ranges_of = [(first, rows) for _, first, rows in pieces]
        kernel = functools.partial(stack_kernel, ranges_of)
        return call(kernel, shape(sum(rows for _, rows in ranges_of)), [VMEM] * len(pieces), *[p[0] for p in pieces])

    odd, even = one_level(1), one_level(0)
    in_hbm = [pltpu.with_memory_space_constraint(x, pltpu.HBM) for x in (up_blocks, level_blocks, down_blocks)]
    sent = call(
        prepare_kernel,
        shape(3 * phases + PEAK_ROWS),
        [SMEM] + [ANY] * 3,
        place,
        *in_hbm,
        scratch=[pltpu.VMEM((levels, cols, cols), F32), pltpu.SemaphoreType.DMA((4,))],
    )
    up_row = phases + PEAK_ROWS
    near_blocks, inner_blocks = near(sent), inner(sent)
    peak, reach = sent[phases:up_row], 1
    while reach < ranges:
        route = [(i, (i + reach) % ranges) for i in range(ranges)]
        peak = jnp.maximum(peak, lax.ppermute(peak, "lvl", route))
        reach *= 2
    hand_blocks = to_ends(after(inner_blocks, peak))
    peak = jnp.maximum(peak, near(peak))
    level_cross = inner(after(near_blocks, peak)[:phases])
    level_last = to_ends(level_cross)
    even_cross = inner(stack((after(near_blocks, level_cross), up_row, 2 * phases), (peak, 0, PEAK_ROWS)))
    even_last = to_ends(even_cross)

    solved = call(
        solve_kernel,
        shape(phases, 2 * cols),
        [SMEM, *[VMEM] * 6, odd, odd],
        place,
        sent,
        near_blocks,
        inner_blocks,
        hand_blocks,
        level_cross,
        level_last,
        up_blocks,
        down_blocks,
        scratch=[
            pltpu.VMEM((phases, cols), F32),
            pltpu.VMEM((phases, phases), BF16),
            pltpu.VMEM((phases, phases), BF16),
            pltpu.VMEM((phases, 2 * cols), BF16),
            pltpu.VMEM((phases, 2 * cols), BF16),
        ],
    )
    from_below = lax.ppermute(solved, "lvl", [(i, i + 1) for i in range(ranges - 1)])

    free = pl.CostEstimate(flops=0, bytes_accessed=0, transcendentals=0)
    evens = (sent, near_blocks, inner_blocks, hand_blocks, even_cross)
    upper_level, part_up = call(
        upper_kernel,
        (shape(phases),) * 2,
        [SMEM, *[VMEM] * 6, even],
        place,
        *evens,
        solved,
        level_blocks,
        cost_estimate=free,
    )
    part_level, part_down, part_peak = call(
        lower_kernel,
        (shape(phases), shape(phases), shape(PEAK_ROWS)),
        [SMEM, *[VMEM] * 8],
        place,
        *evens,
        from_below,
        upper_level,
        peak,
        cost_estimate=free,
    )
    return call(
        output_kernel,
        (jax.ShapeDtypeStruct((1, phases, cols), F32),) * 3,
        [SMEM] + [VMEM] * 7,
        place,
        even_last,
        solved,
        from_below,
        part_level,
        part_up,
        part_down,
        part_peak,
    )


def solution(mesh):
    placed = (P("lvl", None, "col"),) * 3
    return jax.shard_map(per_device, mesh=mesh, in_specs=placed, out_specs=placed, check_vma=False)
```

```python
import functools

import jax
import jax.numpy as jnp
from jax import lax
from jax.experimental import pallas as pl
from jax.experimental.pallas import tpu as pltpu
from jax.sharding import PartitionSpec as P

SWEEPS = 2
PEAK_ROWS = 8
F32 = jnp.float32
BF16 = jnp.bfloat16
VMEM = pl.BlockSpec(memory_space=pltpu.VMEM)
ANY = pl.BlockSpec(memory_space=pl.ANY)
SMEM = pl.BlockSpec(memory_space=pltpu.SMEM)


def split(x):
    high = x.astype(BF16)
    return high, (x - high.astype(F32)).astype(BF16)


def exact_dot(left, right):
    (left_high, left_low), (right_high, right_low) = left, right
    dot = lambda a, b: jnp.dot(a, b, preferred_element_type=F32)
    return dot(left_high, right_high) + (dot(left_high, right_low) + dot(left_low, right_high))


def on_diagonal(rows, cols):
    row = lax.broadcasted_iota(jnp.int32, (rows, cols), 0)
    return row == lax.broadcasted_iota(jnp.int32, (rows, cols), 1)


def prepare_kernel(place, up_ref, level_ref, down_ref, sent_ref, square, sems):
    _, phases, cols = level_ref.shape
    own = rows_of(place, 0, cols)
    sources = [level_ref.at[:, own, :], level_ref.at[1], up_ref.at[0], down_ref.at[0]]
    starts = (0, phases + PEAK_ROWS, 2 * phases + PEAK_ROWS)
    targets = [square, *[sent_ref.at[pl.ds(start, phases), :] for start in starts]]
    copies = [
        pltpu.make_async_copy(source, target, sems.at[at])
        for at, (source, target) in enumerate(zip(sources, targets))
    ]
    for copy in copies:
        copy.start()
    copies[0].wait()
    lowest = jnp.min(jnp.where(on_diagonal(cols, cols)[None], square[...], 0.0))
    sent_ref[pl.ds(phases, PEAK_ROWS), :] = jnp.full((PEAK_ROWS, cols), -lowest, F32)
    for copy in copies[1:]:
        copy.wait()


def stack_kernel(ranges, *refs):
    *parts, out_ref = refs
    at = 0
    for (first, rows), ref in zip(ranges, parts):
        out_ref[pl.ds(at, rows), :] = ref[pl.ds(first, rows), :]
        at += rows


def rows_of(place, slot, cols):
    z = place[0]
    inner = (z ^ (z >> 1)) & 1
    return pl.ds(pl.multiple_of((z ^ (0, 1, 2 + inner, 3 - inner)[slot]) * cols, cols), cols)


def solve_kernel(place, own_ref, near_ref, inner_ref, hand_ref, cross_ref, last_ref, up_ref, down_ref, solved_ref, *scratch):
    inverse, high, low, s_high, s_low = scratch
    phases, cols = inverse.shape
    diagonal = on_diagonal(cols, cols)
    blocks = [(own_ref,), (near_ref,), (inner_ref, hand_ref), (cross_ref, last_ref)]

    def part(refs, rows):
        return sum(ref[rows, :] for ref in refs[1:]) + refs[0][rows, :] if len(refs) > 1 else refs[0][rows, :]

    for slot, refs in enumerate(blocks):
        rows, slot_cols = rows_of(place, slot, cols), pl.ds(slot * cols, cols)
        high[:, slot_cols], low[:, slot_cols] = split(part(refs, pl.ds(0, phases)))
        square = part(refs, rows)
        rate = -jnp.sum(jnp.where(diagonal, square, 0.0), axis=1, keepdims=True)
        inverse[rows, :] = jnp.broadcast_to(1.0 / rate, (cols, cols))
        high[rows, slot_cols], low[rows, slot_cols] = split(jnp.where(diagonal, 0.0, square))
    for side, ref in enumerate((up_ref, down_ref)):
        solved_ref[:, pl.ds(side * cols, cols)] = ref[0] * inverse[...]
    for _ in range(SWEEPS):
        for slot in range(len(blocks)):
            rows, slot_rows = rows_of(place, slot, cols), pl.ds(slot * cols, cols)
            s_high[slot_rows, :], s_low[slot_rows, :] = split(solved_ref[rows, :])
        product = exact_dot((high[...], low[...]), (s_high[...], s_low[...]))
        for side, ref in enumerate((up_ref, down_ref)):
            columns = slice(side * cols, (side + 1) * cols)
            solved_ref[:, columns] = (ref[0] + product[:, columns]) * inverse[...]


def gathered_product(place, blocks, first_slot, solved_ref):
    cols = blocks[0].shape[-1]
    left = split(jnp.concatenate(blocks, axis=1))
    rows = [rows_of(place, first_slot + at, cols) for at in range(len(blocks))]
    right = split(jnp.concatenate([solved_ref[r, :] for r in rows], axis=0))
    return exact_dot(left, right)


def upper_kernel(place, own_ref, near_ref, inner_ref, hand_ref, cross_ref, solved_ref, level_ref, part_level, part_up):
    phases, cols = part_up.shape
    up, top = pl.ds(phases + PEAK_ROWS, phases), pl.ds(0, phases)
    blocks = [own_ref[up, :], near_ref[top, :], inner_ref[top, :] + hand_ref[top, :], cross_ref[top, :]]
    upper = gathered_product(place, blocks, 0, solved_ref)
    part_up[...] = upper[:, :cols]
    part_level[...] = level_ref[0] + upper[:, cols:]


def lower_kernel(place, own_ref, near_ref, inner_ref, hand_ref, cross_ref, below_ref, upper_level, peak_ref, *parts):
    part_level, part_down, part_peak = parts
    phases, cols = part_down.shape
    down, middle = pl.ds(2 * phases + PEAK_ROWS, phases), pl.ds(phases, phases)
    blocks = [own_ref[down, :], near_ref[middle, :], inner_ref[middle, :] + hand_ref[middle, :], cross_ref[middle, :]]
    lower = gathered_product(place, blocks, 0, below_ref)
    part_down[...] = lower[:, cols:]
    part_level[...] = upper_level[...] + lower[:, :cols]
    part_peak[...] = jnp.maximum(peak_ref[...], cross_ref[pl.ds(2 * phases, PEAK_ROWS), :])


def output_kernel(place, last_ref, solved_ref, below_ref, part_level, part_up, part_down, peak_ref, *outs):
    new_level, new_up, new_down = outs
    phases, cols = part_up.shape
    scale = 1.0 / jnp.maximum(peak_ref[...], last_ref[pl.ds(2 * phases, PEAK_ROWS), :])[0:1, :]
    upper = gathered_product(place, [last_ref[pl.ds(0, phases), :]], 3, solved_ref)
    new_up[0] = (part_up[...] + upper[:, :cols]) * scale
    lower = gathered_product(place, [last_ref[pl.ds(phases, phases), :]], 3, below_ref)
    new_down[0] = (part_down[...] + lower[:, cols:]) * scale
    new_level[0] = (part_level[...] + upper[:, cols:] + lower[:, :cols]) * scale


def per_device(up_blocks, level_blocks, down_blocks):
    levels, phases, cols = level_blocks.shape
    shards = lax.axis_size("col")
    ranges = lax.axis_size("lvl")
    assert levels == 2 and shards == 4
    place = lax.axis_index("col").astype(jnp.int32).reshape(1)
    params = pltpu.CompilerParams(vmem_limit_bytes=32 * 2**20)
    shape = lambda rows, columns=cols: jax.ShapeDtypeStruct((rows, columns), F32)

    def call(kernel, out_shape, in_specs, *operands, scratch=(), **options):
        return pl.pallas_call(
            kernel,
            out_shape=out_shape,
            in_specs=in_specs,
            out_specs=jax.tree.map(lambda _: VMEM, out_shape),
            scratch_shapes=scratch,
            grid=(1,),
            compiler_params=params,
            **options,
        )(*operands)

    def one_level(parity):
        return pl.BlockSpec((1, phases, cols), lambda step: (parity, 0, 0))

    def near(part):
        return lax.ppermute(part, "col", [(i, i ^ 1) for i in range(shards)])

    def inner(part):
        return lax.ppermute(part, "col", [(1, 2), (2, 1)])

    def to_ends(part):
        return lax.ppermute(part, "col", [(1, 0), (shards - 2, shards - 1)])

    def after(value, *earlier):
        return lax.optimization_barrier((value, *earlier))[0]

    def stack(*pieces):
        ranges_of = [(first, rows) for _, first, rows in pieces]
        kernel = functools.partial(stack_kernel, ranges_of)
        return call(kernel, shape(sum(rows for _, rows in ranges_of)), [VMEM] * len(pieces), *[p[0] for p in pieces])

    odd, even = one_level(1), one_level(0)
    in_hbm = [pltpu.with_memory_space_constraint(x, pltpu.HBM) for x in (up_blocks, level_blocks, down_blocks)]
    sent = call(
        prepare_kernel,
        shape(3 * phases + PEAK_ROWS),
        [SMEM] + [ANY] * 3,
        place,
        *in_hbm,
        scratch=[pltpu.VMEM((levels, cols, cols), F32), pltpu.SemaphoreType.DMA((4,))],
    )
    up_row = phases + PEAK_ROWS
    level_near, level_inner = near(sent[:up_row]), inner(sent[:up_row])
    even_near = near(after(sent, level_near, level_inner)[up_row:])
    level_cross, level_hand = inner(level_near), to_ends(level_inner)
    even_inner = inner(after(sent, level_cross, level_hand)[up_row:])
    level_last = to_ends(level_cross)
    peak, reach = jnp.maximum(after(sent, level_inner)[phases:up_row], level_near[phases:]), 1
    while reach < ranges:
        route = [(i, (i + reach) % ranges) for i in range(ranges)]
        peak = jnp.maximum(peak, lax.ppermute(peak, "lvl", route))
        reach *= 2
    even_hand = to_ends(even_inner)
    even_cross = inner(stack((after(even_near, even_inner, level_last), 0, 2 * phases), (peak, 0, PEAK_ROWS)))

    solved = call(
        solve_kernel,
        shape(phases, 2 * cols),
        [SMEM, *[VMEM] * 6, odd, odd],
        place,
        sent,
        level_near,
        level_inner,
        level_hand,
        level_cross,
        level_last,
        up_blocks,
        down_blocks,
        scratch=[
            pltpu.VMEM((phases, cols), F32),
            pltpu.VMEM((phases, phases), BF16),
            pltpu.VMEM((phases, phases), BF16),
            pltpu.VMEM((phases, 2 * cols), BF16),
            pltpu.VMEM((phases, 2 * cols), BF16),
        ],
    )
    even_last = to_ends(after(even_cross, solved))
    from_below = lax.ppermute(after(solved, even_hand), "lvl", [(i, i + 1) for i in range(ranges - 1)])

    free = pl.CostEstimate(flops=0, bytes_accessed=0, transcendentals=0)
    evens = (sent, even_near, even_inner, even_hand, even_cross)
    upper_level, part_up = call(
        upper_kernel,
        (shape(phases),) * 2,
        [SMEM, *[VMEM] * 6, even],
        place,
        *evens,
        solved,
        level_blocks,
        cost_estimate=free,
    )
    part_level, part_down, part_peak = call(
        lower_kernel,
        (shape(phases), shape(phases), shape(PEAK_ROWS)),
        [SMEM, *[VMEM] * 8],
        place,
        *evens,
        from_below,
        upper_level,
        peak,
        cost_estimate=free,
    )
    return call(
        output_kernel,
        (jax.ShapeDtypeStruct((1, phases, cols), F32),) * 3,
        [SMEM] + [VMEM] * 7,
        place,
        even_last,
        solved,
        from_below,
        part_level,
        part_up,
        part_down,
        part_peak,
    )


def solution(mesh):
    placed = (P("lvl", None, "col"),) * 3
    return jax.shard_map(per_device, mesh=mesh, in_specs=placed, out_specs=placed, check_vma=False)
```

```python
import functools

import jax
import jax.numpy as jnp
from jax import lax
from jax.experimental import pallas as pl
from jax.experimental.pallas import tpu as pltpu
from jax.sharding import PartitionSpec as P

SWEEPS = 2
PEAK_ROWS = 8
PAD_ROWS = 24
DISTANCES = (0, 1, 3, 2)
F32 = jnp.float32
BF16 = jnp.bfloat16
VMEM = pl.BlockSpec(memory_space=pltpu.VMEM)
ANY = pl.BlockSpec(memory_space=pl.ANY)
SMEM = pl.BlockSpec(memory_space=pltpu.SMEM)


def split(x):
    high = x.astype(BF16)
    return high, (x - high.astype(F32)).astype(BF16)


def exact_dot(left, right):
    (left_high, left_low), (right_high, right_low) = left, right
    dot = lambda a, b: jnp.dot(a, b, preferred_element_type=F32)
    return dot(left_high, right_high) + (dot(left_high, right_low) + dot(left_low, right_high))


def on_diagonal(rows, cols):
    row = lax.broadcasted_iota(jnp.int32, (rows, cols), 0)
    return row == lax.broadcasted_iota(jnp.int32, (rows, cols), 1)


def prepare_kernel(place, up_ref, level_ref, down_ref, sent_ref, square, sems):
    _, phases, cols = level_ref.shape
    own = rows_of(place, 0, cols)
    sources = [level_ref.at[:, own, :], level_ref.at[1], up_ref.at[0], down_ref.at[0]]
    starts = (0, phases + PEAK_ROWS, 2 * phases + PEAK_ROWS)
    targets = [square, *[sent_ref.at[pl.ds(start, phases), :] for start in starts]]
    copies = [
        pltpu.make_async_copy(source, target, sems.at[at])
        for at, (source, target) in enumerate(zip(sources, targets))
    ]
    for copy in copies:
        copy.start()
    copies[0].wait()
    lowest = jnp.min(jnp.where(on_diagonal(cols, cols)[None], square[...], 0.0))
    sent_ref[pl.ds(phases, PEAK_ROWS), :] = jnp.full((PEAK_ROWS, cols), -lowest, F32)
    for copy in copies[1:]:
        copy.wait()


def stack_kernel(ranges, *refs):
    *parts, out_ref = refs
    at = 0
    for (first, rows), ref in zip(ranges, parts):
        out_ref[pl.ds(at, rows), :] = ref[pl.ds(first, rows), :]
        at += rows


def rows_of(place, slot, cols):
    return pl.ds(pl.multiple_of((place[0] ^ DISTANCES[slot]) * cols, cols), cols)


def solve_kernel(place, own_ref, *refs):
    *blocks, up_ref, down_ref, solved_ref, inverse, high, low, s_high, s_low = refs
    phases, cols = inverse.shape
    blocks = [own_ref, *blocks]
    diagonal = on_diagonal(cols, cols)
    for slot, block in enumerate(blocks):
        rows, slot_cols = rows_of(place, slot, cols), pl.ds(slot * cols, cols)
        high[:, slot_cols], low[:, slot_cols] = split(block[pl.ds(0, phases), :])
        square = block[rows, :]
        rate = -jnp.sum(jnp.where(diagonal, square, 0.0), axis=1, keepdims=True)
        inverse[rows, :] = jnp.broadcast_to(1.0 / rate, (cols, cols))
        high[rows, slot_cols], low[rows, slot_cols] = split(jnp.where(diagonal, 0.0, square))
    for side, ref in enumerate((up_ref, down_ref)):
        solved_ref[:, pl.ds(side * cols, cols)] = ref[0] * inverse[...]
    for _ in range(SWEEPS):
        for slot in range(len(blocks)):
            rows, slot_rows = rows_of(place, slot, cols), pl.ds(slot * cols, cols)
            s_high[slot_rows, :], s_low[slot_rows, :] = split(solved_ref[rows, :])
        product = exact_dot((high[...], low[...]), (s_high[...], s_low[...]))
        for side, ref in enumerate((up_ref, down_ref)):
            columns = slice(side * cols, (side + 1) * cols)
            solved_ref[:, columns] = (ref[0] + product[:, columns]) * inverse[...]


def gathered_product(place, blocks, first_slot, solved_ref):
    cols = blocks[0].shape[-1]
    left = split(jnp.concatenate(blocks, axis=1))
    rows = [rows_of(place, first_slot + at, cols) for at in range(len(blocks))]
    right = split(jnp.concatenate([solved_ref[r, :] for r in rows], axis=0))
    return exact_dot(left, right)


def upper_kernel(place, own_ref, near_ref, far_ref, last_ref, solved_ref, level_ref, part_level, part_up):
    phases, cols = part_up.shape
    up = pl.ds(phases + PEAK_ROWS, phases)
    upper = gathered_product(place, [own_ref[up, :], near_ref[up, :], far_ref[...], last_ref[...]], 0, solved_ref)
    part_up[...] = upper[:, :cols]
    part_level[...] = level_ref[0] + upper[:, cols:]


def lower_kernel(place, own_ref, near_ref, far_ref, below_ref, upper_level, part_level, part_down):
    phases, cols = part_down.shape
    blocks = [own_ref[pl.ds(2 * phases + PEAK_ROWS, phases), :], near_ref[...], far_ref[...]]
    lower = gathered_product(place, blocks, 0, below_ref)
    part_down[...] = lower[:, cols:]
    part_level[...] = upper_level[...] + lower[:, :cols]


def output_kernel(place, last_ref, below_ref, part_level, part_up, part_down, peak_ref, new_level, new_up, new_down):
    phases, cols = part_up.shape
    scale = 1.0 / jnp.maximum(peak_ref[...], last_ref[pl.ds(phases, PEAK_ROWS), :])[0:1, :]
    new_up[0] = part_up[...] * scale
    lower = gathered_product(place, [last_ref[pl.ds(0, phases), :]], len(DISTANCES) - 1, below_ref)
    new_down[0] = (part_down[...] + lower[:, cols:]) * scale
    new_level[0] = (part_level[...] + lower[:, :cols]) * scale


def per_device(up_blocks, level_blocks, down_blocks):
    levels, phases, cols = level_blocks.shape
    shards = lax.axis_size("col")
    ranges = lax.axis_size("lvl")
    assert levels == 2 and shards == len(DISTANCES)
    place = lax.axis_index("col").astype(jnp.int32).reshape(1)
    params = pltpu.CompilerParams(vmem_limit_bytes=32 * 2**20)
    shape = lambda rows, columns=cols: jax.ShapeDtypeStruct((rows, columns), F32)

    def call(kernel, out_shape, in_specs, *operands, scratch=(), **options):
        return pl.pallas_call(
            kernel,
            out_shape=out_shape,
            in_specs=in_specs,
            out_specs=jax.tree.map(lambda _: VMEM, out_shape),
            scratch_shapes=scratch,
            grid=(1,),
            compiler_params=params,
            **options,
        )(*operands)

    def one_level(parity):
        return pl.BlockSpec((1, phases, cols), lambda step: (parity, 0, 0))

    def exchanged(part, distance):
        return lax.ppermute(part, "col", [(i, i ^ distance) for i in range(shards)])

    def after(value, *earlier):
        return lax.optimization_barrier((value, *earlier))[0]

    def stack(*pieces):
        ranges_of = [(first, rows) for _, first, rows in pieces]
        kernel = functools.partial(stack_kernel, ranges_of)
        return call(kernel, shape(sum(rows for _, rows in ranges_of)), [VMEM] * len(pieces), *[p[0] for p in pieces])

    odd, even = one_level(1), one_level(0)
    in_hbm = [pltpu.with_memory_space_constraint(x, pltpu.HBM) for x in (up_blocks, level_blocks, down_blocks)]
    sent = call(
        prepare_kernel,
        shape(3 * phases + PEAK_ROWS),
        [SMEM] + [ANY] * 3,
        place,
        *in_hbm,
        scratch=[pltpu.VMEM((levels, cols, cols), F32), pltpu.SemaphoreType.DMA((4,))],
    )
    up_row, down_row = phases + PEAK_ROWS, 2 * phases + PEAK_ROWS
    level_far, near = exchanged(sent[: up_row + PAD_ROWS], 3), exchanged(sent[:down_row], 1)
    level_last = exchanged(level_far, 1)
    up_far = exchanged(after(sent, level_far)[up_row:down_row], 3)
    down_near = exchanged(after(sent, level_far)[down_row:], 1)
    peak = jnp.maximum(sent[phases:up_row], level_far[phases:up_row])
    peaks, reach = [peak], 1
    while reach < ranges:
        route = [(i, (i + reach) % ranges) for i in range(ranges)]
        peaks.append(jnp.maximum(peaks[-1], lax.ppermute(peaks[-1], "lvl", route)))
        reach *= 2
    peak = peaks[-1]
    down_far = exchanged(after(sent, peaks[2 % len(peaks)])[down_row:], 3)
    up_last = exchanged(after(up_far, peak), 1)
    down_last = exchanged(stack((after(down_far, up_last), 0, phases), (peak, 0, PEAK_ROWS)), 1)

    solved = call(
        solve_kernel,
        shape(phases, 2 * cols),
        [SMEM, *[VMEM] * 4, odd, odd],
        after(place, peak),
        sent,
        near,
        level_far,
        level_last,
        up_blocks,
        down_blocks,
        scratch=[
            pltpu.VMEM((phases, cols), F32),
            pltpu.VMEM((phases, phases), BF16),
            pltpu.VMEM((phases, phases), BF16),
            pltpu.VMEM((phases, 2 * cols), BF16),
            pltpu.VMEM((phases, 2 * cols), BF16),
        ],
    )
    from_below = lax.ppermute(after(solved, down_near), "lvl", [(i, i + 1) for i in range(ranges - 1)])

    free = pl.CostEstimate(flops=0, bytes_accessed=0, transcendentals=0)
    upper_level, part_up = call(
        upper_kernel,
        (shape(phases),) * 2,
        [SMEM, *[VMEM] * 5, even],
        place,
        sent,
        near,
        up_far,
        up_last,
        solved,
        level_blocks,
        cost_estimate=free,
    )
    part_level, part_down = call(
        lower_kernel,
        (shape(phases),) * 2,
        [SMEM, *[VMEM] * 5],
        place,
        sent,
        down_near,
        down_far,
        from_below,
        upper_level,
        cost_estimate=free,
    )
    return call(
        output_kernel,
        (jax.ShapeDtypeStruct((1, phases, cols), F32),) * 3,
        [SMEM] + [VMEM] * 6,
        place,
        down_last,
        from_below,
        part_level,
        part_up,
        part_down,
        peak,
    )


def solution(mesh):
    placed = (P("lvl", None, "col"),) * 3
    return jax.shard_map(per_device, mesh=mesh, in_specs=placed, out_specs=placed, check_vma=False)
```

```python
import functools

import jax
import jax.numpy as jnp
from jax import lax
from jax.experimental import pallas as pl
from jax.experimental.pallas import tpu as pltpu
from jax.sharding import PartitionSpec as P

SWEEPS = 2
PEAK_ROWS = 8
PAD_ROWS = 24
DISTANCES = (0, 1, 3, 2)
F32 = jnp.float32
BF16 = jnp.bfloat16
VMEM = pl.BlockSpec(memory_space=pltpu.VMEM)
ANY = pl.BlockSpec(memory_space=pl.ANY)
SMEM = pl.BlockSpec(memory_space=pltpu.SMEM)


def split(x):
    high = x.astype(BF16)
    return high, (x - high.astype(F32)).astype(BF16)


def exact_dot(left, right):
    (left_high, left_low), (right_high, right_low) = left, right
    dot = lambda a, b: jnp.dot(a, b, preferred_element_type=F32)
    return dot(left_high, right_high) + (dot(left_high, right_low) + dot(left_low, right_high))


def on_diagonal(rows, cols):
    row = lax.broadcasted_iota(jnp.int32, (rows, cols), 0)
    return row == lax.broadcasted_iota(jnp.int32, (rows, cols), 1)


def prepare_kernel(place, up_ref, level_ref, down_ref, sent_ref, square, sems):
    _, phases, cols = level_ref.shape
    own = rows_of(place, 0, cols)
    sources = [level_ref.at[:, own, :], level_ref.at[1], up_ref.at[0], down_ref.at[0]]
    starts = (0, phases + PEAK_ROWS, 2 * phases + PEAK_ROWS)
    targets = [square, *[sent_ref.at[pl.ds(start, phases), :] for start in starts]]
    copies = [
        pltpu.make_async_copy(source, target, sems.at[at])
        for at, (source, target) in enumerate(zip(sources, targets))
    ]
    for copy in copies:
        copy.start()
    copies[0].wait()
    lowest = jnp.min(jnp.where(on_diagonal(cols, cols)[None], square[...], 0.0))
    sent_ref[pl.ds(phases, PEAK_ROWS), :] = jnp.full((PEAK_ROWS, cols), -lowest, F32)
    for copy in copies[1:]:
        copy.wait()


def stack_kernel(ranges, *refs):
    *parts, out_ref = refs
    at = 0
    for (first, rows), ref in zip(ranges, parts):
        out_ref[pl.ds(at, rows), :] = ref[pl.ds(first, rows), :]
        at += rows


def rows_of(place, slot, cols):
    return pl.ds(pl.multiple_of((place[0] ^ DISTANCES[slot]) * cols, cols), cols)


def solve_kernel(place, own_ref, *refs):
    *blocks, up_ref, down_ref, solved_ref, inverse, high, low, s_high, s_low = refs
    phases, cols = inverse.shape
    blocks = [own_ref, *blocks]
    diagonal = on_diagonal(cols, cols)
    for slot, block in enumerate(blocks):
        rows, slot_cols = rows_of(place, slot, cols), pl.ds(slot * cols, cols)
        high[:, slot_cols], low[:, slot_cols] = split(block[pl.ds(0, phases), :])
        square = block[rows, :]
        rate = -jnp.sum(jnp.where(diagonal, square, 0.0), axis=1, keepdims=True)
        inverse[rows, :] = jnp.broadcast_to(1.0 / rate, (cols, cols))
        high[rows, slot_cols], low[rows, slot_cols] = split(jnp.where(diagonal, 0.0, square))
    for side, ref in enumerate((up_ref, down_ref)):
        solved_ref[:, pl.ds(side * cols, cols)] = ref[0] * inverse[...]
    for _ in range(SWEEPS):
        for slot in range(len(blocks)):
            rows, slot_rows = rows_of(place, slot, cols), pl.ds(slot * cols, cols)
            s_high[slot_rows, :], s_low[slot_rows, :] = split(solved_ref[rows, :])
        product = exact_dot((high[...], low[...]), (s_high[...], s_low[...]))
        for side, ref in enumerate((up_ref, down_ref)):
            columns = slice(side * cols, (side + 1) * cols)
            solved_ref[:, columns] = (ref[0] + product[:, columns]) * inverse[...]


def gathered_product(place, blocks, first_slot, solved_ref):
    cols = blocks[0].shape[-1]
    left = split(jnp.concatenate(blocks, axis=1))
    rows = [rows_of(place, first_slot + at, cols) for at in range(len(blocks))]
    right = split(jnp.concatenate([solved_ref[r, :] for r in rows], axis=0))
    return exact_dot(left, right)


def upper_kernel(place, own_ref, near_ref, far_ref, last_ref, solved_ref, level_ref, part_level, part_up):
    phases, cols = part_up.shape
    up = pl.ds(phases + PEAK_ROWS, phases)
    upper = gathered_product(place, [own_ref[up, :], near_ref[up, :], far_ref[...], last_ref[...]], 0, solved_ref)
    part_up[...] = upper[:, :cols]
    part_level[...] = level_ref[0] + upper[:, cols:]


def lower_kernel(place, own_ref, near_ref, far_ref, below_ref, upper_level, part_level, part_down):
    phases, cols = part_down.shape
    blocks = [own_ref[pl.ds(2 * phases + PEAK_ROWS, phases), :], near_ref[...], far_ref[...]]
    lower = gathered_product(place, blocks, 0, below_ref)
    part_down[...] = lower[:, cols:]
    part_level[...] = upper_level[...] + lower[:, :cols]


def output_kernel(place, last_ref, below_ref, part_level, part_up, part_down, peak_ref, new_level, new_up, new_down):
    phases, cols = part_up.shape
    scale = 1.0 / jnp.maximum(peak_ref[...], last_ref[pl.ds(phases, PEAK_ROWS), :])[0:1, :]
    new_up[0] = part_up[...] * scale
    lower = gathered_product(place, [last_ref[pl.ds(0, phases), :]], len(DISTANCES) - 1, below_ref)
    new_down[0] = (part_down[...] + lower[:, cols:]) * scale
    new_level[0] = (part_level[...] + lower[:, :cols]) * scale


def per_device(up_blocks, level_blocks, down_blocks):
    levels, phases, cols = level_blocks.shape
    shards = lax.axis_size("col")
    ranges = lax.axis_size("lvl")
    assert levels == 2 and shards == len(DISTANCES)
    place = lax.axis_index("col").astype(jnp.int32).reshape(1)
    params = pltpu.CompilerParams(vmem_limit_bytes=32 * 2**20)
    shape = lambda rows, columns=cols: jax.ShapeDtypeStruct((rows, columns), F32)

    def call(kernel, out_shape, in_specs, *operands, scratch=(), **options):
        return pl.pallas_call(
            kernel,
            out_shape=out_shape,
            in_specs=in_specs,
            out_specs=jax.tree.map(lambda _: VMEM, out_shape),
            scratch_shapes=scratch,
            grid=(1,),
            compiler_params=params,
            **options,
        )(*operands)

    def one_level(parity):
        return pl.BlockSpec((1, phases, cols), lambda step: (parity, 0, 0))

    def exchanged(part, distance):
        return lax.ppermute(part, "col", [(i, i ^ distance) for i in range(shards)])

    def after(value, *earlier):
        return lax.optimization_barrier((value, *earlier))[0]

    def stack(*pieces):
        ranges_of = [(first, rows) for _, first, rows in pieces]
        kernel = functools.partial(stack_kernel, ranges_of)
        return call(kernel, shape(sum(rows for _, rows in ranges_of)), [VMEM] * len(pieces), *[p[0] for p in pieces])

    odd, even = one_level(1), one_level(0)
    in_hbm = [pltpu.with_memory_space_constraint(x, pltpu.HBM) for x in (up_blocks, level_blocks, down_blocks)]
    sent = call(
        prepare_kernel,
        shape(3 * phases + PEAK_ROWS),
        [SMEM] + [ANY] * 3,
        place,
        *in_hbm,
        scratch=[pltpu.VMEM((levels, cols, cols), F32), pltpu.SemaphoreType.DMA((4,))],
    )
    up_row, down_row = phases + PEAK_ROWS, 2 * phases + PEAK_ROWS
    level_far, near = exchanged(sent[: up_row + PAD_ROWS], 3), exchanged(sent[:down_row], 1)
    level_last = exchanged(level_far, 1)
    up_far = exchanged(after(sent, level_far)[up_row:down_row], 3)
    down_near = exchanged(after(sent, level_far)[down_row:], 1)
    peak = jnp.maximum(sent[phases:up_row], level_far[phases:up_row])
    peaks, reach = [peak], 1
    while reach < ranges:
        route = [(i, (i + reach) % ranges) for i in range(ranges)]
        peaks.append(jnp.maximum(peaks[-1], lax.ppermute(peaks[-1], "lvl", route)))
        reach *= 2
    peak = peaks[-1]
    down_far = exchanged(after(sent, peaks[2 % len(peaks)])[down_row:], 3)
    up_last = exchanged(after(up_far, peak), 1)
    down_last = exchanged(stack((down_far, 0, phases), (peak, 0, PEAK_ROWS)), 1)

    solved = call(
        solve_kernel,
        shape(phases, 2 * cols),
        [SMEM, *[VMEM] * 4, odd, odd],
        after(place, peak),
        sent,
        near,
        level_far,
        level_last,
        up_blocks,
        down_blocks,
        scratch=[
            pltpu.VMEM((phases, cols), F32),
            pltpu.VMEM((phases, phases), BF16),
            pltpu.VMEM((phases, phases), BF16),
            pltpu.VMEM((phases, 2 * cols), BF16),
            pltpu.VMEM((phases, 2 * cols), BF16),
        ],
    )
    from_below = lax.ppermute(after(solved, down_near, up_last), "lvl", [(i, i + 1) for i in range(ranges - 1)])

    free = pl.CostEstimate(flops=0, bytes_accessed=0, transcendentals=0)
    upper_level, part_up = call(
        upper_kernel,
        (shape(phases),) * 2,
        [SMEM, *[VMEM] * 5, even],
        place,
        sent,
        near,
        up_far,
        up_last,
        solved,
        level_blocks,
        cost_estimate=free,
    )
    part_level, part_down = call(
        lower_kernel,
        (shape(phases),) * 2,
        [SMEM, *[VMEM] * 5],
        place,
        sent,
        down_near,
        down_far,
        from_below,
        upper_level,
        cost_estimate=free,
    )
    return call(
        output_kernel,
        (jax.ShapeDtypeStruct((1, phases, cols), F32),) * 3,
        [SMEM] + [VMEM] * 6,
        place,
        down_last,
        from_below,
        part_level,
        part_up,
        part_down,
        peak,
    )


def solution(mesh):
    placed = (P("lvl", None, "col"),) * 3
    return jax.shard_map(per_device, mesh=mesh, in_specs=placed, out_specs=placed, check_vma=False)
```

```python
import functools

import jax
import jax.numpy as jnp
from jax import lax
from jax.experimental import pallas as pl
from jax.experimental.pallas import tpu as pltpu
from jax.sharding import PartitionSpec as P

SWEEPS = 2
PEAK_ROWS = 8
PAD_ROWS = 16
DISTANCES = (0, 1, 3, 2)
F32 = jnp.float32
BF16 = jnp.bfloat16
VMEM = pl.BlockSpec(memory_space=pltpu.VMEM)
ANY = pl.BlockSpec(memory_space=pl.ANY)
SMEM = pl.BlockSpec(memory_space=pltpu.SMEM)


def split(x):
    high = x.astype(BF16)
    return high, (x - high.astype(F32)).astype(BF16)


def exact_dot(left, right):
    (left_high, left_low), (right_high, right_low) = left, right
    dot = lambda a, b: jnp.dot(a, b, preferred_element_type=F32)
    return dot(left_high, right_high) + (dot(left_high, right_low) + dot(left_low, right_high))


def on_diagonal(rows, cols):
    row = lax.broadcasted_iota(jnp.int32, (rows, cols), 0)
    return row == lax.broadcasted_iota(jnp.int32, (rows, cols), 1)


def prepare_kernel(place, up_ref, level_ref, down_ref, sent_ref, square, sems):
    _, phases, cols = level_ref.shape
    own = rows_of(place, 0, cols)
    sources = [level_ref.at[:, own, :], level_ref.at[1], up_ref.at[0], down_ref.at[0]]
    starts = (0, phases + PEAK_ROWS, 2 * phases + PEAK_ROWS)
    targets = [square, *[sent_ref.at[pl.ds(start, phases), :] for start in starts]]
    copies = [
        pltpu.make_async_copy(source, target, sems.at[at])
        for at, (source, target) in enumerate(zip(sources, targets))
    ]
    for copy in copies:
        copy.start()
    copies[0].wait()
    lowest = jnp.min(jnp.where(on_diagonal(cols, cols)[None], square[...], 0.0))
    sent_ref[pl.ds(phases, PEAK_ROWS), :] = jnp.full((PEAK_ROWS, cols), -lowest, F32)
    for copy in copies[1:]:
        copy.wait()


def stack_kernel(ranges, *refs):
    *parts, out_ref = refs
    at = 0
    for (first, rows), ref in zip(ranges, parts):
        out_ref[pl.ds(at, rows), :] = ref[pl.ds(first, rows), :]
        at += rows


def rows_of(place, slot, cols):
    return pl.ds(pl.multiple_of((place[0] ^ DISTANCES[slot]) * cols, cols), cols)


def solve_kernel(place, own_ref, *refs):
    *blocks, up_ref, down_ref, solved_ref, inverse, high, low, s_high, s_low = refs
    phases, cols = inverse.shape
    blocks = [own_ref, *blocks]
    diagonal = on_diagonal(cols, cols)
    for slot, block in enumerate(blocks):
        rows, slot_cols = rows_of(place, slot, cols), pl.ds(slot * cols, cols)
        high[:, slot_cols], low[:, slot_cols] = split(block[pl.ds(0, phases), :])
        square = block[rows, :]
        rate = -jnp.sum(jnp.where(diagonal, square, 0.0), axis=1, keepdims=True)
        inverse[rows, :] = jnp.broadcast_to(1.0 / rate, (cols, cols))
        high[rows, slot_cols], low[rows, slot_cols] = split(jnp.where(diagonal, 0.0, square))
    for side, ref in enumerate((up_ref, down_ref)):
        solved_ref[:, pl.ds(side * cols, cols)] = ref[0] * inverse[...]
    for _ in range(SWEEPS):
        for slot in range(len(blocks)):
            rows, slot_rows = rows_of(place, slot, cols), pl.ds(slot * cols, cols)
            s_high[slot_rows, :], s_low[slot_rows, :] = split(solved_ref[rows, :])
        product = exact_dot((high[...], low[...]), (s_high[...], s_low[...]))
        for side, ref in enumerate((up_ref, down_ref)):
            columns = slice(side * cols, (side + 1) * cols)
            solved_ref[:, columns] = (ref[0] + product[:, columns]) * inverse[...]


def gathered_product(place, blocks, first_slot, solved_ref):
    cols = blocks[0].shape[-1]
    left = split(jnp.concatenate(blocks, axis=1))
    rows = [rows_of(place, first_slot + at, cols) for at in range(len(blocks))]
    right = split(jnp.concatenate([solved_ref[r, :] for r in rows], axis=0))
    return exact_dot(left, right)


def upper_kernel(place, own_ref, near_ref, far_ref, solved_ref, level_ref, part_level, part_up):
    phases, cols = part_up.shape
    up = pl.ds(phases + PEAK_ROWS, phases)
    blocks = [own_ref[up, :], near_ref[up, :], far_ref[pl.ds(0, phases), :]]
    upper = gathered_product(place, blocks, 0, solved_ref)
    part_up[...] = upper[:, :cols]
    part_level[...] = level_ref[0] + upper[:, cols:]


def lower_kernel(place, own_ref, near_ref, far_ref, below_ref, upper_level, part_level, part_down):
    phases, cols = part_down.shape
    blocks = [own_ref[pl.ds(2 * phases + PEAK_ROWS, phases), :], near_ref[...], far_ref[pl.ds(phases, phases), :]]
    lower = gathered_product(place, blocks, 0, below_ref)
    part_down[...] = lower[:, cols:]
    part_level[...] = upper_level[...] + lower[:, :cols]


def output_kernel(place, last_ref, solved_ref, below_ref, part_level, part_up, part_down, peak_ref, *refs):
    *outs, made, sems = refs
    phases, cols = part_up.shape
    scale = 1.0 / jnp.maximum(peak_ref[...], last_ref[pl.ds(2 * phases, PEAK_ROWS), :])[0:1, :]
    copies = [pltpu.make_async_copy(made.at[at], out.at[0], sems.at[at]) for at, out in enumerate(outs)]
    last = len(DISTANCES) - 1
    upper = gathered_product(place, [last_ref[pl.ds(0, phases), :]], last, solved_ref)
    made[1] = (part_up[...] + upper[:, :cols]) * scale
    copies[1].start()
    lower = gathered_product(place, [last_ref[pl.ds(phases, phases), :]], last, below_ref)
    made[2] = (part_down[...] + lower[:, cols:]) * scale
    copies[2].start()
    made[0] = (part_level[...] + upper[:, cols:] + lower[:, :cols]) * scale
    copies[0].start()
    for copy in copies:
        copy.wait()


def per_device(up_blocks, level_blocks, down_blocks):
    levels, phases, cols = level_blocks.shape
    shards = lax.axis_size("col")
    ranges = lax.axis_size("lvl")
    assert levels == 2 and shards == len(DISTANCES)
    place = lax.axis_index("col").astype(jnp.int32).reshape(1)
    params = pltpu.CompilerParams(vmem_limit_bytes=32 * 2**20)
    shape = lambda rows, columns=cols: jax.ShapeDtypeStruct((rows, columns), F32)

    def call(kernel, out_shape, in_specs, *operands, scratch=(), out_spec=VMEM, **options):
        return pl.pallas_call(
            kernel,
            out_shape=out_shape,
            in_specs=in_specs,
            out_specs=jax.tree.map(lambda _: out_spec, out_shape),
            scratch_shapes=scratch,
            grid=(1,),
            compiler_params=params,
            **options,
        )(*operands)

    def one_level(parity):
        return pl.BlockSpec((1, phases, cols), lambda step: (parity, 0, 0))

    def exchanged(part, distance):
        return lax.ppermute(part, "col", [(i, i ^ distance) for i in range(shards)])

    def after(value, *earlier):
        return lax.optimization_barrier((value, *earlier))[0]

    def stack(*pieces):
        ranges_of = [(first, rows) for _, first, rows in pieces]
        kernel = functools.partial(stack_kernel, ranges_of)
        return call(kernel, shape(sum(rows for _, rows in ranges_of)), [VMEM] * len(pieces), *[p[0] for p in pieces])

    odd, even = one_level(1), one_level(0)
    in_hbm = [pltpu.with_memory_space_constraint(x, pltpu.HBM) for x in (up_blocks, level_blocks, down_blocks)]
    sent = call(
        prepare_kernel,
        shape(3 * phases + PEAK_ROWS),
        [SMEM] + [ANY] * 3,
        place,
        *in_hbm,
        scratch=[pltpu.VMEM((levels, cols, cols), F32), pltpu.SemaphoreType.DMA((4,))],
    )
    up_row, down_row = phases + PEAK_ROWS, 2 * phases + PEAK_ROWS
    level_far, near = exchanged(sent[: up_row + PAD_ROWS], 3), exchanged(sent[:down_row], 1)
    level_last = exchanged(level_far, 1)
    even_far = exchanged(after(sent, level_far)[up_row:], 3)
    peak = jnp.maximum(sent[phases:up_row], level_far[phases:up_row])
    peaks, reach = [peak], 1
    while reach < ranges:
        route = [(i, (i + reach) % ranges) for i in range(ranges)]
        peaks.append(jnp.maximum(peaks[-1], lax.ppermute(peaks[-1], "lvl", route)))
        reach *= 2
    peak = peaks[-1]
    down_near = exchanged(after(sent, level_far)[down_row:], 1)
    even_last = exchanged(stack((even_far, 0, 2 * phases), (peak, 0, PEAK_ROWS)), 1)

    solved = call(
        solve_kernel,
        shape(phases, 2 * cols),
        [SMEM, *[VMEM] * 4, odd, odd],
        after(place, peak),
        sent,
        near,
        level_far,
        level_last,
        up_blocks,
        down_blocks,
        scratch=[
            pltpu.VMEM((phases, cols), F32),
            pltpu.VMEM((phases, phases), BF16),
            pltpu.VMEM((phases, phases), BF16),
            pltpu.VMEM((phases, 2 * cols), BF16),
            pltpu.VMEM((phases, 2 * cols), BF16),
        ],
    )
    from_below = lax.ppermute(after(solved, down_near), "lvl", [(i, i + 1) for i in range(ranges - 1)])

    free = pl.CostEstimate(flops=0, bytes_accessed=0, transcendentals=0)
    upper_level, part_up = call(
        upper_kernel,
        (shape(phases),) * 2,
        [SMEM, *[VMEM] * 4, even],
        place,
        sent,
        near,
        even_far,
        solved,
        level_blocks,
        cost_estimate=free,
    )
    part_level, part_down = call(
        lower_kernel,
        (shape(phases),) * 2,
        [SMEM, *[VMEM] * 5],
        place,
        sent,
        down_near,
        even_far,
        from_below,
        upper_level,
        cost_estimate=free,
    )
    return call(
        output_kernel,
        (jax.ShapeDtypeStruct((1, phases, cols), F32),) * 3,
        [SMEM] + [VMEM] * 7,
        place,
        even_last,
        solved,
        from_below,
        part_level,
        part_up,
        part_down,
        peak,
        scratch=[pltpu.VMEM((3, phases, cols), F32), pltpu.SemaphoreType.DMA((3,))],
        out_spec=ANY,
    )


def solution(mesh):
    placed = (P("lvl", None, "col"),) * 3
    return jax.shard_map(per_device, mesh=mesh, in_specs=placed, out_specs=placed, check_vma=False)
```

```python
import functools

import jax
import jax.numpy as jnp
from jax import lax
from jax.experimental import pallas as pl
from jax.experimental.pallas import tpu as pltpu
from jax.sharding import PartitionSpec as P

SWEEPS = 2
PEAK_ROWS = 8
PAD_ROWS = 16
DISTANCES = (0, 1, 3, 2)
F32 = jnp.float32
BF16 = jnp.bfloat16
VMEM = pl.BlockSpec(memory_space=pltpu.VMEM)
ANY = pl.BlockSpec(memory_space=pl.ANY)
SMEM = pl.BlockSpec(memory_space=pltpu.SMEM)


def split(x):
    high = x.astype(BF16)
    return high, (x - high.astype(F32)).astype(BF16)


def exact_dot(left, right):
    (left_high, left_low), (right_high, right_low) = left, right
    dot = lambda a, b: jnp.dot(a, b, preferred_element_type=F32)
    return dot(left_high, right_high) + (dot(left_high, right_low) + dot(left_low, right_high))


def joined_dot(left, right):
    (left_high, left_low), (right_high, right_low) = left, right
    joined_left = jnp.concatenate([left_high, left_high, left_low], axis=1)
    joined_right = jnp.concatenate([right_high, right_low, right_high], axis=0)
    return jnp.dot(joined_left, joined_right, preferred_element_type=F32)


def on_diagonal(rows, cols):
    row = lax.broadcasted_iota(jnp.int32, (rows, cols), 0)
    return row == lax.broadcasted_iota(jnp.int32, (rows, cols), 1)


def prepare_kernel(place, up_ref, level_ref, down_ref, sent_ref, square, sems):
    _, phases, cols = level_ref.shape
    own = rows_of(place, 0, cols)
    sources = [level_ref.at[:, own, :], level_ref.at[1], up_ref.at[0], down_ref.at[0]]
    starts = (0, phases + PEAK_ROWS, 2 * phases + PEAK_ROWS)
    targets = [square, *[sent_ref.at[pl.ds(start, phases), :] for start in starts]]
    copies = [
        pltpu.make_async_copy(source, target, sems.at[at])
        for at, (source, target) in enumerate(zip(sources, targets))
    ]
    for copy in copies:
        copy.start()
    copies[0].wait()
    lowest = jnp.min(jnp.where(on_diagonal(cols, cols)[None], square[...], 0.0))
    sent_ref[pl.ds(phases, PEAK_ROWS), :] = jnp.full((PEAK_ROWS, cols), -lowest, F32)
    for copy in copies[1:]:
        copy.wait()


def stack_kernel(ranges, *refs):
    *parts, out_ref = refs
    at = 0
    for (first, rows), ref in zip(ranges, parts):
        out_ref[pl.ds(at, rows), :] = ref[pl.ds(first, rows), :]
        at += rows


def rows_of(place, slot, cols):
    return pl.ds(pl.multiple_of((place[0] ^ DISTANCES[slot]) * cols, cols), cols)


def solve_kernel(place, own_ref, *refs):
    *blocks, up_ref, down_ref, solved_ref, inverse, high, low, s_high, s_low = refs
    phases, cols = inverse.shape
    blocks = [own_ref, *blocks]
    diagonal = on_diagonal(cols, cols)
    for slot, block in enumerate(blocks):
        rows, slot_cols = rows_of(place, slot, cols), pl.ds(slot * cols, cols)
        high[:, slot_cols], low[:, slot_cols] = split(block[pl.ds(0, phases), :])
        square = block[rows, :]
        rate = -jnp.sum(jnp.where(diagonal, square, 0.0), axis=1, keepdims=True)
        inverse[rows, :] = jnp.broadcast_to(1.0 / rate, (cols, cols))
        high[rows, slot_cols], low[rows, slot_cols] = split(jnp.where(diagonal, 0.0, square))
    for side, ref in enumerate((up_ref, down_ref)):
        solved_ref[:, pl.ds(side * cols, cols)] = ref[0] * inverse[...]
    for _ in range(SWEEPS):
        for slot in range(len(blocks)):
            rows, slot_rows = rows_of(place, slot, cols), pl.ds(slot * cols, cols)
            s_high[slot_rows, :], s_low[slot_rows, :] = split(solved_ref[rows, :])
        product = exact_dot((high[...], low[...]), (s_high[...], s_low[...]))
        for side, ref in enumerate((up_ref, down_ref)):
            columns = slice(side * cols, (side + 1) * cols)
            solved_ref[:, columns] = (ref[0] + product[:, columns]) * inverse[...]


def gathered_product(place, blocks, first_slot, solved_ref):
    cols = blocks[0].shape[-1]
    left = split(jnp.concatenate(blocks, axis=1))
    rows = [rows_of(place, first_slot + at, cols) for at in range(len(blocks))]
    right = split(jnp.concatenate([solved_ref[r, :] for r in rows], axis=0))
    return joined_dot(left, right)


def upper_kernel(place, own_ref, near_ref, far_ref, solved_ref, level_ref, part_level, part_up):
    phases, cols = part_up.shape
    up = pl.ds(phases + PEAK_ROWS, phases)
    blocks = [own_ref[up, :], near_ref[up, :], far_ref[pl.ds(0, phases), :]]
    upper = gathered_product(place, blocks, 0, solved_ref)
    part_up[...] = upper[:, :cols]
    part_level[...] = level_ref[0] + upper[:, cols:]


def lower_kernel(place, own_ref, near_ref, far_ref, below_ref, upper_level, part_level, part_down):
    phases, cols = part_down.shape
    blocks = [own_ref[pl.ds(2 * phases + PEAK_ROWS, phases), :], near_ref[...], far_ref[pl.ds(phases, phases), :]]
    lower = gathered_product(place, blocks, 0, below_ref)
    part_down[...] = lower[:, cols:]
    part_level[...] = upper_level[...] + lower[:, :cols]


def output_kernel(place, last_ref, solved_ref, below_ref, part_level, part_up, part_down, peak_ref, *refs):
    *outs, made, sems = refs
    phases, cols = part_up.shape
    scale = 1.0 / jnp.maximum(peak_ref[...], last_ref[pl.ds(2 * phases, PEAK_ROWS), :])[0:1, :]
    copies = [pltpu.make_async_copy(made.at[at], out.at[0], sems.at[at]) for at, out in enumerate(outs)]
    last = len(DISTANCES) - 1
    upper = gathered_product(place, [last_ref[pl.ds(0, phases), :]], last, solved_ref)
    made[1] = (part_up[...] + upper[:, :cols]) * scale
    copies[1].start()
    lower = gathered_product(place, [last_ref[pl.ds(phases, phases), :]], last, below_ref)
    made[2] = (part_down[...] + lower[:, cols:]) * scale
    copies[2].start()
    made[0] = (part_level[...] + upper[:, cols:] + lower[:, :cols]) * scale
    copies[0].start()
    for copy in copies:
        copy.wait()


def per_device(up_blocks, level_blocks, down_blocks):
    levels, phases, cols = level_blocks.shape
    shards = lax.axis_size("col")
    ranges = lax.axis_size("lvl")
    assert levels == 2 and shards == len(DISTANCES)
    place = lax.axis_index("col").astype(jnp.int32).reshape(1)
    params = pltpu.CompilerParams(vmem_limit_bytes=32 * 2**20)
    shape = lambda rows, columns=cols: jax.ShapeDtypeStruct((rows, columns), F32)

    def call(kernel, out_shape, in_specs, *operands, scratch=(), out_spec=VMEM, **options):
        return pl.pallas_call(
            kernel,
            out_shape=out_shape,
            in_specs=in_specs,
            out_specs=jax.tree.map(lambda _: out_spec, out_shape),
            scratch_shapes=scratch,
            grid=(1,),
            compiler_params=params,
            **options,
        )(*operands)

    def one_level(parity):
        return pl.BlockSpec((1, phases, cols), lambda step: (parity, 0, 0))

    def exchanged(part, distance):
        return lax.ppermute(part, "col", [(i, i ^ distance) for i in range(shards)])

    def after(value, *earlier):
        return lax.optimization_barrier((value, *earlier))[0]

    def stack(*pieces):
        ranges_of = [(first, rows) for _, first, rows in pieces]
        kernel = functools.partial(stack_kernel, ranges_of)
        return call(kernel, shape(sum(rows for _, rows in ranges_of)), [VMEM] * len(pieces), *[p[0] for p in pieces])

    odd, even = one_level(1), one_level(0)
    in_hbm = [pltpu.with_memory_space_constraint(x, pltpu.HBM) for x in (up_blocks, level_blocks, down_blocks)]
    sent = call(
        prepare_kernel,
        shape(3 * phases + PEAK_ROWS),
        [SMEM] + [ANY] * 3,
        place,
        *in_hbm,
        scratch=[pltpu.VMEM((levels, cols, cols), F32), pltpu.SemaphoreType.DMA((4,))],
    )
    up_row, down_row = phases + PEAK_ROWS, 2 * phases + PEAK_ROWS
    level_far, near = exchanged(sent[: up_row + PAD_ROWS], 3), exchanged(sent[:down_row], 1)
    level_last = exchanged(level_far, 1)
    even_far = exchanged(after(sent, level_far)[up_row:], 3)
    peak = jnp.maximum(sent[phases:up_row], level_far[phases:up_row])
    peaks, reach = [peak], 1
    while reach < ranges:
        route = [(i, (i + reach) % ranges) for i in range(ranges)]
        peaks.append(jnp.maximum(peaks[-1], lax.ppermute(peaks[-1], "lvl", route)))
        reach *= 2
    peak = peaks[-1]
    down_near = exchanged(after(sent, level_far)[down_row:], 1)
    even_last = exchanged(stack((even_far, 0, 2 * phases), (peak, 0, PEAK_ROWS)), 1)

    solved = call(
        solve_kernel,
        shape(phases, 2 * cols),
        [SMEM, *[VMEM] * 4, odd, odd],
        after(place, peak),
        sent,
        near,
        level_far,
        level_last,
        up_blocks,
        down_blocks,
        scratch=[
            pltpu.VMEM((phases, cols), F32),
            pltpu.VMEM((phases, phases), BF16),
            pltpu.VMEM((phases, phases), BF16),
            pltpu.VMEM((phases, 2 * cols), BF16),
            pltpu.VMEM((phases, 2 * cols), BF16),
        ],
    )
    from_below = lax.ppermute(after(solved, down_near), "lvl", [(i, i + 1) for i in range(ranges - 1)])

    free = pl.CostEstimate(flops=0, bytes_accessed=0, transcendentals=0)
    upper_level, part_up = call(
        upper_kernel,
        (shape(phases),) * 2,
        [SMEM, *[VMEM] * 4, even],
        place,
        sent,
        near,
        even_far,
        solved,
        level_blocks,
        cost_estimate=free,
    )
    part_level, part_down = call(
        lower_kernel,
        (shape(phases),) * 2,
        [SMEM, *[VMEM] * 5],
        place,
        sent,
        down_near,
        even_far,
        from_below,
        upper_level,
        cost_estimate=free,
    )
    return call(
        output_kernel,
        (jax.ShapeDtypeStruct((1, phases, cols), F32),) * 3,
        [SMEM] + [VMEM] * 7,
        place,
        even_last,
        solved,
        from_below,
        part_level,
        part_up,
        part_down,
        peak,
        scratch=[pltpu.VMEM((3, phases, cols), F32), pltpu.SemaphoreType.DMA((3,))],
        out_spec=ANY,
    )


def solution(mesh):
    placed = (P("lvl", None, "col"),) * 3
    return jax.shard_map(per_device, mesh=mesh, in_specs=placed, out_specs=placed, check_vma=False)
```
